32 devices in a mesh: groups: 2 (over x), tm: 16 (over z, y, core).
Axes of the slice: x: 2, y: 2, z: 4, core: 2. Of those that a mesh axis runs over, the one named last changes fastest.
Arguments:
- sharded_latents: bfloat16 [32, 6144], P('groups', 'tm'), parts along dimension 0, may hold values from -6 to 6
- sample_frame_count: int32 [16], P('groups'), parts along dimension 0, may hold values from 5 to 8, as said below
- entry_kernel: bfloat16 [27, 16, 384], replicated, may hold values from -0.3125 to 0.3125
- entry_bias: float32 [384], replicated, may hold values from -3 to 3
- norm_scale_gain: float32 [384], replicated, may hold values from 0.25 to 1.75
- residual_kernel: bfloat16 [27, 384, 384], P(None, 'tm'), may hold values from -0.0625 to 0.0625
- residual_bias: float32 [384], replicated, may hold values from -3 to 3
Outputs:
- decoded: bfloat16 [128, 6, 16, 384], P(('groups', 'tm')), parts along dimension 0
The draws below stay inside these ranges and needn't reach their ends.
There are 2 independent parts, one for each index of `groups`. The reference program is written for one: setup_inputs(seed, part) draws one part's arguments, and reference() takes and returns one part's arrays. A program takes and returns all parts, laid end to end along the dimension named above; an argument that names none is the same for every part. Nothing has to cross between parts.
Inputs may be any that keep to these rules, and one draw needn't show every extreme that they name: `sample_frame_count`: every sample has more than half of its 8 frames valid; some sample has all of them valid.
All inputs are finite; a program needn't handle non-finite values.
Results may differ from the reference program's by a relative error of at most 0.009.
Values may be sent and summed in bfloat16 or wider, within the bound.
No kernel may reach another device: no remote copies, remote signals or barrier semaphores. Data moves between devices by JAX's collectives and lax.ppermute only.
A program may use at most 64 MiB of HBM per device.

```python
import jax
import jax.numpy as jnp
from jax import lax

LATENT_CHANNELS = 16
C = 384
PROMPT_SAMPLES = 8
BLOCK_FRAMES = 4
LATENT_ROWS = 6
LATENT_COLUMNS = 16
FRAME_BLOCKS = 2
FRAMES = 8


def draw_sample_frame_count(key, part):
    first, second = jax.random.split(jax.random.fold_in(key, 7))
    counts = jax.random.randint(first, (PROMPT_SAMPLES,), FRAMES // 2 + 1, FRAMES + 1)
    chosen = jax.random.randint(second, (), 0, PROMPT_SAMPLES)
    return jnp.where(jnp.arange(PROMPT_SAMPLES) == chosen, FRAMES, counts).astype(jnp.int32)


def steps_of(own_key, dims, pieces, least, high):
    loudness = 1.0
    for axis_at, shards_of in pieces:
        draws = jax.random.uniform(jax.random.fold_in(jax.random.fold_in(own_key, 6), axis_at), (shards_of,), jnp.float32, least / len(pieces), high / len(pieces))
        loudness = loudness * jnp.repeat(jnp.exp(draws), dims[axis_at] // shards_of).reshape((-1,) + (1,) * (len(dims) - 1 - axis_at))
    return loudness


def scatter_about(key, dims, deviation, most, shards=(), kind=jnp.bfloat16):
    values = deviation * jax.random.normal(key, dims, jnp.float32)
    if shards:
        values = values * steps_of(key, dims, shards, -0.22, 0.18)
    return jnp.clip(values, -most, most).astype(kind)


def setup_inputs(seed: int = 0, part: int = 0) -> dict:
    seeds = jax.random.split(jax.random.key(seed), 8)
    part_splits = jax.random.split(jax.random.fold_in(seeds[7], part), 8)
    sharded_latents = scatter_about(part_splits[0], (FRAME_BLOCKS * PROMPT_SAMPLES, BLOCK_FRAMES * LATENT_CHANNELS * LATENT_ROWS * LATENT_COLUMNS), 1.0, 6.0, ((1, 16),))
    sample_frame_count = draw_sample_frame_count(jax.random.fold_in(jax.random.fold_in(seeds[7], part), 71), part)
    entry_kernel = scatter_about(seeds[2], (27, LATENT_CHANNELS, C), (27 * LATENT_CHANNELS) ** -0.5, 0.3125)
    entry_bias = scatter_about(seeds[3], (C,), 0.5, 3.0, (), jnp.float32)
    norm_scale_gain = jnp.clip(1.0 + 0.15 * jax.random.normal(seeds[4], (C,), jnp.float32), 0.25, 1.75)
    residual_kernel = scatter_about(seeds[5], (27, C, C), (27 * C) ** -0.5, 0.0625, ((1, 16),))
    residual_bias = scatter_about(seeds[6], (C,), 0.5, 3.0, (), jnp.float32)
    return {"sharded_latents": sharded_latents, "sample_frame_count": sample_frame_count, "entry_kernel": entry_kernel, "entry_bias": entry_bias, "norm_scale_gain": norm_scale_gain, "residual_kernel": residual_kernel, "residual_bias": residual_bias}


def causal_conv(frames, weight):
    frames_out = frames.shape[0] - 2
    inputs = frames.shape[3]
    padded = jnp.pad(frames, ((0, 0), (1, 1), (1, 1), (0, 0)))
    total = jnp.zeros((frames_out * LATENT_ROWS * LATENT_COLUMNS, weight.shape[2]), jnp.float32)
    for time_tap in range(3):
        for row_tap in range(3):
            for col_tap in range(3):
                window = padded[time_tap:time_tap + frames_out, row_tap:row_tap + LATENT_ROWS, col_tap:col_tap + LATENT_COLUMNS, :]
                window = window.reshape(frames_out * LATENT_ROWS * LATENT_COLUMNS, inputs)
                tap = 9 * time_tap + 3 * row_tap + col_tap
                total = total + jnp.dot(window, weight[tap], preferred_element_type=jnp.float32)
    return total

def activate(stream, norm_scale_gain):
    values = stream.astype(jnp.float32)
    scale = lax.rsqrt(lax.optimization_barrier(jnp.mean(values * values, axis=-1, keepdims=True)) + 1e-06)
    return jax.nn.silu(values * scale * norm_scale_gain).astype(jnp.bfloat16)

def reference(sharded_latents, sample_frame_count, entry_kernel, entry_bias, norm_scale_gain, residual_kernel, residual_bias):
    latent_volume = sharded_latents.reshape(FRAME_BLOCKS, PROMPT_SAMPLES, BLOCK_FRAMES, LATENT_CHANNELS, LATENT_ROWS, LATENT_COLUMNS)
    latent_volume = jnp.transpose(latent_volume, (1, 0, 2, 4, 5, 3)).reshape(PROMPT_SAMPLES, FRAMES, LATENT_ROWS, LATENT_COLUMNS, LATENT_CHANNELS)

    def decode(inputs):
        sample, count = inputs
        frames = jnp.concatenate([jnp.zeros((2, LATENT_ROWS, LATENT_COLUMNS, LATENT_CHANNELS), sample.dtype), sample], axis=0)
        stream = (causal_conv(frames, entry_kernel) + entry_bias).astype(jnp.bfloat16)
        active = activate(stream, norm_scale_gain).reshape(FRAMES, LATENT_ROWS, LATENT_COLUMNS, C)
        extended = jnp.concatenate([jnp.zeros((2, LATENT_ROWS, LATENT_COLUMNS, C), active.dtype), active], axis=0)
        branch = causal_conv(extended, residual_kernel) + residual_bias
        total = (stream.astype(jnp.float32) + branch).reshape(FRAMES, LATENT_ROWS, LATENT_COLUMNS, C)
        valid = (jnp.arange(FRAMES) < count)[:, None, None, None]
        return jnp.where(valid, total, jnp.zeros_like(total)).astype(jnp.bfloat16)
    result = lax.map(decode, (latent_volume, sample_frame_count))
    result = result.reshape(PROMPT_SAMPLES, FRAME_BLOCKS, BLOCK_FRAMES, LATENT_ROWS, LATENT_COLUMNS, C)
    result = jnp.transpose(result, (1, 0, 2, 3, 4, 5))
    return result.reshape(PROMPT_SAMPLES * FRAMES, LATENT_ROWS, LATENT_COLUMNS, C)
```

```python
import functools

import jax
import jax.numpy as jnp
from jax import lax
from jax.experimental import pallas as pl
from jax.experimental.pallas import tpu as pltpu
from jax.sharding import PartitionSpec as P

LATENT_CHANNELS = 16
C = 384
PROMPT_SAMPLES = 8
BLOCK_FRAMES = 4
LATENT_ROWS = 6
LATENT_COLUMNS = 16
HW = LATENT_ROWS * LATENT_COLUMNS
LANES = PROMPT_SAMPLES * HW
VMEM = pl.BlockSpec(memory_space=pltpu.VMEM)
SMEM = pl.BlockSpec(memory_space=pltpu.SMEM)
LIMIT = 56 * 1024 * 1024


def shift_mask(j, k):
    lane = lax.broadcasted_iota(jnp.int32, (1, LANES), 1)
    row = (lane % HW) // LATENT_COLUMNS
    col = lane % LATENT_COLUMNS
    ok = lane >= 0
    if j == 0:
        ok = row > 0
    elif j == 2:
        ok = row < LATENT_ROWS - 1
    if k == 0:
        ok = ok & (col > 0)
    elif k == 2:
        ok = ok & (col < LATENT_COLUMNS - 1)
    return ok


def shifted(x, delta):
    return x if delta == 0 else pltpu.roll(x, (-delta) % x.shape[1], 1)


def latent_rows_kernel(x_ref, o_ref):
    x = x_ref[...].astype(jnp.float32)
    rows = []
    for c in range(x.shape[1] // HW):
        pieces = [x[r : r + 1, c * HW : (c + 1) * HW] for r in range(x.shape[0])]
        rows.append(jnp.concatenate(pieces, axis=1))
    o_ref[...] = jnp.concatenate(rows, axis=0).astype(jnp.bfloat16)


def kernel_chunks_kernel(n, w_ref, o_ref):
    own = C // n
    w = w_ref[...].astype(jnp.float32).reshape(3, 9, own, C)
    taps = [w[:, t].reshape(3 * own, C) for t in range(9)]
    pad = o_ref.shape[1] - 9 * own
    for d in range(0, n, 2):
        both = []
        for e in (d, d + 1):
            pieces = [tap[:, e * own : (e + 1) * own] for tap in taps]
            pieces.append(jnp.zeros((3 * own, pad), jnp.float32))
            both.append(jnp.concatenate(pieces, axis=1))
        o_ref[d * 3 * own : (d + 2) * 3 * own, :] = jnp.concatenate(both, axis=0).astype(jnp.bfloat16)


def active_kernel(frames, own, lat_ref, entry_ref, bias_ref, gain_ref, first_ref, x_ref, stream_ref, col_ref, s0_ref, s1_ref):
    weight = jnp.transpose(entry_ref[...])
    taps = 9 * LATENT_CHANNELS
    for f in range(frames):
        b, g = divmod(f, BLOCK_FRAMES)
        lat = lat_ref[g * LATENT_CHANNELS : (g + 1) * LATENT_CHANNELS, b * LANES : (b + 1) * LANES].astype(jnp.float32)
        for j in range(3):
            for k in range(3):
                moved = shifted(lat, LATENT_COLUMNS * (j - 1) + k - 1)
                moved = jnp.where(shift_mask(j, k), moved, 0.0)
                at = f * taps + (3 * j + k) * LATENT_CHANNELS
                col_ref[at : at + LATENT_CHANNELS, :] = moved.astype(jnp.bfloat16)
    bias = bias_ref[...]
    gain = gain_ref[...]
    first = pl.multiple_of(first_ref[0], 8)
    for f in range(frames):
        s_ref = (s0_ref, s1_ref)[f % 2]
        least = max(f - 2, 0)
        s = jnp.dot(
            weight[:, (2 - (f - least)) * taps :],
            col_ref[least * taps : (f + 1) * taps, :],
            preferred_element_type=jnp.float32,
        )
        s = (s + bias).astype(jnp.bfloat16).astype(jnp.float32)
        s_ref[...] = s
        scale = lax.rsqrt(jnp.sum(s * s, axis=0, keepdims=True) * (1.0 / C) + 1e-06)
        half = s_ref[...] * (scale * 0.5) * gain
        x_ref[f * C : (f + 1) * C, :] = (half + half * jnp.tanh(half)).astype(jnp.bfloat16)
        stream_ref[f] = s_ref[pl.ds(first, own), :]


def branch_kernel(frames, n, w_ref, x_ref, stream_ref, bias_ref, count_ref, o_ref, out_ref):
    own = C // n
    w = w_ref[...].astype(jnp.float32).reshape(n, 3, own, w_ref.shape[1])
    w = jnp.transpose(w, (1, 0, 2, 3)).reshape(3 * C, w_ref.shape[1])
    weight = jnp.transpose(w.astype(jnp.bfloat16))
    lane = lax.broadcasted_iota(jnp.int32, (1, LANES), 1)
    count = jnp.zeros((1, LANES), jnp.int32)
    for s in range(PROMPT_SAMPLES):
        count = jnp.where(lane // HW == s, count_ref[s], count)
    for f in range(frames):
        least = max(f - 2, 0)
        z = jnp.dot(
            weight[:, (2 - (f - least)) * C :],
            x_ref[least * C : (f + 1) * C, :],
            preferred_element_type=jnp.float32,
        )
        total = stream_ref[f] + bias_ref[...]
        for k in range(3):
            part = None
            for j in range(3):
                tap = z[(3 * j + k) * own : (3 * j + k + 1) * own]
                if j != 1:
                    tap = jnp.where(shift_mask(j, 1), shifted(tap, LATENT_COLUMNS * (j - 1)), 0.0)
                part = tap if part is None else part + tap
            if k != 1:
                part = jnp.where(shift_mask(1, k), shifted(part, k - 1), 0.0)
            total = total + part
        out_ref[f] = jnp.where(count > f, total, 0.0)
    for b in range(frames // BLOCK_FRAMES):
        parts = [out_ref[b * BLOCK_FRAMES + g] for g in range(BLOCK_FRAMES)]
        for s in range(0, PROMPT_SAMPLES, 2):
            both = [
                jnp.concatenate([p[:, t * HW : (t + 1) * HW] for p in parts], axis=1) for t in (s, s + 1)
            ]
            at = (b * PROMPT_SAMPLES + s) * own
            o_ref[at : at + 2 * own, :] = jnp.concatenate(both, axis=0).astype(jnp.bfloat16)


def transpose_kernel(x_ref, o_ref):
    o_ref[...] = jnp.transpose(x_ref[...])


def call(body, out, specs, scratch=(), flops=0, moved=0):
    return pl.pallas_call(
        body,
        out_shape=out,
        in_specs=specs,
        out_specs=jax.tree.map(lambda _: VMEM, out),
        scratch_shapes=list(scratch),
        compiler_params=pltpu.CompilerParams(vmem_limit_bytes=LIMIT),
        cost_estimate=pl.CostEstimate(flops=flops, bytes_accessed=moved, transcendentals=0),
    )


def by_channel(n, latents, counts, entry_kernel, entry_bias, gain, kernel, bias):
    own = C // n
    frames = n // PROMPT_SAMPLES * BLOCK_FRAMES
    first = (lax.axis_index("tm") * own).astype(jnp.int32)
    shape = jax.ShapeDtypeStruct
    rows = call(
        latent_rows_kernel,
        shape((latents.shape[1] // HW, n * HW), jnp.bfloat16),
        [VMEM],
    )(latents)
    rows = lax.all_gather(rows, "tm", axis=0, tiled=True)
    width = -(-9 * own // 128) * 128
    chunks = call(
        functools.partial(kernel_chunks_kernel, n),
        shape((n * 3 * own, width), jnp.bfloat16),
        [VMEM],
    )(kernel)
    chunks = lax.all_to_all(chunks, "tm", split_axis=0, concat_axis=0, tiled=True)
    active, stream = call(
        functools.partial(active_kernel, frames, own),
        (shape((frames * C, LANES), jnp.bfloat16), shape((frames, own, LANES), jnp.float32)),
        [VMEM, VMEM, VMEM, VMEM, SMEM],
        [
            pltpu.VMEM((frames * 9 * LATENT_CHANNELS, LANES), jnp.bfloat16),
            pltpu.VMEM((C, LANES), jnp.float32),
            pltpu.VMEM((C, LANES), jnp.float32),
        ],
        flops=2 * frames * LANES * 432 * C,
        moved=20_000_000,
    )(
        rows,
        entry_kernel.reshape(27 * LATENT_CHANNELS, C),
        entry_bias.reshape(C, 1),
        gain.reshape(C, 1),
        first.reshape(1),
    )
    own_bias = lax.dynamic_slice(bias, (first,), (own,)).reshape(own, 1)
    out = call(
        functools.partial(branch_kernel, frames, n),
        shape((n * own, BLOCK_FRAMES * HW), jnp.bfloat16),
        [VMEM, VMEM, VMEM, VMEM, SMEM],
        [pltpu.VMEM((frames, own, LANES), jnp.float32)],
        flops=2 * frames * LANES * 27 * C * own,
        moved=20_000_000,
    )(chunks, active, stream, own_bias, counts)
    out = lax.all_to_all(out, "tm", split_axis=0, concat_axis=0, tiled=True)
    out = call(transpose_kernel, shape((BLOCK_FRAMES * HW, C), jnp.bfloat16), [VMEM])(out)
    return out.reshape(BLOCK_FRAMES, LATENT_ROWS, LATENT_COLUMNS, C)


def from_behind(block, axis, distance):
    devices = range(lax.axis_size(axis))
    route = [(i - distance, i) for i in devices if i - distance in devices]
    return lax.ppermute(block, axis, route)


def causal_conv(frames, weight):
    frames_out = frames.shape[0] - 2
    inputs = frames.shape[3]
    padded = jnp.pad(frames, ((0, 0), (1, 1), (1, 1), (0, 0)))
    total = jnp.zeros((frames_out * LATENT_ROWS * LATENT_COLUMNS, weight.shape[2]), jnp.float32)
    for time_tap in range(3):
        for row_tap in range(3):
            for col_tap in range(3):
                window = padded[
                    time_tap : time_tap + frames_out,
                    row_tap : row_tap + LATENT_ROWS,
                    col_tap : col_tap + LATENT_COLUMNS,
                    :,
                ]
                window = window.reshape(frames_out * LATENT_ROWS * LATENT_COLUMNS, inputs)
                tap = 9 * time_tap + 3 * row_tap + col_tap
                total = total + jnp.dot(window, weight[tap], preferred_element_type=jnp.float32)
    return total


def activate(stream, norm_scale_gain):
    values = stream.astype(jnp.float32)
    scale = lax.rsqrt(jnp.mean(values * values, axis=-1, keepdims=True) + 1e-06)
    return jax.nn.silu(values * scale * norm_scale_gain).astype(jnp.bfloat16)


def to_cells(planes):
    return jnp.transpose(
        planes.reshape(planes.shape[0], LATENT_CHANNELS, LATENT_ROWS, LATENT_COLUMNS), (0, 2, 3, 1)
    )


def by_block(
    sharded_latents,
    sample_frame_count,
    entry_kernel,
    entry_bias,
    norm_scale_gain,
    residual_kernel,
    residual_bias,
):
    gathered_latents = lax.all_to_all(
        sharded_latents, "tm", split_axis=0, concat_axis=1, tiled=True
    )
    latent_volume = gathered_latents.reshape(
        BLOCK_FRAMES, LATENT_CHANNELS, LATENT_ROWS * LATENT_COLUMNS
    )
    position = lax.axis_index("tm")
    block = position // PROMPT_SAMPLES
    sample = position % PROMPT_SAMPLES
    keep = block > 0
    earlier = from_behind(latent_volume, "tm", PROMPT_SAMPLES)
    earlier = jnp.where(keep, earlier, jnp.zeros_like(earlier))
    frames = to_cells(jnp.concatenate([earlier, latent_volume], axis=0))
    widened = (causal_conv(frames, entry_kernel) + entry_bias).astype(jnp.bfloat16)
    active_all = activate(widened, norm_scale_gain).reshape(
        BLOCK_FRAMES + 2, LATENT_ROWS, LATENT_COLUMNS, C
    )
    behind = jnp.where(keep, active_all[:2], jnp.zeros_like(active_all[:2]))
    extended = jnp.concatenate([behind, active_all[2:]], axis=0)
    stream = widened[2 * LATENT_ROWS * LATENT_COLUMNS :]
    kernel_all = lax.all_gather(residual_kernel, "tm", axis=1, tiled=True)
    branch = causal_conv(extended, kernel_all)
    total = (stream.astype(jnp.float32) + (branch + residual_bias)).reshape(
        BLOCK_FRAMES, LATENT_ROWS, LATENT_COLUMNS, C
    )
    limit = jnp.sum(jnp.where(jnp.arange(PROMPT_SAMPLES) == sample, sample_frame_count, 0))
    frame_index = block * BLOCK_FRAMES + jnp.arange(BLOCK_FRAMES)
    valid = (frame_index < limit)[:, None, None, None]
    return jnp.where(valid, total, jnp.zeros_like(total)).astype(jnp.bfloat16)


def solution(mesh):
    n = mesh.shape["tm"]
    cells = BLOCK_FRAMES * LATENT_CHANNELS * HW
    whole_rows = cells % (n * HW) == 0 and C % n == 0 and (C // n) % 8 == 0 and n % PROMPT_SAMPLES == 0
    body = functools.partial(by_channel, n) if whole_rows else by_block
    in_specs = (P("groups", "tm"), P("groups"), P(), P(), P(), P(None, "tm", None), P())
    out_specs = P(("groups", "tm"), None, None, None)
    return jax.shard_map(body, mesh=mesh, in_specs=in_specs, out_specs=out_specs, check_vma=False)
```

```python
import functools

import jax
import jax.numpy as jnp
from jax import lax
from jax.experimental import pallas as pl
from jax.experimental.pallas import tpu as pltpu
from jax.sharding import PartitionSpec as P

LATENT_CHANNELS = 16
C = 384
PROMPT_SAMPLES = 8
BLOCK_FRAMES = 4
LATENT_ROWS = 6
LATENT_COLUMNS = 16
HW = LATENT_ROWS * LATENT_COLUMNS
LANES = PROMPT_SAMPLES * HW
VMEM = pl.BlockSpec(memory_space=pltpu.VMEM)
SMEM = pl.BlockSpec(memory_space=pltpu.SMEM)
ANY = pl.BlockSpec(memory_space=pl.ANY)


def shift_mask(j, k):
    lane = lax.broadcasted_iota(jnp.int32, (1, LANES), 1)
    row = (lane % HW) // LATENT_COLUMNS
    col = lane % LATENT_COLUMNS
    ok = lane >= 0
    if j == 0:
        ok = row > 0
    elif j == 2:
        ok = row < LATENT_ROWS - 1
    if k == 0:
        ok = ok & (col > 0)
    elif k == 2:
        ok = ok & (col < LATENT_COLUMNS - 1)
    return ok


def shifted(x, delta):
    return x if delta == 0 else pltpu.roll(x, (-delta) % x.shape[1], 1)


def latent_rows_kernel(n, x_ref, o_ref):
    x = x_ref[...].astype(jnp.float32)
    rows = []
    for b in range(x.shape[0] // PROMPT_SAMPLES):
        for c in range(x.shape[1] // HW):
            at = b * PROMPT_SAMPLES
            pieces = [x[r : r + 1, c * HW : (c + 1) * HW] for r in range(at, at + PROMPT_SAMPLES)]
            rows.append(jnp.concatenate(pieces, axis=1))
    rows = jnp.concatenate(rows, axis=0)
    o_ref[...] = jnp.concatenate([rows] * n, axis=0).astype(jnp.bfloat16)


def kernel_chunks_kernel(n, w_ref, o_ref):
    own = C // n
    w = w_ref[...].astype(jnp.float32).reshape(3, 9, own, C)
    taps = [w[:, t].reshape(3 * own, C) for t in range(9)]
    pad = o_ref.shape[1] - 9 * own
    for d in range(0, n, 2):
        both = []
        for e in (d, d + 1):
            pieces = [tap[:, e * own : (e + 1) * own] for tap in taps]
            pieces.append(jnp.zeros((3 * own, pad), jnp.float32))
            both.append(jnp.concatenate(pieces, axis=1))
        o_ref[d * 3 * own : (d + 2) * 3 * own, :] = jnp.concatenate(both, axis=0).astype(jnp.bfloat16)


def column(row_ref, width):
    tile = jnp.transpose(jnp.broadcast_to(row_ref[...], (128, row_ref.shape[1])))
    return jnp.concatenate([tile] * (width // 128), axis=1)


def active_kernel(n, lat_ref, entry_ref, bias_ref, gain_ref, first_ref, x_hbm, stream_ref, col_ref, row_ref, x_ref, sem):
    own = C // n
    frames = n // PROMPT_SAMPLES * BLOCK_FRAMES
    each = LATENT_CHANNELS * BLOCK_FRAMES // n
    taps = 9 * LATENT_CHANNELS
    ahead = -(-own // 16) * 16
    first = pl.multiple_of(first_ref[0], 8)
    bias = column(bias_ref, LANES)
    half_gain = (column(gain_ref, LANES) * 0.5).astype(jnp.bfloat16)
    full = jnp.transpose(entry_ref[...].astype(jnp.float32))
    row_ref[:, 0 : 3 * taps] = full
    row_ref[:, 3 * taps : 3 * taps + 128] = bias[:, 0:128]
    mine = row_ref[pl.ds(first, own), :]
    mine_bias = mine[:, 3 * taps : 3 * taps + 128]
    mine_bias = jnp.concatenate([mine_bias] * (LANES // 128), axis=1)
    spare = jnp.zeros((ahead - own, 3 * taps), jnp.float32)
    weight = jnp.concatenate([mine[:, : 3 * taps], spare, full], axis=0).astype(jnp.bfloat16)
    per_frame = LATENT_CHANNELS // each
    blocks = n // PROMPT_SAMPLES
    lats = lat_ref[...].astype(jnp.float32).reshape(BLOCK_FRAMES, per_frame, blocks, each, LANES)
    copies = []
    for f in range(frames):
        b, g = divmod(f, BLOCK_FRAMES)
        lat = lats[g, :, b].reshape(LATENT_CHANNELS, LANES)
        for j in range(3):
            for k in range(3):
                moved = shifted(lat, LATENT_COLUMNS * (j - 1) + k - 1)
                moved = jnp.where(shift_mask(j, k), moved, 0.0)
                at = f * taps + (3 * j + k) * LATENT_CHANNELS
                col_ref[at : at + LATENT_CHANNELS, :] = moved.astype(jnp.bfloat16)
        least = max(f - 2, 0)
        z = jnp.dot(
            weight[:, (2 - (f - least)) * taps :],
            col_ref[least * taps : (f + 1) * taps, :],
            preferred_element_type=jnp.float32,
        )
        stream_ref[f] = (z[:own] + mine_bias).astype(jnp.bfloat16).astype(jnp.float32)
        s = z[ahead:] + bias
        scale = lax.rsqrt(jnp.sum(s * s, axis=0, keepdims=True) * (1.0 / C) + 1e-06)
        half = s.astype(jnp.bfloat16) * half_gain * scale.astype(jnp.bfloat16)
        x_ref[f * C : (f + 1) * C, :] = half + half * jnp.tanh(half)
        rows = pl.ds(f * C, C)
        copy = pltpu.make_async_copy(x_ref.at[rows], x_hbm.at[rows], sem.at[f])
        copy.start()
        copies.append(copy)
    for copy in copies:
        copy.wait()


def branch_kernel(n, w_ref, x_hbm, stream_ref, bias_ref, first_ref, count_ref, o_ref, x_ref, bias_col_ref, out_ref, sem):
    own = C // n
    frames = n // PROMPT_SAMPLES * BLOCK_FRAMES
    copies = []
    for f in range(frames):
        rows = pl.ds(f * C, C)
        copy = pltpu.make_async_copy(x_hbm.at[rows], x_ref.at[rows], sem.at[f])
        copy.start()
        copies.append(copy)
    w = w_ref[...].astype(jnp.float32).reshape(n, 3, own, w_ref.shape[1])
    w = jnp.transpose(w, (1, 0, 2, 3)).reshape(3 * C, w_ref.shape[1])
    weight = jnp.transpose(w.astype(jnp.bfloat16))[: -(-9 * own // 16) * 16]
    bias_col_ref[...] = column(bias_ref, 128)
    bias = bias_col_ref[pl.ds(pl.multiple_of(first_ref[0], 8), own), :]
    bias = jnp.concatenate([bias] * (LANES // 128), axis=1)
    lane = lax.broadcasted_iota(jnp.int32, (1, LANES), 1)
    count = jnp.zeros((1, LANES), jnp.int32)
    for s in range(PROMPT_SAMPLES):
        count = jnp.where(lane // HW == s, count_ref[s], count)
    for f in range(frames):
        copies[f].wait()
        least = max(f - 2, 0)
        z = jnp.dot(
            weight[:, (2 - (f - least)) * C :],
            x_ref[least * C : (f + 1) * C, :],
            preferred_element_type=jnp.float32,
        )
        total = stream_ref[f] + bias
        for k in range(3):
            part = None
            for j in range(3):
                tap = z[(3 * j + k) * own : (3 * j + k + 1) * own]
                if j != 1:
                    tap = jnp.where(shift_mask(j, 1), shifted(tap, LATENT_COLUMNS * (j - 1)), 0.0)
                part = tap if part is None else part + tap
            if k != 1:
                part = jnp.where(shift_mask(1, k), shifted(part, k - 1), 0.0)
            total = total + part
        out_ref[f] = jnp.where(count > f, total, 0.0)
        b, g = divmod(f, BLOCK_FRAMES)
        if g == BLOCK_FRAMES - 1:
            parts = [out_ref[b * BLOCK_FRAMES + t] for t in range(BLOCK_FRAMES)]
            for s in range(0, PROMPT_SAMPLES, 2):
                both = [
                    jnp.concatenate([p[:, t * HW : (t + 1) * HW] for p in parts], axis=1) for t in (s, s + 1)
                ]
                at = (b * PROMPT_SAMPLES + s) * own
                o_ref[at : at + 2 * own, :] = jnp.concatenate(both, axis=0).astype(jnp.bfloat16)


def transpose_kernel(x_ref, o_ref):
    o_ref[...] = jnp.transpose(x_ref[...])


def call(body, out, ins, outs, scratch=(), flops=0, moved=0, limit=8):
    return pl.pallas_call(
        body,
        out_shape=out,
        in_specs=ins,
        out_specs=outs,
        scratch_shapes=list(scratch),
        compiler_params=pltpu.CompilerParams(vmem_limit_bytes=limit * 1024 * 1024),
        cost_estimate=pl.CostEstimate(flops=flops, bytes_accessed=moved, transcendentals=0),
    )


def by_channel(n, latents, counts, entry_kernel, entry_bias, gain, kernel, bias):
    own = C // n
    frames = n // PROMPT_SAMPLES * BLOCK_FRAMES
    first = (lax.axis_index("tm") * own).astype(jnp.int32).reshape(1)
    shape = jax.ShapeDtypeStruct
    bf16, f32 = jnp.bfloat16, jnp.float32
    each = latents.shape[1] // HW * (n // PROMPT_SAMPLES)
    rows = call(
        functools.partial(latent_rows_kernel, n), shape((n * each, LANES), bf16), [VMEM], VMEM
    )(latents)
    rows = lax.all_to_all(rows, "tm", split_axis=0, concat_axis=0, tiled=True)
    width = -(-9 * own // 128) * 128
    chunks = call(
        functools.partial(kernel_chunks_kernel, n), shape((n * 3 * own, width), bf16), [VMEM], VMEM
    )(kernel)
    chunks = lax.all_to_all(chunks, "tm", split_axis=0, concat_axis=0, tiled=True)
    active, stream = call(
        functools.partial(active_kernel, n),
        (shape((frames * C, LANES), bf16), shape((frames, own, LANES), f32)),
        [VMEM, VMEM, VMEM, VMEM, SMEM],
        (ANY, VMEM),
        [
            pltpu.VMEM((frames * 9 * LATENT_CHANNELS, LANES), bf16),
            pltpu.VMEM((C, 27 * LATENT_CHANNELS + 128), f32),
            pltpu.VMEM((frames * C, LANES), bf16),
            pltpu.SemaphoreType.DMA((frames,)),
        ],
        flops=2 * frames * LANES * 432 * C,
        moved=20_000_000,
        limit=32,
    )(
        rows,
        entry_kernel.reshape(27 * LATENT_CHANNELS, C),
        entry_bias.reshape(1, C),
        gain.reshape(1, C),
        first,
    )
    out = call(
        functools.partial(branch_kernel, n),
        shape((n * own, BLOCK_FRAMES * HW), bf16),
        [VMEM, ANY, VMEM, VMEM, SMEM, SMEM],
        VMEM,
        [
            pltpu.VMEM((frames * C, LANES), bf16),
            pltpu.VMEM((C, 128), f32),
            pltpu.VMEM((frames, own, LANES), f32),
            pltpu.SemaphoreType.DMA((frames,)),
        ],
        flops=2 * frames * LANES * 27 * C * own,
        moved=20_000_000,
        limit=32,
    )(chunks, active, stream, bias.reshape(1, C), first, counts)
    out = lax.all_to_all(out, "tm", split_axis=0, concat_axis=0, tiled=True)
    out = call(transpose_kernel, shape((BLOCK_FRAMES * HW, C), bf16), [VMEM], VMEM)(out)
    return out.reshape(BLOCK_FRAMES, LATENT_ROWS, LATENT_COLUMNS, C)


def from_behind(block, axis, distance):
    devices = range(lax.axis_size(axis))
    route = [(i - distance, i) for i in devices if i - distance in devices]
    return lax.ppermute(block, axis, route)


def causal_conv(frames, weight):
    frames_out = frames.shape[0] - 2
    inputs = frames.shape[3]
    padded = jnp.pad(frames, ((0, 0), (1, 1), (1, 1), (0, 0)))
    total = jnp.zeros((frames_out * LATENT_ROWS * LATENT_COLUMNS, weight.shape[2]), jnp.float32)
    for time_tap in range(3):
        for row_tap in range(3):
            for col_tap in range(3):
                window = padded[
                    time_tap : time_tap + frames_out,
                    row_tap : row_tap + LATENT_ROWS,
                    col_tap : col_tap + LATENT_COLUMNS,
                    :,
                ]
                window = window.reshape(frames_out * LATENT_ROWS * LATENT_COLUMNS, inputs)
                tap = 9 * time_tap + 3 * row_tap + col_tap
                total = total + jnp.dot(window, weight[tap], preferred_element_type=jnp.float32)
    return total


def activate(stream, norm_scale_gain):
    values = stream.astype(jnp.float32)
    scale = lax.rsqrt(jnp.mean(values * values, axis=-1, keepdims=True) + 1e-06)
    return jax.nn.silu(values * scale * norm_scale_gain).astype(jnp.bfloat16)


def to_cells(planes):
    return jnp.transpose(
        planes.reshape(planes.shape[0], LATENT_CHANNELS, LATENT_ROWS, LATENT_COLUMNS), (0, 2, 3, 1)
    )


def by_block(
    sharded_latents,
    sample_frame_count,
    entry_kernel,
    entry_bias,
    norm_scale_gain,
    residual_kernel,
    residual_bias,
):
    gathered_latents = lax.all_to_all(
        sharded_latents, "tm", split_axis=0, concat_axis=1, tiled=True
    )
    latent_volume = gathered_latents.reshape(
        BLOCK_FRAMES, LATENT_CHANNELS, LATENT_ROWS * LATENT_COLUMNS
    )
    position = lax.axis_index("tm")
    block = position // PROMPT_SAMPLES
    sample = position % PROMPT_SAMPLES
    keep = block > 0
    earlier = from_behind(latent_volume, "tm", PROMPT_SAMPLES)
    earlier = jnp.where(keep, earlier, jnp.zeros_like(earlier))
    frames = to_cells(jnp.concatenate([earlier, latent_volume], axis=0))
    widened = (causal_conv(frames, entry_kernel) + entry_bias).astype(jnp.bfloat16)
    active_all = activate(widened, norm_scale_gain).reshape(
        BLOCK_FRAMES + 2, LATENT_ROWS, LATENT_COLUMNS, C
    )
    behind = jnp.where(keep, active_all[:2], jnp.zeros_like(active_all[:2]))
    extended = jnp.concatenate([behind, active_all[2:]], axis=0)
    stream = widened[2 * LATENT_ROWS * LATENT_COLUMNS :]
    kernel_all = lax.all_gather(residual_kernel, "tm", axis=1, tiled=True)
    branch = causal_conv(extended, kernel_all)
    total = (stream.astype(jnp.float32) + (branch + residual_bias)).reshape(
        BLOCK_FRAMES, LATENT_ROWS, LATENT_COLUMNS, C
    )
    limit = jnp.sum(jnp.where(jnp.arange(PROMPT_SAMPLES) == sample, sample_frame_count, 0))
    frame_index = block * BLOCK_FRAMES + jnp.arange(BLOCK_FRAMES)
    valid = (frame_index < limit)[:, None, None, None]
    return jnp.where(valid, total, jnp.zeros_like(total)).astype(jnp.bfloat16)


def solution(mesh):
    n = mesh.shape["tm"]
    cells = BLOCK_FRAMES * LATENT_CHANNELS * HW
    whole_rows = cells % (n * HW) == 0 and C % n == 0 and (C // n) % 8 == 0 and n % PROMPT_SAMPLES == 0
    body = functools.partial(by_channel, n) if whole_rows else by_block
    in_specs = (P("groups", "tm"), P("groups"), P(), P(), P(), P(None, "tm", None), P())
    out_specs = P(("groups", "tm"), None, None, None)
    return jax.shard_map(body, mesh=mesh, in_specs=in_specs, out_specs=out_specs, check_vma=False)
```

```python
import functools

import jax
import jax.numpy as jnp
from jax import lax
from jax.experimental import pallas as pl
from jax.experimental.pallas import tpu as pltpu
from jax.sharding import PartitionSpec as P

LATENT_CHANNELS = 16
C = 384
PROMPT_SAMPLES = 8
BLOCK_FRAMES = 4
LATENT_ROWS = 6
LATENT_COLUMNS = 16
HW = LATENT_ROWS * LATENT_COLUMNS
LANES = PROMPT_SAMPLES * HW
VMEM = pl.BlockSpec(memory_space=pltpu.VMEM)
SMEM = pl.BlockSpec(memory_space=pltpu.SMEM)
ANY = pl.BlockSpec(memory_space=pl.ANY)


def shift_mask(j, k):
    lane = lax.broadcasted_iota(jnp.int32, (1, LANES), 1)
    row = (lane % HW) // LATENT_COLUMNS
    col = lane % LATENT_COLUMNS
    ok = lane >= 0
    if j == 0:
        ok = row > 0
    elif j == 2:
        ok = row < LATENT_ROWS - 1
    if k == 0:
        ok = ok & (col > 0)
    elif k == 2:
        ok = ok & (col < LATENT_COLUMNS - 1)
    return ok


def shifted(x, delta):
    return x if delta == 0 else pltpu.roll(x, (-delta) % x.shape[1], 1)


def parcels_kernel(n, x_ref, w_ref, side_ref, o_ref):
    own = C // n
    x = x_ref[...].astype(jnp.float32)
    rows = []
    for b in range(x.shape[0] // PROMPT_SAMPLES):
        for c in range(x.shape[1] // HW):
            at = b * PROMPT_SAMPLES
            pieces = [x[r : r + 1, c * HW : (c + 1) * HW] for r in range(at, at + PROMPT_SAMPLES)]
            rows.append(jnp.concatenate(pieces, axis=1))
    rows = jnp.concatenate(rows, axis=0)
    tiles = [rows[:, t * 128 : (t + 1) * 128] for t in range(LANES // 128)]
    w = w_ref[...].astype(jnp.float32).reshape(3, 9, own, C)
    taps = [w[:, t].reshape(3 * own, C) for t in range(9)]
    left = jnp.broadcast_to(side_ref[0] == 0, (3 * own, 128))
    for d in range(0, n, 2):
        both = []
        for e in (d, d + 1):
            pieces = [tap[:, e * own : (e + 1) * own] for tap in taps]
            pieces.append(jnp.zeros((3 * own, 256 - 9 * own), jnp.float32))
            share = jnp.concatenate(pieces, axis=1)
            both += [jnp.where(left, share[:, :128], share[:, 128:])] + tiles
        both = jnp.concatenate(both, axis=0).astype(jnp.bfloat16)
        o_ref[d // 2 * both.shape[0] : (d // 2 + 1) * both.shape[0], :] = both


def column(row_ref, width):
    tile = jnp.transpose(jnp.broadcast_to(row_ref[...], (128, row_ref.shape[1])))
    return jnp.concatenate([tile] * (width // 128), axis=1)


def active_kernel(n, got_ref, entry_ref, bias_ref, gain_ref, first_ref, x_hbm, stream_ref, col_ref, row_ref, x_ref, sem):
    own = C // n
    frames = n // PROMPT_SAMPLES * BLOCK_FRAMES
    each = LATENT_CHANNELS * BLOCK_FRAMES // n
    taps = 9 * LATENT_CHANNELS
    ahead = -(-own // 16) * 16
    first = pl.multiple_of(first_ref[0], 8)
    bias = column(bias_ref, LANES)
    half_gain = (column(gain_ref, LANES) * 0.5).astype(jnp.bfloat16)
    full = jnp.transpose(entry_ref[...].astype(jnp.float32))
    row_ref[:, 0 : 3 * taps] = full
    row_ref[:, 3 * taps : 3 * taps + 128] = bias[:, 0:128]
    mine = row_ref[pl.ds(first, own), :]
    mine_bias = mine[:, 3 * taps : 3 * taps + 128]
    mine_bias = jnp.concatenate([mine_bias] * (LANES // 128), axis=1)
    spare = jnp.zeros((ahead - own, 3 * taps), jnp.float32)
    weight = jnp.concatenate([mine[:, : 3 * taps], spare, full], axis=0).astype(jnp.bfloat16)
    per_frame = LATENT_CHANNELS // each
    blocks = n // PROMPT_SAMPLES
    lats = got_ref[...].astype(jnp.float32).reshape(n, -1, 128)[:, 3 * own :]
    lats = lats.reshape(n, LANES // 128, blocks * each, 128)
    lats = jnp.concatenate([lats[:, t] for t in range(LANES // 128)], axis=2)
    lats = lats.reshape(BLOCK_FRAMES, per_frame, blocks, each, LANES)
    copies = []
    for f in range(frames):
        b, g = divmod(f, BLOCK_FRAMES)
        lat = lats[g, :, b].reshape(LATENT_CHANNELS, LANES)
        for j in range(3):
            for k in range(3):
                moved = shifted(lat, LATENT_COLUMNS * (j - 1) + k - 1)
                moved = jnp.where(shift_mask(j, k), moved, 0.0)
                at = f * taps + (3 * j + k) * LATENT_CHANNELS
                col_ref[at : at + LATENT_CHANNELS, :] = moved.astype(jnp.bfloat16)
        least = max(f - 2, 0)
        z = jnp.dot(
            weight[:, (2 - (f - least)) * taps :],
            col_ref[least * taps : (f + 1) * taps, :],
            preferred_element_type=jnp.float32,
        )
        stream_ref[f] = (z[:own] + mine_bias).astype(jnp.bfloat16).astype(jnp.float32)
        s = z[ahead:] + bias
        scale = lax.rsqrt(jnp.sum(s * s, axis=0, keepdims=True) * (1.0 / C) + 1e-06)
        half = s.astype(jnp.bfloat16) * half_gain * scale.astype(jnp.bfloat16)
        x_ref[f * C : (f + 1) * C, :] = half + half * jnp.tanh(half)
        rows = pl.ds(f * C, C)
        copy = pltpu.make_async_copy(x_ref.at[rows], x_hbm.at[rows], sem.at[f])
        copy.start()
        copies.append(copy)
    for copy in copies:
        copy.wait()


def branch_kernel(n, got_ref, w_ref, x_hbm, stream_ref, bias_ref, first_ref, side_ref, count_ref, o_ref, x_ref, bias_col_ref, out_ref, sem):
    own = C // n
    frames = n // PROMPT_SAMPLES * BLOCK_FRAMES
    copies = []
    for f in range(frames):
        rows = pl.ds(f * C, C)
        copy = pltpu.make_async_copy(x_hbm.at[rows], x_ref.at[rows], sem.at[f])
        copy.start()
        copies.append(copy)
    mine = got_ref[...].astype(jnp.float32).reshape(n, -1, 128)[:, : 3 * own].reshape(n, 3, own, 128)
    other = w_ref[...].astype(jnp.float32).reshape(n, 3, own, 128)
    left = jnp.broadcast_to(side_ref[0] == 0, other.shape)
    w = jnp.concatenate([jnp.where(left, mine, other), jnp.where(left, other, mine)], axis=3)
    w = jnp.transpose(w, (1, 0, 2, 3)).reshape(3 * C, 256)
    weight = jnp.transpose(w.astype(jnp.bfloat16))[: -(-9 * own // 16) * 16]
    bias_col_ref[...] = column(bias_ref, 128)
    bias = bias_col_ref[pl.ds(pl.multiple_of(first_ref[0], 8), own), :]
    bias = jnp.concatenate([bias] * (LANES // 128), axis=1)
    lane = lax.broadcasted_iota(jnp.int32, (1, LANES), 1)
    count = jnp.zeros((1, LANES), jnp.int32)
    for s in range(PROMPT_SAMPLES):
        count = jnp.where(lane // HW == s, count_ref[s], count)
    for f in range(frames):
        copies[f].wait()
        least = max(f - 2, 0)
        z = jnp.dot(
            weight[:, (2 - (f - least)) * C :],
            x_ref[least * C : (f + 1) * C, :],
            preferred_element_type=jnp.float32,
        )
        total = stream_ref[f] + bias
        for k in range(3):
            part = None
            for j in range(3):
                tap = z[(3 * j + k) * own : (3 * j + k + 1) * own]
                if j != 1:
                    tap = jnp.where(shift_mask(j, 1), shifted(tap, LATENT_COLUMNS * (j - 1)), 0.0)
                part = tap if part is None else part + tap
            if k != 1:
                part = jnp.where(shift_mask(1, k), shifted(part, k - 1), 0.0)
            total = total + part
        out_ref[f] = jnp.where(count > f, total, 0.0)
        b, g = divmod(f, BLOCK_FRAMES)
        if g == BLOCK_FRAMES - 1:
            parts = [out_ref[b * BLOCK_FRAMES + t] for t in range(BLOCK_FRAMES)]
            for s in range(0, PROMPT_SAMPLES, 2):
                both = [
                    jnp.concatenate([p[:, t * HW : (t + 1) * HW] for p in parts], axis=1) for t in (s, s + 1)
                ]
                at = (b * PROMPT_SAMPLES + s) * own
                o_ref[at : at + 2 * own, :] = jnp.concatenate(both, axis=0).astype(jnp.bfloat16)


def transpose_kernel(x_ref, o_ref):
    o_ref[...] = jnp.transpose(x_ref[...])


def call(body, out, ins, outs, scratch=(), flops=0, moved=0, limit=8):
    return pl.pallas_call(
        body,
        out_shape=out,
        in_specs=ins,
        out_specs=outs,
        scratch_shapes=list(scratch),
        compiler_params=pltpu.CompilerParams(vmem_limit_bytes=limit * 1024 * 1024),
        cost_estimate=pl.CostEstimate(flops=flops, bytes_accessed=moved, transcendentals=0),
    )


def by_channel(n, latents, counts, entry_kernel, entry_bias, gain, kernel, bias):
    own = C // n
    frames = n // PROMPT_SAMPLES * BLOCK_FRAMES
    first = (lax.axis_index("tm") * own).astype(jnp.int32).reshape(1)
    shape = jax.ShapeDtypeStruct
    bf16, f32 = jnp.bfloat16, jnp.float32
    side = lax.axis_index("groups").astype(jnp.int32).reshape(1)
    each = latents.shape[1] // HW * (n // PROMPT_SAMPLES)
    height = 3 * own + each * LANES // 128
    parcels = call(
        functools.partial(parcels_kernel, n), shape((n * height, 128), bf16), [VMEM, VMEM, SMEM], VMEM
    )(latents, kernel, side)
    got = lax.all_to_all(parcels, "tm", split_axis=0, concat_axis=0, tiled=True)
    other = got.reshape(n, height, 128)[:, : 3 * own].reshape(n * 3 * own, 128)
    other = lax.ppermute(other, "groups", [(0, 1), (1, 0)])
    active, stream = call(
        functools.partial(active_kernel, n),
        (shape((frames * C, LANES), bf16), shape((frames, own, LANES), f32)),
        [VMEM, VMEM, VMEM, VMEM, SMEM],
        (ANY, VMEM),
        [
            pltpu.VMEM((frames * 9 * LATENT_CHANNELS, LANES), bf16),
            pltpu.VMEM((C, 27 * LATENT_CHANNELS + 128), f32),
            pltpu.VMEM((frames * C, LANES), bf16),
            pltpu.SemaphoreType.DMA((frames,)),
        ],
        flops=2 * frames * LANES * 432 * C,
        moved=20_000_000,
        limit=32,
    )(
        got,
        entry_kernel.reshape(27 * LATENT_CHANNELS, C),
        entry_bias.reshape(1, C),
        gain.reshape(1, C),
        first,
    )
    out = call(
        functools.partial(branch_kernel, n),
        shape((n * own, BLOCK_FRAMES * HW), bf16),
        [VMEM, VMEM, ANY, VMEM, VMEM, SMEM, SMEM, SMEM],
        VMEM,
        [
            pltpu.VMEM((frames * C, LANES), bf16),
            pltpu.VMEM((C, 128), f32),
            pltpu.VMEM((frames, own, LANES), f32),
            pltpu.SemaphoreType.DMA((frames,)),
        ],
        flops=2 * frames * LANES * 27 * C * own,
        moved=20_000_000,
        limit=32,
    )(got, other, active, stream, bias.reshape(1, C), first, side, counts)
    out = lax.all_to_all(out, "tm", split_axis=0, concat_axis=0, tiled=True)
    out = call(transpose_kernel, shape((BLOCK_FRAMES * HW, C), bf16), [VMEM], VMEM)(out)
    return out.reshape(BLOCK_FRAMES, LATENT_ROWS, LATENT_COLUMNS, C)


def from_behind(block, axis, distance):
    devices = range(lax.axis_size(axis))
    route = [(i - distance, i) for i in devices if i - distance in devices]
    return lax.ppermute(block, axis, route)


def causal_conv(frames, weight):
    frames_out = frames.shape[0] - 2
    inputs = frames.shape[3]
    padded = jnp.pad(frames, ((0, 0), (1, 1), (1, 1), (0, 0)))
    total = jnp.zeros((frames_out * LATENT_ROWS * LATENT_COLUMNS, weight.shape[2]), jnp.float32)
    for time_tap in range(3):
        for row_tap in range(3):
            for col_tap in range(3):
                window = padded[
                    time_tap : time_tap + frames_out,
                    row_tap : row_tap + LATENT_ROWS,
                    col_tap : col_tap + LATENT_COLUMNS,
                    :,
                ]
                window = window.reshape(frames_out * LATENT_ROWS * LATENT_COLUMNS, inputs)
                tap = 9 * time_tap + 3 * row_tap + col_tap
                total = total + jnp.dot(window, weight[tap], preferred_element_type=jnp.float32)
    return total


def activate(stream, norm_scale_gain):
    values = stream.astype(jnp.float32)
    scale = lax.rsqrt(jnp.mean(values * values, axis=-1, keepdims=True) + 1e-06)
    return jax.nn.silu(values * scale * norm_scale_gain).astype(jnp.bfloat16)


def to_cells(planes):
    return jnp.transpose(
        planes.reshape(planes.shape[0], LATENT_CHANNELS, LATENT_ROWS, LATENT_COLUMNS), (0, 2, 3, 1)
    )


def by_block(
    sharded_latents,
    sample_frame_count,
    entry_kernel,
    entry_bias,
    norm_scale_gain,
    residual_kernel,
    residual_bias,
):
    gathered_latents = lax.all_to_all(
        sharded_latents, "tm", split_axis=0, concat_axis=1, tiled=True
    )
    latent_volume = gathered_latents.reshape(
        BLOCK_FRAMES, LATENT_CHANNELS, LATENT_ROWS * LATENT_COLUMNS
    )
    position = lax.axis_index("tm")
    block = position // PROMPT_SAMPLES
    sample = position % PROMPT_SAMPLES
    keep = block > 0
    earlier = from_behind(latent_volume, "tm", PROMPT_SAMPLES)
    earlier = jnp.where(keep, earlier, jnp.zeros_like(earlier))
    frames = to_cells(jnp.concatenate([earlier, latent_volume], axis=0))
    widened = (causal_conv(frames, entry_kernel) + entry_bias).astype(jnp.bfloat16)
    active_all = activate(widened, norm_scale_gain).reshape(
        BLOCK_FRAMES + 2, LATENT_ROWS, LATENT_COLUMNS, C
    )
    behind = jnp.where(keep, active_all[:2], jnp.zeros_like(active_all[:2]))
    extended = jnp.concatenate([behind, active_all[2:]], axis=0)
    stream = widened[2 * LATENT_ROWS * LATENT_COLUMNS :]
    kernel_all = lax.all_gather(residual_kernel, "tm", axis=1, tiled=True)
    branch = causal_conv(extended, kernel_all)
    total = (stream.astype(jnp.float32) + (branch + residual_bias)).reshape(
        BLOCK_FRAMES, LATENT_ROWS, LATENT_COLUMNS, C
    )
    limit = jnp.sum(jnp.where(jnp.arange(PROMPT_SAMPLES) == sample, sample_frame_count, 0))
    frame_index = block * BLOCK_FRAMES + jnp.arange(BLOCK_FRAMES)
    valid = (frame_index < limit)[:, None, None, None]
    return jnp.where(valid, total, jnp.zeros_like(total)).astype(jnp.bfloat16)


def solution(mesh):
    n = mesh.shape["tm"]
    cells = BLOCK_FRAMES * LATENT_CHANNELS * HW
    fits = mesh.shape["groups"] == 2 and 9 * (C // n) <= 256 and n * HW % 128 == 0
    whole_rows = fits and cells % (n * HW) == 0 and C % n == 0 and (C // n) % 8 == 0 and n % PROMPT_SAMPLES == 0
    body = functools.partial(by_channel, n) if whole_rows else by_block
    in_specs = (P("groups", "tm"), P("groups"), P(), P(), P(), P(None, "tm", None), P())
    out_specs = P(("groups", "tm"), None, None, None)
    return jax.shard_map(body, mesh=mesh, in_specs=in_specs, out_specs=out_specs, check_vma=False)
```

```python
import functools

import jax
import jax.numpy as jnp
from jax import lax
from jax.experimental import pallas as pl
from jax.experimental.pallas import tpu as pltpu
from jax.sharding import PartitionSpec as P

LATENT_CHANNELS = 16
C = 384
PROMPT_SAMPLES = 8
BLOCK_FRAMES = 4
LATENT_ROWS = 6
LATENT_COLUMNS = 16
HW = LATENT_ROWS * LATENT_COLUMNS
LANES = PROMPT_SAMPLES * HW
VMEM = pl.BlockSpec(memory_space=pltpu.VMEM)
SMEM = pl.BlockSpec(memory_space=pltpu.SMEM)


def shift_mask(j, k):
    lane = lax.broadcasted_iota(jnp.int32, (1, LANES), 1)
    row = (lane % HW) // LATENT_COLUMNS
    col = lane % LATENT_COLUMNS
    ok = lane >= 0
    if j == 0:
        ok = row > 0
    elif j == 2:
        ok = row < LATENT_ROWS - 1
    if k == 0:
        ok = ok & (col > 0)
    elif k == 2:
        ok = ok & (col < LATENT_COLUMNS - 1)
    return ok


def shifted(x, delta):
    return x if delta == 0 else pltpu.roll(x, (-delta) % x.shape[1], 1)


def parcels_kernel(n, x_ref, w_ref, side_ref, o_ref):
    own = C // n
    x = x_ref[...].astype(jnp.float32)
    rows = []
    for b in range(x.shape[0] // PROMPT_SAMPLES):
        for c in range(x.shape[1] // HW):
            at = b * PROMPT_SAMPLES
            pieces = [x[r : r + 1, c * HW : (c + 1) * HW] for r in range(at, at + PROMPT_SAMPLES)]
            rows.append(jnp.concatenate(pieces, axis=1))
    rows = jnp.concatenate(rows, axis=0)
    tiles = [rows[:, t * 128 : (t + 1) * 128] for t in range(LANES // 128)]
    w = w_ref[...].astype(jnp.float32).reshape(3, 9, own, C)
    taps = [w[:, t].reshape(3 * own, C) for t in range(9)]
    left = jnp.broadcast_to(side_ref[0] == 0, (3 * own, 128))
    for d in range(0, n, 2):
        both = []
        for e in (d, d + 1):
            pieces = [tap[:, e * own : (e + 1) * own] for tap in taps]
            pieces.append(jnp.zeros((3 * own, 256 - 9 * own), jnp.float32))
            share = jnp.concatenate(pieces, axis=1)
            both += [jnp.where(left, share[:, :128], share[:, 128:])] + tiles
        both = jnp.concatenate(both, axis=0).astype(jnp.bfloat16)
        o_ref[d // 2 * both.shape[0] : (d // 2 + 1) * both.shape[0], :] = both


def column(row_ref, width):
    tile = jnp.transpose(jnp.broadcast_to(row_ref[...], (128, row_ref.shape[1])))
    return jnp.concatenate([tile] * (width // 128), axis=1)


def thirds(x):
    parts = []
    for _ in range(3):
        part = x.astype(jnp.bfloat16).astype(jnp.float32)
        parts.append(part)
        x = x - part
    return parts


def params_kernel(n, entry_ref, bias_ref, gain_ref, after_ref, first_ref, o_ref, row_ref):
    own = C // n
    depth = 27 * LATENT_CHANNELS
    first = pl.multiple_of(first_ref[0], 8)
    lane = lax.broadcasted_iota(jnp.int32, (C, 16), 1)

    def spread(ref):
        tile = column(ref, 128)[:, :16]
        out = jnp.zeros((C, 16), jnp.float32)
        for t, part in enumerate(thirds(tile)):
            out = jnp.where(lane == t, part, out)
        return out

    half_gain = column(gain_ref, 128) * 0.5
    gap = jnp.zeros((C, 512 - depth - 16), jnp.float32)
    weight = jnp.transpose(entry_ref[...].astype(jnp.float32))
    full = jnp.concatenate([weight, spread(bias_ref), gap, half_gain], axis=1)
    row_ref[0:C, :] = full
    row_ref[C : 2 * C, :] = jnp.concatenate([jnp.zeros_like(weight), spread(after_ref), gap, half_gain], axis=1)
    mine = row_ref[pl.ds(first, own), :]
    after = row_ref[pl.ds(first + C, own), :]
    o_ref[...] = jnp.concatenate([mine, after, full], axis=0).astype(jnp.bfloat16)


def active_kernel(n, got_ref, params_ref, x_ref, stream_ref, col_ref):
    own = C // n
    frames = n // PROMPT_SAMPLES * BLOCK_FRAMES
    each = LATENT_CHANNELS * BLOCK_FRAMES // n
    taps = 9 * LATENT_CHANNELS
    weight = params_ref[:, : 3 * taps + 16]
    half_gain = jnp.concatenate([params_ref[2 * own :, 512:]] * (LANES // 128), axis=1)
    ones = (lax.broadcasted_iota(jnp.int32, (16, LANES), 0) < 3).astype(jnp.float32).astype(jnp.bfloat16)
    per_frame = LATENT_CHANNELS // each
    blocks = n // PROMPT_SAMPLES
    lats = got_ref[...].astype(jnp.float32).reshape(n, -1, 128)[:, 3 * own :]
    lats = lats.reshape(n, LANES // 128, blocks * each, 128)
    lats = jnp.concatenate([lats[:, t] for t in range(LANES // 128)], axis=2)
    lats = lats.reshape(BLOCK_FRAMES, per_frame, blocks, each, LANES)
    for f in range(frames):
        b, g = divmod(f, BLOCK_FRAMES)
        lat = lats[g, :, b].reshape(LATENT_CHANNELS, LANES)
        for j in range(3):
            for k in range(3):
                moved = shifted(lat, LATENT_COLUMNS * (j - 1) + k - 1)
                moved = jnp.where(shift_mask(j, k), moved, 0.0)
                at = f * taps + (3 * j + k) * LATENT_CHANNELS
                col_ref[at : at + LATENT_CHANNELS, :] = moved.astype(jnp.bfloat16)
        least = max(f - 2, 0)
        z = jnp.dot(
            weight[:, (2 - (f - least)) * taps :],
            jnp.concatenate([col_ref[least * taps : (f + 1) * taps, :], ones], axis=0),
            preferred_element_type=jnp.float32,
        )
        stream_ref[f] = z[:own].astype(jnp.bfloat16).astype(jnp.float32) + z[own : 2 * own]
        s = z[2 * own :]
        scale = lax.rsqrt(jnp.sum(s * s, axis=0, keepdims=True) * (1.0 / C) + 1e-06)
        half = s.astype(jnp.bfloat16) * half_gain * scale.astype(jnp.bfloat16)
        x_ref[f * C : (f + 1) * C, :] = half + half * jnp.tanh(half)


def branch_kernel(n, got_ref, w_ref, x_ref, stream_ref, side_ref, count_ref, o_ref, out_ref):
    own = C // n
    frames = n // PROMPT_SAMPLES * BLOCK_FRAMES
    mine = got_ref[...].astype(jnp.float32).reshape(n, -1, 128)[:, : 3 * own].reshape(n, 3, own, 128)
    other = w_ref[...].astype(jnp.float32).reshape(n, 3, own, 128)
    left = jnp.broadcast_to(side_ref[0] == 0, other.shape)
    w = jnp.concatenate([jnp.where(left, mine, other), jnp.where(left, other, mine)], axis=3)
    w = jnp.transpose(w, (1, 0, 2, 3)).reshape(3 * C, 256)
    weight = jnp.transpose(w.astype(jnp.bfloat16))[: -(-9 * own // 16) * 16]
    lane = lax.broadcasted_iota(jnp.int32, (1, LANES), 1)
    count = jnp.zeros((1, LANES), jnp.int32)
    for s in range(PROMPT_SAMPLES):
        count = jnp.where(lane // HW == s, count_ref[s], count)
    for f in range(frames):
        least = max(f - 2, 0)
        z = jnp.dot(
            weight[:, (2 - (f - least)) * C :],
            x_ref[least * C : (f + 1) * C, :],
            preferred_element_type=jnp.float32,
        )
        total = stream_ref[f]
        for k in range(3):
            part = None
            for j in range(3):
                tap = z[(3 * j + k) * own : (3 * j + k + 1) * own]
                if j != 1:
                    tap = jnp.where(shift_mask(j, 1), shifted(tap, LATENT_COLUMNS * (j - 1)), 0.0)
                part = tap if part is None else part + tap
            if k != 1:
                part = jnp.where(shift_mask(1, k), shifted(part, k - 1), 0.0)
            total = total + part
        out_ref[f] = jnp.where(count > f, total, 0.0)
        b, g = divmod(f, BLOCK_FRAMES)
        if g == BLOCK_FRAMES - 1:
            parts = [out_ref[b * BLOCK_FRAMES + t] for t in range(BLOCK_FRAMES)]
            for s in range(0, PROMPT_SAMPLES, 2):
                both = [
                    jnp.concatenate([p[:, t * HW : (t + 1) * HW] for p in parts], axis=1) for t in (s, s + 1)
                ]
                at = (b * PROMPT_SAMPLES + s) * own
                o_ref[at : at + 2 * own, :] = jnp.concatenate(both, axis=0).astype(jnp.bfloat16)


def transpose_kernel(x_ref, o_ref):
    o_ref[...] = jnp.transpose(x_ref[...])


def call(body, out, ins, outs, scratch=(), flops=0, moved=0, limit=8):
    return pl.pallas_call(
        body,
        out_shape=out,
        in_specs=ins,
        out_specs=outs,
        scratch_shapes=list(scratch),
        compiler_params=pltpu.CompilerParams(vmem_limit_bytes=limit * 1024 * 1024),
        cost_estimate=pl.CostEstimate(flops=flops, bytes_accessed=moved, transcendentals=0),
    )


def by_channel(n, latents, counts, entry_kernel, entry_bias, gain, kernel, bias):
    own = C // n
    frames = n // PROMPT_SAMPLES * BLOCK_FRAMES
    first = (lax.axis_index("tm") * own).astype(jnp.int32).reshape(1)
    shape = jax.ShapeDtypeStruct
    bf16, f32 = jnp.bfloat16, jnp.float32
    side = lax.axis_index("groups").astype(jnp.int32).reshape(1)
    each = latents.shape[1] // HW * (n // PROMPT_SAMPLES)
    height = 3 * own + each * LANES // 128
    parcels = call(
        functools.partial(parcels_kernel, n), shape((n * height, 128), bf16), [VMEM, VMEM, SMEM], VMEM
    )(latents, kernel, side)
    got = lax.all_to_all(parcels, "tm", split_axis=0, concat_axis=0, tiled=True)
    other = got.reshape(n, height, 128)[:, : 3 * own].reshape(n * 3 * own, 128)
    other = lax.ppermute(other, "groups", [(0, 1), (1, 0)])
    params = call(
        functools.partial(params_kernel, n),
        shape((2 * own + C, 640), bf16),
        [VMEM, VMEM, VMEM, VMEM, SMEM],
        VMEM,
        [pltpu.VMEM((2 * C, 640), f32)],
        flops=500_000_000,
        moved=2_000_000,
    )(
        entry_kernel.reshape(27 * LATENT_CHANNELS, C),
        entry_bias.reshape(1, C),
        gain.reshape(1, C),
        bias.reshape(1, C),
        first,
    )
    active, stream = call(
        functools.partial(active_kernel, n),
        (shape((frames * C, LANES), bf16), shape((frames, own, LANES), f32)),
        [VMEM, VMEM],
        (VMEM, VMEM),
        [pltpu.VMEM((frames * 9 * LATENT_CHANNELS, LANES), bf16)],
        flops=2 * frames * LANES * 432 * C,
        moved=20_000_000,
        limit=24,
    )(got, params)
    out = call(
        functools.partial(branch_kernel, n),
        shape((n * own, BLOCK_FRAMES * HW), bf16),
        [VMEM, VMEM, VMEM, VMEM, SMEM, SMEM],
        VMEM,
        [pltpu.VMEM((frames, own, LANES), f32)],
        flops=2 * frames * LANES * 27 * C * own,
        moved=20_000_000,
        limit=24,
    )(got, other, active, stream, side, counts)
    out = lax.all_to_all(out, "tm", split_axis=0, concat_axis=0, tiled=True)
    out = call(transpose_kernel, shape((BLOCK_FRAMES * HW, C), bf16), [VMEM], VMEM)(out)
    return out.reshape(BLOCK_FRAMES, LATENT_ROWS, LATENT_COLUMNS, C)


def from_behind(block, axis, distance):
    devices = range(lax.axis_size(axis))
    route = [(i - distance, i) for i in devices if i - distance in devices]
    return lax.ppermute(block, axis, route)


def causal_conv(frames, weight):
    frames_out = frames.shape[0] - 2
    inputs = frames.shape[3]
    padded = jnp.pad(frames, ((0, 0), (1, 1), (1, 1), (0, 0)))
    total = jnp.zeros((frames_out * LATENT_ROWS * LATENT_COLUMNS, weight.shape[2]), jnp.float32)
    for time_tap in range(3):
        for row_tap in range(3):
            for col_tap in range(3):
                window = padded[
                    time_tap : time_tap + frames_out,
                    row_tap : row_tap + LATENT_ROWS,
                    col_tap : col_tap + LATENT_COLUMNS,
                    :,
                ]
                window = window.reshape(frames_out * LATENT_ROWS * LATENT_COLUMNS, inputs)
                tap = 9 * time_tap + 3 * row_tap + col_tap
                total = total + jnp.dot(window, weight[tap], preferred_element_type=jnp.float32)
    return total


def activate(stream, norm_scale_gain):
    values = stream.astype(jnp.float32)
    scale = lax.rsqrt(jnp.mean(values * values, axis=-1, keepdims=True) + 1e-06)
    return jax.nn.silu(values * scale * norm_scale_gain).astype(jnp.bfloat16)


def to_cells(planes):
    return jnp.transpose(
        planes.reshape(planes.shape[0], LATENT_CHANNELS, LATENT_ROWS, LATENT_COLUMNS), (0, 2, 3, 1)
    )


def by_block(
    sharded_latents,
    sample_frame_count,
    entry_kernel,
    entry_bias,
    norm_scale_gain,
    residual_kernel,
    residual_bias,
):
    gathered_latents = lax.all_to_all(
        sharded_latents, "tm", split_axis=0, concat_axis=1, tiled=True
    )
    latent_volume = gathered_latents.reshape(
        BLOCK_FRAMES, LATENT_CHANNELS, LATENT_ROWS * LATENT_COLUMNS
    )
    position = lax.axis_index("tm")
    block = position // PROMPT_SAMPLES
    sample = position % PROMPT_SAMPLES
    keep = block > 0
    earlier = from_behind(latent_volume, "tm", PROMPT_SAMPLES)
    earlier = jnp.where(keep, earlier, jnp.zeros_like(earlier))
    frames = to_cells(jnp.concatenate([earlier, latent_volume], axis=0))
    widened = (causal_conv(frames, entry_kernel) + entry_bias).astype(jnp.bfloat16)
    active_all = activate(widened, norm_scale_gain).reshape(
        BLOCK_FRAMES + 2, LATENT_ROWS, LATENT_COLUMNS, C
    )
    behind = jnp.where(keep, active_all[:2], jnp.zeros_like(active_all[:2]))
    extended = jnp.concatenate([behind, active_all[2:]], axis=0)
    stream = widened[2 * LATENT_ROWS * LATENT_COLUMNS :]
    kernel_all = lax.all_gather(residual_kernel, "tm", axis=1, tiled=True)
    branch = causal_conv(extended, kernel_all)
    total = (stream.astype(jnp.float32) + (branch + residual_bias)).reshape(
        BLOCK_FRAMES, LATENT_ROWS, LATENT_COLUMNS, C
    )
    limit = jnp.sum(jnp.where(jnp.arange(PROMPT_SAMPLES) == sample, sample_frame_count, 0))
    frame_index = block * BLOCK_FRAMES + jnp.arange(BLOCK_FRAMES)
    valid = (frame_index < limit)[:, None, None, None]
    return jnp.where(valid, total, jnp.zeros_like(total)).astype(jnp.bfloat16)


def solution(mesh):
    n = mesh.shape["tm"]
    cells = BLOCK_FRAMES * LATENT_CHANNELS * HW
    fits = mesh.shape["groups"] == 2 and 9 * (C // n) <= 256 and n * HW % 128 == 0
    whole_rows = fits and cells % (n * HW) == 0 and C % n == 0 and (C // n) % 8 == 0 and n % PROMPT_SAMPLES == 0
    body = functools.partial(by_channel, n) if whole_rows else by_block
    in_specs = (P("groups", "tm"), P("groups"), P(), P(), P(), P(None, "tm", None), P())
    out_specs = P(("groups", "tm"), None, None, None)
    return jax.shard_map(body, mesh=mesh, in_specs=in_specs, out_specs=out_specs, check_vma=False)
```

```python
import functools

import jax
import jax.numpy as jnp
from jax import lax
from jax.experimental import pallas as pl
from jax.experimental.pallas import tpu as pltpu
from jax.sharding import PartitionSpec as P

LATENT_CHANNELS = 16
C = 384
PROMPT_SAMPLES = 8
BLOCK_FRAMES = 4
LATENT_ROWS = 6
LATENT_COLUMNS = 16
HW = LATENT_ROWS * LATENT_COLUMNS
LANES = PROMPT_SAMPLES * HW
VMEM = pl.BlockSpec(memory_space=pltpu.VMEM)
SMEM = pl.BlockSpec(memory_space=pltpu.SMEM)


def shift_mask(j, k):
    lane = lax.broadcasted_iota(jnp.int32, (1, LANES), 1)
    row = (lane % HW) // LATENT_COLUMNS
    col = lane % LATENT_COLUMNS
    ok = lane >= 0
    if j == 0:
        ok = row > 0
    elif j == 2:
        ok = row < LATENT_ROWS - 1
    if k == 0:
        ok = ok & (col > 0)
    elif k == 2:
        ok = ok & (col < LATENT_COLUMNS - 1)
    return ok


def shifted(x, delta):
    return x if delta == 0 else pltpu.roll(x, (-delta) % x.shape[1], 1)


def parcels_kernel(n, x_ref, w_ref, side_ref, o_ref):
    own = C // n
    x = x_ref[...].astype(jnp.float32)
    rows = []
    for b in range(x.shape[0] // PROMPT_SAMPLES):
        for c in range(x.shape[1] // HW):
            at = b * PROMPT_SAMPLES
            pieces = [x[r : r + 1, c * HW : (c + 1) * HW] for r in range(at, at + PROMPT_SAMPLES)]
            rows.append(jnp.concatenate(pieces, axis=1))
    rows = jnp.concatenate(rows, axis=0)
    tiles = [rows[:, t * 128 : (t + 1) * 128] for t in range(LANES // 128)]
    w = w_ref[...].astype(jnp.float32).reshape(3, 9, own, C)
    taps = [w[:, t].reshape(3 * own, C) for t in range(9)]
    left = jnp.broadcast_to(side_ref[0] == 0, (3 * own, 128))
    for d in range(0, n, 2):
        both = []
        for e in (d, d + 1):
            pieces = [tap[:, e * own : (e + 1) * own] for tap in taps]
            pieces.append(jnp.zeros((3 * own, 256 - 9 * own), jnp.float32))
            share = jnp.concatenate(pieces, axis=1)
            half = len(tiles) // 2
            own_tiles = tiles[half:] if e % 2 else tiles[:half]
            both += [jnp.where(left, share[:, :128], share[:, 128:])] + own_tiles
        both = jnp.concatenate(both, axis=0).astype(jnp.bfloat16)
        o_ref[d // 2 * both.shape[0] : (d // 2 + 1) * both.shape[0], :] = both


def column(rows):
    parts = [jnp.transpose(jnp.broadcast_to(rows[t : t + 1], (128, 128))) for t in range(rows.shape[0])]
    return jnp.concatenate(parts, axis=0)


def thirds(x):
    parts = []
    for _ in range(3):
        part = x.astype(jnp.bfloat16).astype(jnp.float32)
        parts.append(part)
        x = x - part
    return parts


def params_kernel(n, entry_ref, vectors_ref, first_ref, o_ref, row_ref):
    own = C // n
    depth = 27 * LATENT_CHANNELS
    tall = C // 128
    first = pl.multiple_of(first_ref[0], 8)
    lane = lax.broadcasted_iota(jnp.int32, (C, 16), 1)

    def spread(t):
        tile = column(vectors_ref[t * tall : (t + 1) * tall])[:, :16]
        out = jnp.zeros((C, 16), jnp.float32)
        for t, part in enumerate(thirds(tile)):
            out = jnp.where(lane == t, part, out)
        return out

    half_gain = column(vectors_ref[tall : 2 * tall]) * 0.5
    gap = jnp.zeros((C, 512 - depth - 16), jnp.float32)
    weight = jnp.transpose(entry_ref[...].astype(jnp.float32))
    full = jnp.concatenate([weight, spread(0), gap, half_gain], axis=1)
    row_ref[0:C, :] = full
    row_ref[C : 2 * C, :] = jnp.concatenate([jnp.zeros_like(weight), spread(2), gap, half_gain], axis=1)
    mine = row_ref[pl.ds(first, own), :]
    after = row_ref[pl.ds(first + C, own), :]
    o_ref[...] = jnp.concatenate([mine, after, full], axis=0).astype(jnp.bfloat16)


def active_kernel(n, got_ref, lat_ref, params_ref, odd_ref, x_ref, stream_ref, col_ref):
    own = C // n
    frames = n // PROMPT_SAMPLES * BLOCK_FRAMES
    each = LATENT_CHANNELS * BLOCK_FRAMES // n
    taps = 9 * LATENT_CHANNELS
    weight = params_ref[:, : 3 * taps + 16]
    half_gain = jnp.concatenate([params_ref[2 * own :, 512:]] * (LANES // 128), axis=1)
    ones = (lax.broadcasted_iota(jnp.int32, (16, LANES), 0) < 3).astype(jnp.float32).astype(jnp.bfloat16)
    per_frame = LATENT_CHANNELS // each
    blocks = n // PROMPT_SAMPLES
    mine = got_ref[...].astype(jnp.float32).reshape(n, -1, 128)[:, 3 * own :]
    other = lat_ref[...].astype(jnp.float32).reshape(mine.shape)
    even = jnp.broadcast_to(odd_ref[0] == 0, mine.shape)
    lats = jnp.concatenate([jnp.where(even, mine, other), jnp.where(even, other, mine)], axis=1)
    lats = lats.reshape(n, LANES // 128, blocks * each, 128)
    lats = jnp.concatenate([lats[:, t] for t in range(LANES // 128)], axis=2)
    lats = lats.reshape(BLOCK_FRAMES, per_frame, blocks, each, LANES)
    for f in range(frames):
        b, g = divmod(f, BLOCK_FRAMES)
        lat = lats[g, :, b].reshape(LATENT_CHANNELS, LANES)
        for j in range(3):
            for k in range(3):
                moved = shifted(lat, LATENT_COLUMNS * (j - 1) + k - 1)
                moved = jnp.where(shift_mask(j, k), moved, 0.0)
                at = f * taps + (3 * j + k) * LATENT_CHANNELS
                col_ref[at : at + LATENT_CHANNELS, :] = moved.astype(jnp.bfloat16)
        least = max(f - 2, 0)
        z = jnp.dot(
            weight[:, (2 - (f - least)) * taps :],
            jnp.concatenate([col_ref[least * taps : (f + 1) * taps, :], ones], axis=0),
            preferred_element_type=jnp.float32,
        )
        stream_ref[f] = z[:own].astype(jnp.bfloat16).astype(jnp.float32) + z[own : 2 * own]
        s = z[2 * own :]
        scale = lax.rsqrt(jnp.sum(s * s, axis=0, keepdims=True) * (1.0 / C) + 1e-06)
        half = s.astype(jnp.bfloat16) * half_gain * scale.astype(jnp.bfloat16)
        x_ref[f * C : (f + 1) * C, :] = half + half * jnp.tanh(half)


def branch_kernel(n, got_ref, w_ref, x_ref, stream_ref, side_ref, count_ref, o_ref, out_ref):
    own = C // n
    frames = n // PROMPT_SAMPLES * BLOCK_FRAMES
    mine = got_ref[...].astype(jnp.float32).reshape(n, -1, 128)[:, : 3 * own].reshape(n, 3, own, 128)
    other = w_ref[...].astype(jnp.float32).reshape(n, 3, own, 128)
    left = jnp.broadcast_to(side_ref[0] == 0, other.shape)
    w = jnp.concatenate([jnp.where(left, mine, other), jnp.where(left, other, mine)], axis=3)
    w = jnp.transpose(w, (1, 0, 2, 3)).reshape(3 * C, 256)
    weight = jnp.transpose(w.astype(jnp.bfloat16))[: -(-9 * own // 16) * 16]
    lane = lax.broadcasted_iota(jnp.int32, (1, LANES), 1)
    count = jnp.zeros((1, LANES), jnp.int32)
    for s in range(PROMPT_SAMPLES):
        count = jnp.where(lane // HW == s, count_ref[s], count)
    for f in range(frames):
        least = max(f - 2, 0)
        z = jnp.dot(
            weight[:, (2 - (f - least)) * C :],
            x_ref[least * C : (f + 1) * C, :],
            preferred_element_type=jnp.float32,
        )
        total = stream_ref[f]
        for k in range(3):
            part = None
            for j in range(3):
                tap = z[(3 * j + k) * own : (3 * j + k + 1) * own]
                if j != 1:
                    tap = jnp.where(shift_mask(j, 1), shifted(tap, LATENT_COLUMNS * (j - 1)), 0.0)
                part = tap if part is None else part + tap
            if k != 1:
                part = jnp.where(shift_mask(1, k), shifted(part, k - 1), 0.0)
            total = total + part
        out_ref[f] = jnp.where(count > f, total, 0.0)
        b, g = divmod(f, BLOCK_FRAMES)
        if g == BLOCK_FRAMES - 1:
            parts = [out_ref[b * BLOCK_FRAMES + t] for t in range(BLOCK_FRAMES)]
            for s in range(0, PROMPT_SAMPLES, 2):
                both = [
                    jnp.concatenate([p[:, t * HW : (t + 1) * HW] for p in parts], axis=1) for t in (s, s + 1)
                ]
                at = (b * PROMPT_SAMPLES + s) * own
                o_ref[at : at + 2 * own, :] = jnp.concatenate(both, axis=0).astype(jnp.bfloat16)


def transpose_kernel(x_ref, o_ref):
    o_ref[...] = jnp.transpose(x_ref[...])


def call(body, out, ins, outs, scratch=(), flops=0, moved=0, limit=8):
    return pl.pallas_call(
        body,
        out_shape=out,
        in_specs=ins,
        out_specs=outs,
        scratch_shapes=list(scratch),
        compiler_params=pltpu.CompilerParams(vmem_limit_bytes=limit * 1024 * 1024),
        cost_estimate=pl.CostEstimate(flops=flops, bytes_accessed=moved, transcendentals=0),
    )


def by_channel(n, latents, counts, entry_kernel, entry_bias, gain, kernel, bias):
    own = C // n
    frames = n // PROMPT_SAMPLES * BLOCK_FRAMES
    first = (lax.axis_index("tm") * own).astype(jnp.int32).reshape(1)
    shape = jax.ShapeDtypeStruct
    bf16, f32 = jnp.bfloat16, jnp.float32
    side = lax.axis_index("groups").astype(jnp.int32).reshape(1)
    each = latents.shape[1] // HW * (n // PROMPT_SAMPLES)
    odd = (lax.axis_index("tm") % 2).astype(jnp.int32).reshape(1)
    height = 3 * own + each * LANES // 256
    parcels = call(
        functools.partial(parcels_kernel, n), shape((n * height, 128), bf16), [VMEM, VMEM, SMEM], VMEM
    )(latents, kernel, side)
    got = lax.all_to_all(parcels, "tm", split_axis=0, concat_axis=0, tiled=True)
    params = call(
        functools.partial(params_kernel, n),
        shape((2 * own + C, 640), bf16),
        [VMEM, VMEM, SMEM],
        VMEM,
        [pltpu.VMEM((2 * C, 640), f32)],
        flops=500_000_000,
        moved=2_000_000,
    )(
        entry_kernel.reshape(27 * LATENT_CHANNELS, C),
        jnp.concatenate([entry_bias, gain, bias]).reshape(-1, 128),
        first,
    )
    split = got.reshape(n, height, 128)
    other, params = lax.optimization_barrier((split[:, : 3 * own].reshape(n * 3 * own, 128), params))
    other = lax.ppermute(other, "groups", [(0, 1), (1, 0)])
    lats = split[:, 3 * own :].reshape(-1, 128)
    lats = lax.ppermute(lats, "tm", [(i, i ^ 1) for i in range(n)])
    active, stream = call(
        functools.partial(active_kernel, n),
        (shape((frames * C, LANES), bf16), shape((frames, own, LANES), f32)),
        [VMEM, VMEM, VMEM, SMEM],
        (VMEM, VMEM),
        [pltpu.VMEM((frames * 9 * LATENT_CHANNELS, LANES), bf16)],
        flops=2 * frames * LANES * 432 * C,
        moved=20_000_000,
        limit=24,
    )(got, lats, params, odd)
    out = call(
        functools.partial(branch_kernel, n),
        shape((n * own, BLOCK_FRAMES * HW), bf16),
        [VMEM, VMEM, VMEM, VMEM, SMEM, SMEM],
        VMEM,
        [pltpu.VMEM((frames, own, LANES), f32)],
        flops=2 * frames * LANES * 27 * C * own,
        moved=20_000_000,
        limit=24,
    )(got, other, active, stream, side, counts)
    out = lax.all_to_all(out, "tm", split_axis=0, concat_axis=0, tiled=True)
    out = call(transpose_kernel, shape((BLOCK_FRAMES * HW, C), bf16), [VMEM], VMEM)(out)
    return out.reshape(BLOCK_FRAMES, LATENT_ROWS, LATENT_COLUMNS, C)


def from_behind(block, axis, distance):
    devices = range(lax.axis_size(axis))
    route = [(i - distance, i) for i in devices if i - distance in devices]
    return lax.ppermute(block, axis, route)


def causal_conv(frames, weight):
    frames_out = frames.shape[0] - 2
    inputs = frames.shape[3]
    padded = jnp.pad(frames, ((0, 0), (1, 1), (1, 1), (0, 0)))
    total = jnp.zeros((frames_out * LATENT_ROWS * LATENT_COLUMNS, weight.shape[2]), jnp.float32)
    for time_tap in range(3):
        for row_tap in range(3):
            for col_tap in range(3):
                window = padded[
                    time_tap : time_tap + frames_out,
                    row_tap : row_tap + LATENT_ROWS,
                    col_tap : col_tap + LATENT_COLUMNS,
                    :,
                ]
                window = window.reshape(frames_out * LATENT_ROWS * LATENT_COLUMNS, inputs)
                tap = 9 * time_tap + 3 * row_tap + col_tap
                total = total + jnp.dot(window, weight[tap], preferred_element_type=jnp.float32)
    return total


def activate(stream, norm_scale_gain):
    values = stream.astype(jnp.float32)
    scale = lax.rsqrt(jnp.mean(values * values, axis=-1, keepdims=True) + 1e-06)
    return jax.nn.silu(values * scale * norm_scale_gain).astype(jnp.bfloat16)


def to_cells(planes):
    return jnp.transpose(
        planes.reshape(planes.shape[0], LATENT_CHANNELS, LATENT_ROWS, LATENT_COLUMNS), (0, 2, 3, 1)
    )


def by_block(
    sharded_latents,
    sample_frame_count,
    entry_kernel,
    entry_bias,
    norm_scale_gain,
    residual_kernel,
    residual_bias,
):
    gathered_latents = lax.all_to_all(
        sharded_latents, "tm", split_axis=0, concat_axis=1, tiled=True
    )
    latent_volume = gathered_latents.reshape(
        BLOCK_FRAMES, LATENT_CHANNELS, LATENT_ROWS * LATENT_COLUMNS
    )
    position = lax.axis_index("tm")
    block = position // PROMPT_SAMPLES
    sample = position % PROMPT_SAMPLES
    keep = block > 0
    earlier = from_behind(latent_volume, "tm", PROMPT_SAMPLES)
    earlier = jnp.where(keep, earlier, jnp.zeros_like(earlier))
    frames = to_cells(jnp.concatenate([earlier, latent_volume], axis=0))
    widened = (causal_conv(frames, entry_kernel) + entry_bias).astype(jnp.bfloat16)
    active_all = activate(widened, norm_scale_gain).reshape(
        BLOCK_FRAMES + 2, LATENT_ROWS, LATENT_COLUMNS, C
    )
    behind = jnp.where(keep, active_all[:2], jnp.zeros_like(active_all[:2]))
    extended = jnp.concatenate([behind, active_all[2:]], axis=0)
    stream = widened[2 * LATENT_ROWS * LATENT_COLUMNS :]
    kernel_all = lax.all_gather(residual_kernel, "tm", axis=1, tiled=True)
    branch = causal_conv(extended, kernel_all)
    total = (stream.astype(jnp.float32) + (branch + residual_bias)).reshape(
        BLOCK_FRAMES, LATENT_ROWS, LATENT_COLUMNS, C
    )
    limit = jnp.sum(jnp.where(jnp.arange(PROMPT_SAMPLES) == sample, sample_frame_count, 0))
    frame_index = block * BLOCK_FRAMES + jnp.arange(BLOCK_FRAMES)
    valid = (frame_index < limit)[:, None, None, None]
    return jnp.where(valid, total, jnp.zeros_like(total)).astype(jnp.bfloat16)


def solution(mesh):
    n = mesh.shape["tm"]
    cells = BLOCK_FRAMES * LATENT_CHANNELS * HW
    fits = mesh.shape["groups"] == 2 and 9 * (C // n) <= 256 and n % 2 == 0 and LANES % 256 == 0
    whole_rows = fits and cells % (n * HW) == 0 and C % n == 0 and (C // n) % 8 == 0 and n % PROMPT_SAMPLES == 0
    body = functools.partial(by_channel, n) if whole_rows else by_block
    in_specs = (P("groups", "tm"), P("groups"), P(), P(), P(), P(None, "tm", None), P())
    out_specs = P(("groups", "tm"), None, None, None)
    return jax.shard_map(body, mesh=mesh, in_specs=in_specs, out_specs=out_specs, check_vma=False)
```

```python
import functools

import jax
import jax.numpy as jnp
from jax import lax
from jax.experimental import pallas as pl
from jax.experimental.pallas import tpu as pltpu
from jax.sharding import PartitionSpec as P

LATENT_CHANNELS = 16
C = 384
PROMPT_SAMPLES = 8
BLOCK_FRAMES = 4
LATENT_ROWS = 6
LATENT_COLUMNS = 16
HW = LATENT_ROWS * LATENT_COLUMNS
LANES = PROMPT_SAMPLES * HW
VMEM = pl.BlockSpec(memory_space=pltpu.VMEM)
SMEM = pl.BlockSpec(memory_space=pltpu.SMEM)


def shift_mask(j, k):
    lane = lax.broadcasted_iota(jnp.int32, (1, LANES), 1)
    row = (lane % HW) // LATENT_COLUMNS
    col = lane % LATENT_COLUMNS
    ok = lane >= 0
    if j == 0:
        ok = row > 0
    elif j == 2:
        ok = row < LATENT_ROWS - 1
    if k == 0:
        ok = ok & (col > 0)
    elif k == 2:
        ok = ok & (col < LATENT_COLUMNS - 1)
    return ok


def shifted(x, delta):
    return x if delta == 0 else pltpu.roll(x, (-delta) % x.shape[1], 1)


def packing(own):
    runs = 3 * (own // 8)
    places = {}
    for run in range(runs):
        for t in range(9):
            if run < runs // 2 * 2:
                place = (run // (runs // 2), (run % (runs // 2) * 9 + t) * own)
            else:
                place = (0 if t < 5 else 1, (runs // 2 * 9 + (t if t < 5 else t - 5)) * own)
            places[run // (own // 8), run % (own // 8), t] = place
    longest = max(lane for _, lane in places.values()) + own
    return places, -(-longest // 128) * 128


def parcels_kernel(n, x_ref, w_ref, side_ref, o_ref):
    own = C // n
    x = x_ref[...].astype(jnp.float32)
    rows = []
    for b in range(x.shape[0] // PROMPT_SAMPLES):
        for c in range(x.shape[1] // HW):
            at = b * PROMPT_SAMPLES
            pieces = [x[r : r + 1, c * HW : (c + 1) * HW] for r in range(at, at + PROMPT_SAMPLES)]
            rows.append(jnp.concatenate(pieces, axis=1))
    rows = jnp.concatenate(rows, axis=0)
    tiles = [rows[:, t * 128 : (t + 1) * 128] for t in range(LANES // 128)]
    w = w_ref[...].astype(jnp.float32).reshape(3, 9, own // 8, 8, C)
    places, width = packing(own)
    left = jnp.broadcast_to(side_ref[0] == 0, (8, width))
    half = len(tiles) // 2
    for d in range(0, n, 2):
        both = []
        for e in (d, d + 1):
            halves = []
            for side in range(2):
                pieces = [
                    w[i, t, c, :, e * own : (e + 1) * own]
                    for i in range(3)
                    for c in range(own // 8)
                    for t in range(9)
                    if places[i, c, t][0] == side
                ]
                pieces.append(jnp.zeros((8, width - len(pieces) * own), jnp.float32))
                halves.append(jnp.concatenate(pieces, axis=1))
            share = jnp.where(left, halves[0], halves[1])
            both += [share[:, t * 128 : (t + 1) * 128] for t in range(width // 128)]
            both += tiles[half:] if e % 2 else tiles[:half]
        both = jnp.concatenate(both, axis=0).astype(jnp.bfloat16)
        o_ref[d // 2 * both.shape[0] : (d // 2 + 1) * both.shape[0], :] = both


def column(rows):
    parts = [jnp.transpose(jnp.broadcast_to(rows[t : t + 1], (128, 128))) for t in range(rows.shape[0])]
    return jnp.concatenate(parts, axis=0)


def thirds(x):
    parts = []
    for _ in range(3):
        part = x.astype(jnp.bfloat16).astype(jnp.float32)
        parts.append(part)
        x = x - part
    return parts


def params_kernel(n, entry_ref, vectors_ref, first_ref, o_ref, row_ref):
    own = C // n
    depth = 27 * LATENT_CHANNELS
    tall = C // 128
    first = pl.multiple_of(first_ref[0], 8)
    lane = lax.broadcasted_iota(jnp.int32, (C, 16), 1)

    def spread(t):
        tile = column(vectors_ref[t * tall : (t + 1) * tall])[:, :16]
        out = jnp.zeros((C, 16), jnp.float32)
        for t, part in enumerate(thirds(tile)):
            out = jnp.where(lane == t, part, out)
        return out

    half_gain = column(vectors_ref[tall : 2 * tall]) * 0.5
    gap = jnp.zeros((C, 512 - depth - 16), jnp.float32)
    weight = jnp.transpose(entry_ref[...].astype(jnp.float32))
    full = jnp.concatenate([weight, spread(0), gap, half_gain], axis=1)
    row_ref[0:C, :] = full
    row_ref[C : 2 * C, :] = jnp.concatenate([jnp.zeros_like(weight), spread(2), gap, half_gain], axis=1)
    mine = row_ref[pl.ds(first, own), :]
    after = row_ref[pl.ds(first + C, own), :]
    o_ref[...] = jnp.concatenate([mine, after, full], axis=0).astype(jnp.bfloat16)


def active_kernel(n, got_ref, lat_ref, params_ref, odd_ref, x_ref, stream_ref, col_ref):
    own = C // n
    frames = n // PROMPT_SAMPLES * BLOCK_FRAMES
    each = LATENT_CHANNELS * BLOCK_FRAMES // n
    taps = 9 * LATENT_CHANNELS
    weight = params_ref[:, : 3 * taps + 16]
    half_gain = jnp.concatenate([params_ref[2 * own :, 512:]] * (LANES // 128), axis=1)
    ones = (lax.broadcasted_iota(jnp.int32, (16, LANES), 0) < 3).astype(jnp.float32).astype(jnp.bfloat16)
    per_frame = LATENT_CHANNELS // each
    blocks = n // PROMPT_SAMPLES
    mine = got_ref[...].astype(jnp.float32).reshape(n, -1, 128)[:, packing(own)[1] // 16 :]
    other = lat_ref[...].astype(jnp.float32).reshape(mine.shape)
    even = jnp.broadcast_to(odd_ref[0] == 0, mine.shape)
    lats = jnp.concatenate([jnp.where(even, mine, other), jnp.where(even, other, mine)], axis=1)
    lats = lats.reshape(n, LANES // 128, blocks * each, 128)
    lats = jnp.concatenate([lats[:, t] for t in range(LANES // 128)], axis=2)
    lats = lats.reshape(BLOCK_FRAMES, per_frame, blocks, each, LANES)
    for f in range(frames):
        b, g = divmod(f, BLOCK_FRAMES)
        lat = lats[g, :, b].reshape(LATENT_CHANNELS, LANES)
        for j in range(3):
            for k in range(3):
                moved = shifted(lat, LATENT_COLUMNS * (j - 1) + k - 1)
                moved = jnp.where(shift_mask(j, k), moved, 0.0)
                at = f * taps + (3 * j + k) * LATENT_CHANNELS
                col_ref[at : at + LATENT_CHANNELS, :] = moved.astype(jnp.bfloat16)
        least = max(f - 2, 0)
        z = jnp.dot(
            weight[:, (2 - (f - least)) * taps :],
            jnp.concatenate([col_ref[least * taps : (f + 1) * taps, :], ones], axis=0),
            preferred_element_type=jnp.float32,
        )
        stream_ref[f] = z[:own].astype(jnp.bfloat16).astype(jnp.float32) + z[own : 2 * own]
        s = z[2 * own :]
        scale = lax.rsqrt(jnp.sum(s * s, axis=0, keepdims=True) * (1.0 / C) + 1e-06)
        half = s.astype(jnp.bfloat16) * half_gain * scale.astype(jnp.bfloat16)
        x_ref[f * C : (f + 1) * C, :] = half + half * jnp.tanh(half)


def branch_kernel(n, got_ref, w_ref, x_ref, stream_ref, side_ref, count_ref, o_ref, out_ref):
    own = C // n
    frames = n // PROMPT_SAMPLES * BLOCK_FRAMES
    places, width = packing(own)

    def lanes(x):
        x = x.reshape(n, width // 128, 8, 128)
        return jnp.concatenate([x[:, t] for t in range(width // 128)], axis=2).reshape(n * 8, width)

    mine = lanes(got_ref[...].astype(jnp.float32).reshape(n, -1, 128)[:, : width // 16])
    other = lanes(w_ref[...].astype(jnp.float32))
    left = jnp.broadcast_to(side_ref[0] == 0, other.shape)
    halves = (jnp.where(left, mine, other), jnp.where(left, other, mine))
    pad = jnp.zeros((n * 8, 256 - 9 * own), jnp.float32)
    depths = []
    for i in range(3):
        runs = []
        for c in range(own // 8):
            side, lane = places[i, c, 0]
            if places[i, c, 8][0] == side:
                parts = [halves[side][:, lane : lane + 9 * own]]
            else:
                end = places[i, c, 5][1]
                parts = [halves[0][:, lane : lane + 5 * own], halves[1][:, end : end + 4 * own]]
            runs.append(jnp.concatenate(parts + [pad], axis=1).reshape(n, 1, 8, 256))
        depths.append(jnp.concatenate(runs, axis=1).reshape(C, 256))
    w = jnp.concatenate(depths, axis=0)
    weight = jnp.transpose(w.astype(jnp.bfloat16))[: -(-9 * own // 16) * 16]
    lane = lax.broadcasted_iota(jnp.int32, (1, LANES), 1)
    count = jnp.zeros((1, LANES), jnp.int32)
    for s in range(PROMPT_SAMPLES):
        count = jnp.where(lane // HW == s, count_ref[s], count)
    for f in range(frames):
        least = max(f - 2, 0)
        z = jnp.dot(
            weight[:, (2 - (f - least)) * C :],
            x_ref[least * C : (f + 1) * C, :],
            preferred_element_type=jnp.float32,
        )
        total = stream_ref[f]
        for k in range(3):
            part = None
            for j in range(3):
                tap = z[(3 * j + k) * own : (3 * j + k + 1) * own]
                if j != 1:
                    tap = jnp.where(shift_mask(j, 1), shifted(tap, LATENT_COLUMNS * (j - 1)), 0.0)
                part = tap if part is None else part + tap
            if k != 1:
                part = jnp.where(shift_mask(1, k), shifted(part, k - 1), 0.0)
            total = total + part
        out_ref[f] = jnp.where(count > f, total, 0.0)
        b, g = divmod(f, BLOCK_FRAMES)
        if g == BLOCK_FRAMES - 1:
            parts = [out_ref[b * BLOCK_FRAMES + t] for t in range(BLOCK_FRAMES)]
            for s in range(0, PROMPT_SAMPLES, 2):
                both = [
                    jnp.concatenate([p[:, t * HW : (t + 1) * HW] for p in parts], axis=1) for t in (s, s + 1)
                ]
                at = (b * PROMPT_SAMPLES + s) * own
                o_ref[at : at + 2 * own, :] = jnp.concatenate(both, axis=0).astype(jnp.bfloat16)


def transpose_kernel(x_ref, o_ref):
    o_ref[...] = jnp.transpose(x_ref[...])


def call(body, out, ins, outs, scratch=(), flops=0, moved=0, limit=8):
    return pl.pallas_call(
        body,
        out_shape=out,
        in_specs=ins,
        out_specs=outs,
        scratch_shapes=list(scratch),
        compiler_params=pltpu.CompilerParams(vmem_limit_bytes=limit * 1024 * 1024),
        cost_estimate=pl.CostEstimate(flops=flops, bytes_accessed=moved, transcendentals=0),
    )


def by_channel(n, latents, counts, entry_kernel, entry_bias, gain, kernel, bias):
    own = C // n
    frames = n // PROMPT_SAMPLES * BLOCK_FRAMES
    first = (lax.axis_index("tm") * own).astype(jnp.int32).reshape(1)
    shape = jax.ShapeDtypeStruct
    bf16, f32 = jnp.bfloat16, jnp.float32
    side = lax.axis_index("groups").astype(jnp.int32).reshape(1)
    each = latents.shape[1] // HW * (n // PROMPT_SAMPLES)
    odd = (lax.axis_index("tm") % 2).astype(jnp.int32).reshape(1)
    height = packing(own)[1] // 16
    extra = each * LANES // 256
    parcels = call(
        functools.partial(parcels_kernel, n), shape((n * (height + extra), 128), bf16), [VMEM, VMEM, SMEM], VMEM, limit=58
    )(latents, kernel, side)
    got = lax.all_to_all(parcels, "tm", split_axis=0, concat_axis=0, tiled=True)
    params = call(
        functools.partial(params_kernel, n),
        shape((2 * own + C, 640), bf16),
        [VMEM, VMEM, SMEM],
        VMEM,
        [pltpu.VMEM((2 * C, 640), f32)],
        flops=500_000_000,
        moved=2_000_000,
    )(
        entry_kernel.reshape(27 * LATENT_CHANNELS, C),
        jnp.concatenate([entry_bias, gain, bias]).reshape(-1, 128),
        first,
    )
    split = got.reshape(n, height + extra, 128)
    other, params = lax.optimization_barrier((split[:, :height].reshape(n * height, 128), params))
    other = lax.ppermute(other, "groups", [(0, 1), (1, 0)])
    lats = split[:, height:].reshape(-1, 128)
    lats = lax.ppermute(lats, "tm", [(i, i ^ 1) for i in range(n)])
    active, stream = call(
        functools.partial(active_kernel, n),
        (shape((frames * C, LANES), bf16), shape((frames, own, LANES), f32)),
        [VMEM, VMEM, VMEM, SMEM],
        (VMEM, VMEM),
        [pltpu.VMEM((frames * 9 * LATENT_CHANNELS, LANES), bf16)],
        flops=2 * frames * LANES * 432 * C,
        moved=20_000_000,
        limit=24,
    )(got, lats, params, odd)
    out = call(
        functools.partial(branch_kernel, n),
        shape((n * own, BLOCK_FRAMES * HW), bf16),
        [VMEM, VMEM, VMEM, VMEM, SMEM, SMEM],
        VMEM,
        [pltpu.VMEM((frames, own, LANES), f32)],
        flops=2 * frames * LANES * 27 * C * own,
        moved=20_000_000,
        limit=24,
    )(got, other, active, stream, side, counts)
    out = lax.all_to_all(out, "tm", split_axis=0, concat_axis=0, tiled=True)
    out = call(transpose_kernel, shape((BLOCK_FRAMES * HW, C), bf16), [VMEM], VMEM)(out)
    return out.reshape(BLOCK_FRAMES, LATENT_ROWS, LATENT_COLUMNS, C)


def from_behind(block, axis, distance):
    devices = range(lax.axis_size(axis))
    route = [(i - distance, i) for i in devices if i - distance in devices]
    return lax.ppermute(block, axis, route)


def causal_conv(frames, weight):
    frames_out = frames.shape[0] - 2
    inputs = frames.shape[3]
    padded = jnp.pad(frames, ((0, 0), (1, 1), (1, 1), (0, 0)))
    total = jnp.zeros((frames_out * LATENT_ROWS * LATENT_COLUMNS, weight.shape[2]), jnp.float32)
    for time_tap in range(3):
        for row_tap in range(3):
            for col_tap in range(3):
                window = padded[
                    time_tap : time_tap + frames_out,
                    row_tap : row_tap + LATENT_ROWS,
                    col_tap : col_tap + LATENT_COLUMNS,
                    :,
                ]
                window = window.reshape(frames_out * LATENT_ROWS * LATENT_COLUMNS, inputs)
                tap = 9 * time_tap + 3 * row_tap + col_tap
                total = total + jnp.dot(window, weight[tap], preferred_element_type=jnp.float32)
    return total


def activate(stream, norm_scale_gain):
    values = stream.astype(jnp.float32)
    scale = lax.rsqrt(jnp.mean(values * values, axis=-1, keepdims=True) + 1e-06)
    return jax.nn.silu(values * scale * norm_scale_gain).astype(jnp.bfloat16)


def to_cells(planes):
    return jnp.transpose(
        planes.reshape(planes.shape[0], LATENT_CHANNELS, LATENT_ROWS, LATENT_COLUMNS), (0, 2, 3, 1)
    )


def by_block(
    sharded_latents,
    sample_frame_count,
    entry_kernel,
    entry_bias,
    norm_scale_gain,
    residual_kernel,
    residual_bias,
):
    gathered_latents = lax.all_to_all(
        sharded_latents, "tm", split_axis=0, concat_axis=1, tiled=True
    )
    latent_volume = gathered_latents.reshape(
        BLOCK_FRAMES, LATENT_CHANNELS, LATENT_ROWS * LATENT_COLUMNS
    )
    position = lax.axis_index("tm")
    block = position // PROMPT_SAMPLES
    sample = position % PROMPT_SAMPLES
    keep = block > 0
    earlier = from_behind(latent_volume, "tm", PROMPT_SAMPLES)
    earlier = jnp.where(keep, earlier, jnp.zeros_like(earlier))
    frames = to_cells(jnp.concatenate([earlier, latent_volume], axis=0))
    widened = (causal_conv(frames, entry_kernel) + entry_bias).astype(jnp.bfloat16)
    active_all = activate(widened, norm_scale_gain).reshape(
        BLOCK_FRAMES + 2, LATENT_ROWS, LATENT_COLUMNS, C
    )
    behind = jnp.where(keep, active_all[:2], jnp.zeros_like(active_all[:2]))
    extended = jnp.concatenate([behind, active_all[2:]], axis=0)
    stream = widened[2 * LATENT_ROWS * LATENT_COLUMNS :]
    kernel_all = lax.all_gather(residual_kernel, "tm", axis=1, tiled=True)
    branch = causal_conv(extended, kernel_all)
    total = (stream.astype(jnp.float32) + (branch + residual_bias)).reshape(
        BLOCK_FRAMES, LATENT_ROWS, LATENT_COLUMNS, C
    )
    limit = jnp.sum(jnp.where(jnp.arange(PROMPT_SAMPLES) == sample, sample_frame_count, 0))
    frame_index = block * BLOCK_FRAMES + jnp.arange(BLOCK_FRAMES)
    valid = (frame_index < limit)[:, None, None, None]
    return jnp.where(valid, total, jnp.zeros_like(total)).astype(jnp.bfloat16)


def solution(mesh):
    n = mesh.shape["tm"]
    cells = BLOCK_FRAMES * LATENT_CHANNELS * HW
    fits = mesh.shape["groups"] == 2 and 9 * (C // n) <= 256 and n % 2 == 0 and LANES % 256 == 0
    whole_rows = fits and cells % (n * HW) == 0 and C % n == 0 and (C // n) % 8 == 0 and n % PROMPT_SAMPLES == 0
    body = functools.partial(by_channel, n) if whole_rows else by_block
    in_specs = (P("groups", "tm"), P("groups"), P(), P(), P(), P(None, "tm", None), P())
    out_specs = P(("groups", "tm"), None, None, None)
    return jax.shard_map(body, mesh=mesh, in_specs=in_specs, out_specs=out_specs, check_vma=False)
```

```python
import functools

import jax
import jax.numpy as jnp
from jax import lax
from jax.experimental import pallas as pl
from jax.experimental.pallas import tpu as pltpu
from jax.sharding import PartitionSpec as P

LATENT_CHANNELS = 16
C = 384
PROMPT_SAMPLES = 8
BLOCK_FRAMES = 4
LATENT_ROWS = 6
LATENT_COLUMNS = 16
HW = LATENT_ROWS * LATENT_COLUMNS
LANES = PROMPT_SAMPLES * HW
VMEM = pl.BlockSpec(memory_space=pltpu.VMEM)
SMEM = pl.BlockSpec(memory_space=pltpu.SMEM)
ANY = pl.BlockSpec(memory_space=pl.ANY)


def shift_mask(j, k):
    lane = lax.broadcasted_iota(jnp.int32, (1, LANES), 1)
    row = (lane % HW) // LATENT_COLUMNS
    col = lane % LATENT_COLUMNS
    ok = lane >= 0
    if j == 0:
        ok = row > 0
    elif j == 2:
        ok = row < LATENT_ROWS - 1
    if k == 0:
        ok = ok & (col > 0)
    elif k == 2:
        ok = ok & (col < LATENT_COLUMNS - 1)
    return ok


def shifted(x, delta):
    return x if delta == 0 else pltpu.roll(x, (-delta) % x.shape[1], 1)


def packing(own):
    runs = 3 * (own // 8)
    places = {}
    for run in range(runs):
        for t in range(9):
            if run < runs // 2 * 2:
                place = (run // (runs // 2), (run % (runs // 2) * 9 + t) * own)
            else:
                place = (0 if t < 5 else 1, (runs // 2 * 9 + (t if t < 5 else t - 5)) * own)
            places[run // (own // 8), run % (own // 8), t] = place
    longest = max(lane for _, lane in places.values()) + own
    return places, -(-longest // 128) * 128


def parcels_kernel(n, x_hbm, w_hbm, side_ref, o_hbm, x_ref, w_ref, o_ref, in_sem, out_sem):
    own = C // n
    get_x = pltpu.make_async_copy(x_hbm, x_ref, in_sem.at[0])
    get_w = pltpu.make_async_copy(w_hbm, w_ref, in_sem.at[1])
    get_x.start()
    get_w.start()
    get_x.wait()
    x = x_ref[...].astype(jnp.float32)
    rows = []
    for b in range(x.shape[0] // PROMPT_SAMPLES):
        for c in range(x.shape[1] // HW):
            at = b * PROMPT_SAMPLES
            pieces = [x[r : r + 1, c * HW : (c + 1) * HW] for r in range(at, at + PROMPT_SAMPLES)]
            rows.append(jnp.concatenate(pieces, axis=1))
    rows = jnp.concatenate(rows, axis=0)
    tiles = [rows[:, t * 128 : (t + 1) * 128] for t in range(LANES // 128)]
    get_w.wait()
    w = w_ref[...].astype(jnp.float32).reshape(3, 9, own // 8, 8, C)
    puts = []
    places, width = packing(own)
    left = jnp.broadcast_to(side_ref[0] == 0, (8, width))
    half = len(tiles) // 2
    for d in range(0, n, 2):
        both = []
        for e in (d, d + 1):
            halves = []
            for side in range(2):
                pieces = [
                    w[i, t, c, :, e * own : (e + 1) * own]
                    for i in range(3)
                    for c in range(own // 8)
                    for t in range(9)
                    if places[i, c, t][0] == side
                ]
                pieces.append(jnp.zeros((8, width - len(pieces) * own), jnp.float32))
                halves.append(jnp.concatenate(pieces, axis=1))
            share = jnp.where(left, halves[0], halves[1])
            both += [share[:, t * 128 : (t + 1) * 128] for t in range(width // 128)]
            both += tiles[half:] if e % 2 else tiles[:half]
        both = jnp.concatenate(both, axis=0).astype(jnp.bfloat16)
        o_ref[d // 2 * both.shape[0] : (d // 2 + 1) * both.shape[0], :] = both
        if d % 4 == 2:
            rows = pl.ds((d // 4) * 2 * both.shape[0], 2 * both.shape[0])
            puts.append(pltpu.make_async_copy(o_ref.at[rows], o_hbm.at[rows], out_sem.at[d // 4]))
            puts[-1].start()
    for put in puts:
        put.wait()


def column(rows):
    parts = [jnp.transpose(jnp.broadcast_to(rows[t : t + 1], (128, 128))) for t in range(rows.shape[0])]
    return jnp.concatenate(parts, axis=0)


def thirds(x):
    parts = []
    for _ in range(3):
        part = x.astype(jnp.bfloat16).astype(jnp.float32)
        parts.append(part)
        x = x - part
    return parts


def params_kernel(n, entry_ref, vectors_ref, first_ref, o_ref, row_ref):
    own = C // n
    depth = 27 * LATENT_CHANNELS
    tall = C // 128
    first = pl.multiple_of(first_ref[0], 8)
    lane = lax.broadcasted_iota(jnp.int32, (C, 16), 1)

    def spread(t):
        tile = column(vectors_ref[t * tall : (t + 1) * tall])[:, :16]
        out = jnp.zeros((C, 16), jnp.float32)
        for t, part in enumerate(thirds(tile)):
            out = jnp.where(lane == t, part, out)
        return out

    half_gain = column(vectors_ref[tall : 2 * tall]) * 0.5
    gap = jnp.zeros((C, 512 - depth - 16), jnp.float32)
    weight = jnp.transpose(entry_ref[...].astype(jnp.float32))
    full = jnp.concatenate([weight, spread(0), gap, half_gain], axis=1)
    row_ref[0:C, :] = full
    row_ref[C : 2 * C, :] = jnp.concatenate([jnp.zeros_like(weight), spread(2), gap, half_gain], axis=1)
    mine = row_ref[pl.ds(first, own), :]
    after = row_ref[pl.ds(first + C, own), :]
    o_ref[...] = jnp.concatenate([mine, after, full], axis=0).astype(jnp.bfloat16)


def active_kernel(n, got_ref, lat_ref, params_ref, odd_ref, x_ref, stream_ref, col_ref):
    own = C // n
    frames = n // PROMPT_SAMPLES * BLOCK_FRAMES
    each = LATENT_CHANNELS * BLOCK_FRAMES // n
    taps = 9 * LATENT_CHANNELS
    weight = params_ref[:, : 3 * taps + 16]
    half_gain = jnp.concatenate([params_ref[2 * own :, 512:]] * (LANES // 128), axis=1)
    ones = (lax.broadcasted_iota(jnp.int32, (16, LANES), 0) < 3).astype(jnp.float32).astype(jnp.bfloat16)
    per_frame = LATENT_CHANNELS // each
    blocks = n // PROMPT_SAMPLES
    mine = got_ref[...].astype(jnp.float32).reshape(n, -1, 128)[:, packing(own)[1] // 16 :]
    other = lat_ref[...].astype(jnp.float32).reshape(mine.shape)
    even = jnp.broadcast_to(odd_ref[0] == 0, mine.shape)
    lats = jnp.concatenate([jnp.where(even, mine, other), jnp.where(even, other, mine)], axis=1)
    lats = lats.reshape(n, LANES // 128, blocks * each, 128)
    lats = jnp.concatenate([lats[:, t] for t in range(LANES // 128)], axis=2)
    lats = lats.reshape(BLOCK_FRAMES, per_frame, blocks, each, LANES)
    for f in range(frames):
        b, g = divmod(f, BLOCK_FRAMES)
        lat = lats[g, :, b].reshape(LATENT_CHANNELS, LANES)
        for j in range(3):
            for k in range(3):
                moved = shifted(lat, LATENT_COLUMNS * (j - 1) + k - 1)
                moved = jnp.where(shift_mask(j, k), moved, 0.0)
                at = f * taps + (3 * j + k) * LATENT_CHANNELS
                col_ref[at : at + LATENT_CHANNELS, :] = moved.astype(jnp.bfloat16)
        least = max(f - 2, 0)
        z = jnp.dot(
            weight[:, (2 - (f - least)) * taps :],
            jnp.concatenate([col_ref[least * taps : (f + 1) * taps, :], ones], axis=0),
            preferred_element_type=jnp.float32,
        )
        stream_ref[f] = z[:own].astype(jnp.bfloat16).astype(jnp.float32) + z[own : 2 * own]
        s = z[2 * own :]
        scale = lax.rsqrt(jnp.sum(s * s, axis=0, keepdims=True) * (1.0 / C) + 1e-06)
        half = s.astype(jnp.bfloat16) * half_gain * scale.astype(jnp.bfloat16)
        x_ref[f * C : (f + 1) * C, :] = half + half * jnp.tanh(half)


def branch_kernel(n, got_ref, w_ref, x_ref, stream_ref, side_ref, count_ref, o_ref, out_ref):
    own = C // n
    frames = n // PROMPT_SAMPLES * BLOCK_FRAMES
    places, width = packing(own)

    def lanes(x):
        x = x.reshape(n, width // 128, 8, 128)
        return jnp.concatenate([x[:, t] for t in range(width // 128)], axis=2).reshape(n * 8, width)

    mine = lanes(got_ref[...].astype(jnp.float32).reshape(n, -1, 128)[:, : width // 16])
    other = lanes(w_ref[...].astype(jnp.float32))
    left = jnp.broadcast_to(side_ref[0] == 0, other.shape)
    halves = (jnp.where(left, mine, other), jnp.where(left, other, mine))
    pad = jnp.zeros((n * 8, 256 - 9 * own), jnp.float32)
    depths = []
    for i in range(3):
        runs = []
        for c in range(own // 8):
            side, lane = places[i, c, 0]
            if places[i, c, 8][0] == side:
                parts = [halves[side][:, lane : lane + 9 * own]]
            else:
                end = places[i, c, 5][1]
                parts = [halves[0][:, lane : lane + 5 * own], halves[1][:, end : end + 4 * own]]
            runs.append(jnp.concatenate(parts + [pad], axis=1).reshape(n, 1, 8, 256))
        depths.append(jnp.concatenate(runs, axis=1).reshape(C, 256))
    w = jnp.concatenate(depths, axis=0)
    weight = jnp.transpose(w.astype(jnp.bfloat16))[: -(-9 * own // 16) * 16]
    lane = lax.broadcasted_iota(jnp.int32, (1, LANES), 1)
    count = jnp.zeros((1, LANES), jnp.int32)
    for s in range(PROMPT_SAMPLES):
        count = jnp.where(lane // HW == s, count_ref[s], count)
    for f in range(frames):
        least = max(f - 2, 0)
        z = jnp.dot(
            weight[:, (2 - (f - least)) * C :],
            x_ref[least * C : (f + 1) * C, :],
            preferred_element_type=jnp.float32,
        )
        total = stream_ref[f]
        for k in range(3):
            part = None
            for j in range(3):
                tap = z[(3 * j + k) * own : (3 * j + k + 1) * own]
                if j != 1:
                    tap = jnp.where(shift_mask(j, 1), shifted(tap, LATENT_COLUMNS * (j - 1)), 0.0)
                part = tap if part is None else part + tap
            if k != 1:
                part = jnp.where(shift_mask(1, k), shifted(part, k - 1), 0.0)
            total = total + part
        out_ref[f] = jnp.where(count > f, total, 0.0)
        b, g = divmod(f, BLOCK_FRAMES)
        if g == BLOCK_FRAMES - 1:
            parts = [out_ref[b * BLOCK_FRAMES + t] for t in range(BLOCK_FRAMES)]
            for s in range(0, PROMPT_SAMPLES, 2):
                both = [
                    jnp.concatenate([p[:, t * HW : (t + 1) * HW] for p in parts], axis=1) for t in (s, s + 1)
                ]
                at = (b * PROMPT_SAMPLES + s) * own
                o_ref[at : at + 2 * own, :] = jnp.concatenate(both, axis=0).astype(jnp.bfloat16)


def transpose_kernel(x_ref, o_ref):
    o_ref[...] = jnp.transpose(x_ref[...])


def call(body, out, ins, outs, scratch=(), flops=0, moved=0, limit=8):
    return pl.pallas_call(
        body,
        out_shape=out,
        in_specs=ins,
        out_specs=outs,
        scratch_shapes=list(scratch),
        compiler_params=pltpu.CompilerParams(vmem_limit_bytes=limit * 1024 * 1024),
        cost_estimate=pl.CostEstimate(flops=flops, bytes_accessed=moved, transcendentals=0),
    )


def by_channel(n, latents, counts, entry_kernel, entry_bias, gain, kernel, bias):
    own = C // n
    frames = n // PROMPT_SAMPLES * BLOCK_FRAMES
    first = (lax.axis_index("tm") * own).astype(jnp.int32).reshape(1)
    shape = jax.ShapeDtypeStruct
    bf16, f32 = jnp.bfloat16, jnp.float32
    side = lax.axis_index("groups").astype(jnp.int32).reshape(1)
    each = latents.shape[1] // HW * (n // PROMPT_SAMPLES)
    odd = (lax.axis_index("tm") % 2).astype(jnp.int32).reshape(1)
    height = packing(own)[1] // 16
    extra = each * LANES // 256
    parcels = call(
        functools.partial(parcels_kernel, n),
        shape((n * (height + extra), 128), bf16),
        [ANY, ANY, SMEM],
        ANY,
        [
            pltpu.VMEM(latents.shape, bf16),
            pltpu.VMEM(kernel.shape, bf16),
            pltpu.VMEM((n * (height + extra), 128), bf16),
            pltpu.SemaphoreType.DMA((2,)),
            pltpu.SemaphoreType.DMA((n // 4,)),
        ],
        limit=58,
    )(latents, kernel, side)
    got = lax.all_to_all(parcels, "tm", split_axis=0, concat_axis=0, tiled=True)
    params = call(
        functools.partial(params_kernel, n),
        shape((2 * own + C, 640), bf16),
        [VMEM, VMEM, SMEM],
        VMEM,
        [pltpu.VMEM((2 * C, 640), f32)],
        flops=500_000_000,
        moved=2_000_000,
    )(
        entry_kernel.reshape(27 * LATENT_CHANNELS, C),
        jnp.concatenate([entry_bias, gain, bias]).reshape(-1, 128),
        first,
    )
    split = got.reshape(n, height + extra, 128)
    other = lax.ppermute(split[:, :height].reshape(n * height, 128), "groups", [(0, 1), (1, 0)])
    lats = split[:, height:].reshape(-1, 128)
    lats = lax.ppermute(lats, "tm", [(i, i ^ 1) for i in range(n)])
    active, stream = call(
        functools.partial(active_kernel, n),
        (shape((frames * C, LANES), bf16), shape((frames, own, LANES), f32)),
        [VMEM, VMEM, VMEM, SMEM],
        (VMEM, VMEM),
        [pltpu.VMEM((frames * 9 * LATENT_CHANNELS, LANES), bf16)],
        flops=2 * frames * LANES * 432 * C,
        moved=20_000_000,
        limit=24,
    )(got, lats, params, odd)
    out = call(
        functools.partial(branch_kernel, n),
        shape((n * own, BLOCK_FRAMES * HW), bf16),
        [VMEM, VMEM, VMEM, VMEM, SMEM, SMEM],
        VMEM,
        [pltpu.VMEM((frames, own, LANES), f32)],
        flops=2 * frames * LANES * 27 * C * own,
        moved=20_000_000,
        limit=24,
    )(got, other, active, stream, side, counts)
    out = lax.all_to_all(out, "tm", split_axis=0, concat_axis=0, tiled=True)
    out = call(transpose_kernel, shape((BLOCK_FRAMES * HW, C), bf16), [VMEM], VMEM)(out)
    return out.reshape(BLOCK_FRAMES, LATENT_ROWS, LATENT_COLUMNS, C)


def from_behind(block, axis, distance):
    devices = range(lax.axis_size(axis))
    route = [(i - distance, i) for i in devices if i - distance in devices]
    return lax.ppermute(block, axis, route)


def causal_conv(frames, weight):
    frames_out = frames.shape[0] - 2
    inputs = frames.shape[3]
    padded = jnp.pad(frames, ((0, 0), (1, 1), (1, 1), (0, 0)))
    total = jnp.zeros((frames_out * LATENT_ROWS * LATENT_COLUMNS, weight.shape[2]), jnp.float32)
    for time_tap in range(3):
        for row_tap in range(3):
            for col_tap in range(3):
                window = padded[
                    time_tap : time_tap + frames_out,
                    row_tap : row_tap + LATENT_ROWS,
                    col_tap : col_tap + LATENT_COLUMNS,
                    :,
                ]
                window = window.reshape(frames_out * LATENT_ROWS * LATENT_COLUMNS, inputs)
                tap = 9 * time_tap + 3 * row_tap + col_tap
                total = total + jnp.dot(window, weight[tap], preferred_element_type=jnp.float32)
    return total


def activate(stream, norm_scale_gain):
    values = stream.astype(jnp.float32)
    scale = lax.rsqrt(jnp.mean(values * values, axis=-1, keepdims=True) + 1e-06)
    return jax.nn.silu(values * scale * norm_scale_gain).astype(jnp.bfloat16)


def to_cells(planes):
    return jnp.transpose(
        planes.reshape(planes.shape[0], LATENT_CHANNELS, LATENT_ROWS, LATENT_COLUMNS), (0, 2, 3, 1)
    )


def by_block(
    sharded_latents,
    sample_frame_count,
    entry_kernel,
    entry_bias,
    norm_scale_gain,
    residual_kernel,
    residual_bias,
):
    gathered_latents = lax.all_to_all(
        sharded_latents, "tm", split_axis=0, concat_axis=1, tiled=True
    )
    latent_volume = gathered_latents.reshape(
        BLOCK_FRAMES, LATENT_CHANNELS, LATENT_ROWS * LATENT_COLUMNS
    )
    position = lax.axis_index("tm")
    block = position // PROMPT_SAMPLES
    sample = position % PROMPT_SAMPLES
    keep = block > 0
    earlier = from_behind(latent_volume, "tm", PROMPT_SAMPLES)
    earlier = jnp.where(keep, earlier, jnp.zeros_like(earlier))
    frames = to_cells(jnp.concatenate([earlier, latent_volume], axis=0))
    widened = (causal_conv(frames, entry_kernel) + entry_bias).astype(jnp.bfloat16)
    active_all = activate(widened, norm_scale_gain).reshape(
        BLOCK_FRAMES + 2, LATENT_ROWS, LATENT_COLUMNS, C
    )
    behind = jnp.where(keep, active_all[:2], jnp.zeros_like(active_all[:2]))
    extended = jnp.concatenate([behind, active_all[2:]], axis=0)
    stream = widened[2 * LATENT_ROWS * LATENT_COLUMNS :]
    kernel_all = lax.all_gather(residual_kernel, "tm", axis=1, tiled=True)
    branch = causal_conv(extended, kernel_all)
    total = (stream.astype(jnp.float32) + (branch + residual_bias)).reshape(
        BLOCK_FRAMES, LATENT_ROWS, LATENT_COLUMNS, C
    )
    limit = jnp.sum(jnp.where(jnp.arange(PROMPT_SAMPLES) == sample, sample_frame_count, 0))
    frame_index = block * BLOCK_FRAMES + jnp.arange(BLOCK_FRAMES)
    valid = (frame_index < limit)[:, None, None, None]
    return jnp.where(valid, total, jnp.zeros_like(total)).astype(jnp.bfloat16)


def solution(mesh):
    n = mesh.shape["tm"]
    cells = BLOCK_FRAMES * LATENT_CHANNELS * HW
    fits = mesh.shape["groups"] == 2 and 9 * (C // n) <= 256 and n % 4 == 0 and LANES % 256 == 0
    whole_rows = fits and cells % (n * HW) == 0 and C % n == 0 and (C // n) % 8 == 0 and n % PROMPT_SAMPLES == 0
    body = functools.partial(by_channel, n) if whole_rows else by_block
    in_specs = (P("groups", "tm"), P("groups"), P(), P(), P(), P(None, "tm", None), P())
    out_specs = P(("groups", "tm"), None, None, None)
    return jax.shard_map(body, mesh=mesh, in_specs=in_specs, out_specs=out_specs, check_vma=False)
```

```python
import functools

import jax
import jax.numpy as jnp
from jax import lax
from jax.experimental import pallas as pl
from jax.experimental.pallas import tpu as pltpu
from jax.sharding import PartitionSpec as P

LATENT_CHANNELS = 16
C = 384
PROMPT_SAMPLES = 8
BLOCK_FRAMES = 4
LATENT_ROWS = 6
LATENT_COLUMNS = 16
HW = LATENT_ROWS * LATENT_COLUMNS
LANES = PROMPT_SAMPLES * HW
VMEM = pl.BlockSpec(memory_space=pltpu.VMEM)
SMEM = pl.BlockSpec(memory_space=pltpu.SMEM)
ANY = pl.BlockSpec(memory_space=pl.ANY)


def shift_mask(j, k):
    lane = lax.broadcasted_iota(jnp.int32, (1, LANES), 1)
    row = (lane % HW) // LATENT_COLUMNS
    col = lane % LATENT_COLUMNS
    ok = lane >= 0
    if j == 0:
        ok = row > 0
    elif j == 2:
        ok = row < LATENT_ROWS - 1
    if k == 0:
        ok = ok & (col > 0)
    elif k == 2:
        ok = ok & (col < LATENT_COLUMNS - 1)
    return ok


def shifted(x, delta):
    return x if delta == 0 else pltpu.roll(x, (-delta) % x.shape[1], 1)


def packing(own):
    runs = 3 * (own // 8)
    places = {}
    for run in range(runs):
        for t in range(9):
            if run < runs // 2 * 2:
                place = (run // (runs // 2), (run % (runs // 2) * 9 + t) * own)
            else:
                place = (0 if t < 5 else 1, (runs // 2 * 9 + (t if t < 5 else t - 5)) * own)
            places[run // (own // 8), run % (own // 8), t] = place
    longest = max(lane for _, lane in places.values()) + own
    return places, -(-longest // 128) * 128


def parcels_kernel(n, x_hbm, w_hbm, side_ref, o_hbm, lat_ref, x_ref, w_ref, o_ref, in_sem, out_sem):
    own = C // n
    get_x = pltpu.make_async_copy(x_hbm, x_ref, in_sem.at[0])
    get_w = pltpu.make_async_copy(w_hbm, w_ref, in_sem.at[1])
    get_x.start()
    get_w.start()
    get_x.wait()
    x = x_ref[...].astype(jnp.float32)
    rows = []
    for b in range(x.shape[0] // PROMPT_SAMPLES):
        for c in range(x.shape[1] // HW):
            at = b * PROMPT_SAMPLES
            pieces = [x[r : r + 1, c * HW : (c + 1) * HW] for r in range(at, at + PROMPT_SAMPLES)]
            rows.append(jnp.concatenate(pieces, axis=1))
    lat_ref[...] = jnp.concatenate(rows, axis=0).astype(jnp.bfloat16)
    get_w.wait()
    w = w_ref[...].astype(jnp.float32).reshape(3, 9, own // 8, 8, C)
    puts = []
    places, width = packing(own)
    left = jnp.broadcast_to(side_ref[0] == 0, (8, width))
    for d in range(0, n, 2):
        both = []
        for e in (d, d + 1):
            halves = []
            for side in range(2):
                pieces = [
                    w[i, t, c, :, e * own : (e + 1) * own]
                    for i in range(3)
                    for c in range(own // 8)
                    for t in range(9)
                    if places[i, c, t][0] == side
                ]
                pieces.append(jnp.zeros((8, width - len(pieces) * own), jnp.float32))
                halves.append(jnp.concatenate(pieces, axis=1))
            share = jnp.where(left, halves[0], halves[1])
            both += [share[:, t * 128 : (t + 1) * 128] for t in range(width // 128)]
        both = jnp.concatenate(both, axis=0).astype(jnp.bfloat16)
        o_ref[d // 2 * both.shape[0] : (d // 2 + 1) * both.shape[0], :] = both
        if d % 4 == 2:
            rows = pl.ds((d // 4) * 2 * both.shape[0], 2 * both.shape[0])
            puts.append(pltpu.make_async_copy(o_ref.at[rows], o_hbm.at[rows], out_sem.at[d // 4]))
            puts[-1].start()
    for put in puts:
        put.wait()


def column(rows):
    parts = [jnp.transpose(jnp.broadcast_to(rows[t : t + 1], (128, 128))) for t in range(rows.shape[0])]
    return jnp.concatenate(parts, axis=0)


def thirds(x):
    parts = []
    for _ in range(3):
        part = x.astype(jnp.bfloat16).astype(jnp.float32)
        parts.append(part)
        x = x - part
    return parts


def params_kernel(n, entry_ref, vectors_ref, first_ref, o_ref, row_ref):
    own = C // n
    depth = 27 * LATENT_CHANNELS
    tall = C // 128
    first = pl.multiple_of(first_ref[0], 8)
    lane = lax.broadcasted_iota(jnp.int32, (C, 16), 1)

    def spread(t):
        tile = column(vectors_ref[t * tall : (t + 1) * tall])[:, :16]
        out = jnp.zeros((C, 16), jnp.float32)
        for t, part in enumerate(thirds(tile)):
            out = jnp.where(lane == t, part, out)
        return out

    half_gain = column(vectors_ref[tall : 2 * tall]) * 0.5
    gap = jnp.zeros((C, 512 - depth - 16), jnp.float32)
    weight = jnp.transpose(entry_ref[...].astype(jnp.float32))
    full = jnp.concatenate([weight, spread(0), gap, half_gain], axis=1)
    row_ref[0:C, :] = full
    row_ref[C : 2 * C, :] = jnp.concatenate([jnp.zeros_like(weight), spread(2), gap, half_gain], axis=1)
    mine = row_ref[pl.ds(first, own), :]
    after = row_ref[pl.ds(first + C, own), :]
    o_ref[...] = jnp.concatenate([mine, after, full], axis=0).astype(jnp.bfloat16)


def active_kernel(n, near_ref, far_ref, params_ref, me_ref, x_ref, stream_ref, col_ref, lat_ref):
    own = C // n
    frames = n // PROMPT_SAMPLES * BLOCK_FRAMES
    each = LATENT_CHANNELS * BLOCK_FRAMES // n
    taps = 9 * LATENT_CHANNELS
    weight = params_ref[:, : 3 * taps + 16]
    half_gain = jnp.concatenate([params_ref[2 * own :, 512:]] * (LANES // 128), axis=1)
    ones = (lax.broadcasted_iota(jnp.int32, (16, LANES), 0) < 3).astype(jnp.float32).astype(jnp.bfloat16)
    per_frame = LATENT_CHANNELS // each
    blocks = n // PROMPT_SAMPLES
    rows = blocks * each
    lat_ref[: n // 2 * rows] = near_ref[...].astype(jnp.float32)
    lat_ref[n // 2 * rows :] = far_ref[...].astype(jnp.float32)
    lats = []
    for p in range(n):
        apart = jnp.bitwise_xor(me_ref[0], p)
        slot, bits = 0, n.bit_length() - 1
        for bit in range(bits):
            slot = slot + ((apart >> bit) & 1) * (1 << (bits - 1 - bit))
        lats.append(lat_ref[pl.ds(pl.multiple_of(slot * rows, 8), rows), :])
    lats = jnp.stack(lats)
    lats = lats.reshape(BLOCK_FRAMES, per_frame, blocks, each, LANES)
    for f in range(frames):
        b, g = divmod(f, BLOCK_FRAMES)
        lat = lats[g, :, b].reshape(LATENT_CHANNELS, LANES)
        for j in range(3):
            for k in range(3):
                moved = shifted(lat, LATENT_COLUMNS * (j - 1) + k - 1)
                moved = jnp.where(shift_mask(j, k), moved, 0.0)
                at = f * taps + (3 * j + k) * LATENT_CHANNELS
                col_ref[at : at + LATENT_CHANNELS, :] = moved.astype(jnp.bfloat16)
        least = max(f - 2, 0)
        z = jnp.dot(
            weight[:, (2 - (f - least)) * taps :],
            jnp.concatenate([col_ref[least * taps : (f + 1) * taps, :], ones], axis=0),
            preferred_element_type=jnp.float32,
        )
        stream_ref[f] = z[:own].astype(jnp.bfloat16).astype(jnp.float32) + z[own : 2 * own]
        s = z[2 * own :]
        scale = lax.rsqrt(jnp.sum(s * s, axis=0, keepdims=True) * (1.0 / C) + 1e-06)
        half = s.astype(jnp.bfloat16) * half_gain * scale.astype(jnp.bfloat16)
        x_ref[f * C : (f + 1) * C, :] = half + half * jnp.tanh(half)


def branch_kernel(n, got_ref, w_ref, x_ref, stream_ref, side_ref, count_ref, o_ref, out_ref):
    own = C // n
    frames = n // PROMPT_SAMPLES * BLOCK_FRAMES
    places, width = packing(own)

    def lanes(x):
        x = x.reshape(n, width // 128, 8, 128)
        return jnp.concatenate([x[:, t] for t in range(width // 128)], axis=2).reshape(n * 8, width)

    mine = lanes(got_ref[...].astype(jnp.float32))
    other = lanes(w_ref[...].astype(jnp.float32))
    left = jnp.broadcast_to(side_ref[0] == 0, other.shape)
    halves = (jnp.where(left, mine, other), jnp.where(left, other, mine))
    pad = jnp.zeros((n * 8, 256 - 9 * own), jnp.float32)
    depths = []
    for i in range(3):
        runs = []
        for c in range(own // 8):
            side, lane = places[i, c, 0]
            if places[i, c, 8][0] == side:
                parts = [halves[side][:, lane : lane + 9 * own]]
            else:
                end = places[i, c, 5][1]
                parts = [halves[0][:, lane : lane + 5 * own], halves[1][:, end : end + 4 * own]]
            runs.append(jnp.concatenate(parts + [pad], axis=1).reshape(n, 1, 8, 256))
        depths.append(jnp.concatenate(runs, axis=1).reshape(C, 256))
    w = jnp.concatenate(depths, axis=0)
    weight = jnp.transpose(w.astype(jnp.bfloat16))[: -(-9 * own // 16) * 16]
    lane = lax.broadcasted_iota(jnp.int32, (1, LANES), 1)
    count = jnp.zeros((1, LANES), jnp.int32)
    for s in range(PROMPT_SAMPLES):
        count = jnp.where(lane // HW == s, count_ref[s], count)
    for f in range(frames):
        least = max(f - 2, 0)
        z = jnp.dot(
            weight[:, (2 - (f - least)) * C :],
            x_ref[least * C : (f + 1) * C, :],
            preferred_element_type=jnp.float32,
        )
        total = stream_ref[f]
        for k in range(3):
            part = None
            for j in range(3):
                tap = z[(3 * j + k) * own : (3 * j + k + 1) * own]
                if j != 1:
                    tap = jnp.where(shift_mask(j, 1), shifted(tap, LATENT_COLUMNS * (j - 1)), 0.0)
                part = tap if part is None else part + tap
            if k != 1:
                part = jnp.where(shift_mask(1, k), shifted(part, k - 1), 0.0)
            total = total + part
        out_ref[f] = jnp.where(count > f, total, 0.0)
        b, g = divmod(f, BLOCK_FRAMES)
        if g == BLOCK_FRAMES - 1:
            parts = [out_ref[b * BLOCK_FRAMES + t] for t in range(BLOCK_FRAMES)]
            for s in range(0, PROMPT_SAMPLES, 2):
                both = [
                    jnp.concatenate([p[:, t * HW : (t + 1) * HW] for p in parts], axis=1) for t in (s, s + 1)
                ]
                at = (b * PROMPT_SAMPLES + s) * own
                o_ref[at : at + 2 * own, :] = jnp.concatenate(both, axis=0).astype(jnp.bfloat16)


def transpose_kernel(x_ref, o_ref):
    o_ref[...] = jnp.transpose(x_ref[...])


def call(body, out, ins, outs, scratch=(), flops=0, moved=0, limit=8):
    return pl.pallas_call(
        body,
        out_shape=out,
        in_specs=ins,
        out_specs=outs,
        scratch_shapes=list(scratch),
        compiler_params=pltpu.CompilerParams(vmem_limit_bytes=limit * 1024 * 1024),
        cost_estimate=pl.CostEstimate(flops=flops, bytes_accessed=moved, transcendentals=0),
    )


def by_channel(n, latents, counts, entry_kernel, entry_bias, gain, kernel, bias):
    own = C // n
    frames = n // PROMPT_SAMPLES * BLOCK_FRAMES
    first = (lax.axis_index("tm") * own).astype(jnp.int32).reshape(1)
    shape = jax.ShapeDtypeStruct
    bf16, f32 = jnp.bfloat16, jnp.float32
    side = lax.axis_index("groups").astype(jnp.int32).reshape(1)
    each = latents.shape[1] // HW * (n // PROMPT_SAMPLES)
    me = lax.axis_index("tm").astype(jnp.int32).reshape(1)
    height = packing(own)[1] // 16
    parcels, lats = call(
        functools.partial(parcels_kernel, n),
        (shape((n * height, 128), bf16), shape((each, LANES), bf16)),
        [ANY, ANY, SMEM],
        (ANY, VMEM),
        [
            pltpu.VMEM(latents.shape, bf16),
            pltpu.VMEM(kernel.shape, bf16),
            pltpu.VMEM((n * height, 128), bf16),
            pltpu.SemaphoreType.DMA((2,)),
            pltpu.SemaphoreType.DMA((n // 4,)),
        ],
        limit=58,
    )(latents, kernel, side)
    got = lax.all_to_all(parcels, "tm", split_axis=0, concat_axis=0, tiled=True)
    params = call(
        functools.partial(params_kernel, n),
        shape((2 * own + C, 640), bf16),
        [VMEM, VMEM, SMEM],
        VMEM,
        [pltpu.VMEM((2 * C, 640), f32)],
        flops=500_000_000,
        moved=2_000_000,
    )(
        entry_kernel.reshape(27 * LATENT_CHANNELS, C),
        jnp.concatenate([entry_bias, gain, bias]).reshape(-1, 128),
        first,
    )
    bit = n // 2
    while True:
        far = lax.ppermute(lats, "tm", [(i, i ^ bit) for i in range(n)])
        if bit == 1:
            break
        lats = jnp.concatenate([lats, far], axis=0)
        bit //= 2
    got, far = lax.optimization_barrier((got, far))
    other = lax.ppermute(got, "groups", [(0, 1), (1, 0)])
    active, stream = call(
        functools.partial(active_kernel, n),
        (shape((frames * C, LANES), bf16), shape((frames, own, LANES), f32)),
        [VMEM, VMEM, VMEM, SMEM],
        (VMEM, VMEM),
        [pltpu.VMEM((frames * 9 * LATENT_CHANNELS, LANES), bf16), pltpu.VMEM((n * each, LANES), f32)],
        flops=2 * frames * LANES * 432 * C,
        moved=20_000_000,
        limit=24,
    )(lats, far, params, me)
    out = call(
        functools.partial(branch_kernel, n),
        shape((n * own, BLOCK_FRAMES * HW), bf16),
        [VMEM, VMEM, VMEM, VMEM, SMEM, SMEM],
        VMEM,
        [pltpu.VMEM((frames, own, LANES), f32)],
        flops=2 * frames * LANES * 27 * C * own,
        moved=20_000_000,
        limit=24,
    )(got, other, active, stream, side, counts)
    out = lax.all_to_all(out, "tm", split_axis=0, concat_axis=0, tiled=True)
    out = call(transpose_kernel, shape((BLOCK_FRAMES * HW, C), bf16), [VMEM], VMEM)(out)
    return out.reshape(BLOCK_FRAMES, LATENT_ROWS, LATENT_COLUMNS, C)


def from_behind(block, axis, distance):
    devices = range(lax.axis_size(axis))
    route = [(i - distance, i) for i in devices if i - distance in devices]
    return lax.ppermute(block, axis, route)


def causal_conv(frames, weight):
    frames_out = frames.shape[0] - 2
    inputs = frames.shape[3]
    padded = jnp.pad(frames, ((0, 0), (1, 1), (1, 1), (0, 0)))
    total = jnp.zeros((frames_out * LATENT_ROWS * LATENT_COLUMNS, weight.shape[2]), jnp.float32)
    for time_tap in range(3):
        for row_tap in range(3):
            for col_tap in range(3):
                window = padded[
                    time_tap : time_tap + frames_out,
                    row_tap : row_tap + LATENT_ROWS,
                    col_tap : col_tap + LATENT_COLUMNS,
                    :,
                ]
                window = window.reshape(frames_out * LATENT_ROWS * LATENT_COLUMNS, inputs)
                tap = 9 * time_tap + 3 * row_tap + col_tap
                total = total + jnp.dot(window, weight[tap], preferred_element_type=jnp.float32)
    return total


def activate(stream, norm_scale_gain):
    values = stream.astype(jnp.float32)
    scale = lax.rsqrt(jnp.mean(values * values, axis=-1, keepdims=True) + 1e-06)
    return jax.nn.silu(values * scale * norm_scale_gain).astype(jnp.bfloat16)


def to_cells(planes):
    return jnp.transpose(
        planes.reshape(planes.shape[0], LATENT_CHANNELS, LATENT_ROWS, LATENT_COLUMNS), (0, 2, 3, 1)
    )


def by_block(
    sharded_latents,
    sample_frame_count,
    entry_kernel,
    entry_bias,
    norm_scale_gain,
    residual_kernel,
    residual_bias,
):
    gathered_latents = lax.all_to_all(
        sharded_latents, "tm", split_axis=0, concat_axis=1, tiled=True
    )
    latent_volume = gathered_latents.reshape(
        BLOCK_FRAMES, LATENT_CHANNELS, LATENT_ROWS * LATENT_COLUMNS
    )
    position = lax.axis_index("tm")
    block = position // PROMPT_SAMPLES
    sample = position % PROMPT_SAMPLES
    keep = block > 0
    earlier = from_behind(latent_volume, "tm", PROMPT_SAMPLES)
    earlier = jnp.where(keep, earlier, jnp.zeros_like(earlier))
    frames = to_cells(jnp.concatenate([earlier, latent_volume], axis=0))
    widened = (causal_conv(frames, entry_kernel) + entry_bias).astype(jnp.bfloat16)
    active_all = activate(widened, norm_scale_gain).reshape(
        BLOCK_FRAMES + 2, LATENT_ROWS, LATENT_COLUMNS, C
    )
    behind = jnp.where(keep, active_all[:2], jnp.zeros_like(active_all[:2]))
    extended = jnp.concatenate([behind, active_all[2:]], axis=0)
    stream = widened[2 * LATENT_ROWS * LATENT_COLUMNS :]
    kernel_all = lax.all_gather(residual_kernel, "tm", axis=1, tiled=True)
    branch = causal_conv(extended, kernel_all)
    total = (stream.astype(jnp.float32) + (branch + residual_bias)).reshape(
        BLOCK_FRAMES, LATENT_ROWS, LATENT_COLUMNS, C
    )
    limit = jnp.sum(jnp.where(jnp.arange(PROMPT_SAMPLES) == sample, sample_frame_count, 0))
    frame_index = block * BLOCK_FRAMES + jnp.arange(BLOCK_FRAMES)
    valid = (frame_index < limit)[:, None, None, None]
    return jnp.where(valid, total, jnp.zeros_like(total)).astype(jnp.bfloat16)


def solution(mesh):
    n = mesh.shape["tm"]
    cells = BLOCK_FRAMES * LATENT_CHANNELS * HW
    fits = mesh.shape["groups"] == 2 and 9 * (C // n) <= 256 and n % 4 == 0 and n & (n - 1) == 0
    whole_rows = fits and cells % (n * HW) == 0 and C % n == 0 and (C // n) % 8 == 0 and n % PROMPT_SAMPLES == 0
    body = functools.partial(by_channel, n) if whole_rows else by_block
    in_specs = (P("groups", "tm"), P("groups"), P(), P(), P(), P(None, "tm", None), P())
    out_specs = P(("groups", "tm"), None, None, None)
    return jax.shard_map(body, mesh=mesh, in_specs=in_specs, out_specs=out_specs, check_vma=False)
```

```python
import functools

import jax
import jax.numpy as jnp
from jax import lax
from jax.experimental import pallas as pl
from jax.experimental.pallas import tpu as pltpu
from jax.sharding import PartitionSpec as P

LATENT_CHANNELS = 16
C = 384
PROMPT_SAMPLES = 8
BLOCK_FRAMES = 4
LATENT_ROWS = 6
LATENT_COLUMNS = 16
HW = LATENT_ROWS * LATENT_COLUMNS
LANES = PROMPT_SAMPLES * HW
VMEM = pl.BlockSpec(memory_space=pltpu.VMEM)
SMEM = pl.BlockSpec(memory_space=pltpu.SMEM)
ANY = pl.BlockSpec(memory_space=pl.ANY)


def shift_mask(j, k):
    lane = lax.broadcasted_iota(jnp.int32, (1, LANES), 1)
    row = (lane % HW) // LATENT_COLUMNS
    col = lane % LATENT_COLUMNS
    ok = lane >= 0
    if j == 0:
        ok = row > 0
    elif j == 2:
        ok = row < LATENT_ROWS - 1
    if k == 0:
        ok = ok & (col > 0)
    elif k == 2:
        ok = ok & (col < LATENT_COLUMNS - 1)
    return ok


def shifted(x, delta):
    return x if delta == 0 else pltpu.roll(x, (-delta) % x.shape[1], 1)


def packing(own):
    runs = 3 * (own // 8)
    places = {}
    for run in range(runs):
        for t in range(9):
            if run < runs // 2 * 2:
                place = (run // (runs // 2), (run % (runs // 2) * 9 + t) * own)
            else:
                place = (0 if t < 5 else 1, (runs // 2 * 9 + (t if t < 5 else t - 5)) * own)
            places[run // (own // 8), run % (own // 8), t] = place
    longest = max(lane for _, lane in places.values()) + own
    return places, -(-longest // 128) * 128


def parcels_kernel(n, x_hbm, w_hbm, side_ref, o_hbm, x_ref, w_ref, o_ref, in_sem, out_sem):
    own = C // n
    get_x = pltpu.make_async_copy(x_hbm, x_ref, in_sem.at[0])
    get_w = pltpu.make_async_copy(w_hbm, w_ref, in_sem.at[1])
    get_x.start()
    get_w.start()
    get_x.wait()
    x = x_ref[...].astype(jnp.float32)
    rows = []
    for b in range(x.shape[0] // PROMPT_SAMPLES):
        for c in range(x.shape[1] // HW):
            at = b * PROMPT_SAMPLES
            pieces = [x[r : r + 1, c * HW : (c + 1) * HW] for r in range(at, at + PROMPT_SAMPLES)]
            rows.append(jnp.concatenate(pieces, axis=1))
    rows = jnp.concatenate(rows, axis=0)
    tiles = [rows[:, t * 128 : (t + 1) * 128] for t in range(LANES // 128)]
    get_w.wait()
    w = w_ref[...].astype(jnp.float32).reshape(3, 9, own // 8, 8, C)
    puts = []
    places, width = packing(own)
    left = jnp.broadcast_to(side_ref[0] == 0, (8, C))
    by_lane = [{place[1]: w[i, t, c] for (i, c, t), place in places.items() if place[0] == side} for side in range(2)]
    chosen = []
    for lane in sorted(by_lane[0]):
        first = by_lane[0][lane]
        chosen.append(jnp.where(left, first, by_lane[1].get(lane, first)))
    gap = jnp.zeros((8, width - len(chosen) * own), jnp.float32)
    half = len(tiles) // 2
    for d in range(0, n, 2):
        both = []
        for e in (d, d + 1):
            share = jnp.concatenate([piece[:, e * own : (e + 1) * own] for piece in chosen] + [gap], axis=1)
            both += [share[:, t * 128 : (t + 1) * 128] for t in range(width // 128)]
            both += tiles[half:] if e % 2 else tiles[:half]
        both = jnp.concatenate(both, axis=0).astype(jnp.bfloat16)
        o_ref[d // 2 * both.shape[0] : (d // 2 + 1) * both.shape[0], :] = both
        if d % 4 == 2:
            rows = pl.ds((d // 4) * 2 * both.shape[0], 2 * both.shape[0])
            puts.append(pltpu.make_async_copy(o_ref.at[rows], o_hbm.at[rows], out_sem.at[d // 4]))
            puts[-1].start()
    for put in puts:
        put.wait()


def column(rows):
    parts = [jnp.transpose(jnp.broadcast_to(rows[t : t + 1], (128, 128))) for t in range(rows.shape[0])]
    return jnp.concatenate(parts, axis=0)


def thirds(x):
    parts = []
    for _ in range(3):
        part = x.astype(jnp.bfloat16).astype(jnp.float32)
        parts.append(part)
        x = x - part
    return parts


def params_kernel(n, entry_ref, vectors_ref, first_ref, o_ref, row_ref):
    own = C // n
    depth = 27 * LATENT_CHANNELS
    tall = C // 128
    first = pl.multiple_of(first_ref[0], 8)
    lane = lax.broadcasted_iota(jnp.int32, (C, 16), 1)

    def spread(t):
        tile = column(vectors_ref[t * tall : (t + 1) * tall])[:, :16]
        out = jnp.zeros((C, 16), jnp.float32)
        for t, part in enumerate(thirds(tile)):
            out = jnp.where(lane == t, part, out)
        return out

    half_gain = column(vectors_ref[tall : 2 * tall]) * 0.5
    gap = jnp.zeros((C, 512 - depth - 16), jnp.float32)
    weight = jnp.transpose(entry_ref[...].astype(jnp.float32))
    full = jnp.concatenate([weight, spread(0), gap, half_gain], axis=1)
    row_ref[0:C, :] = full
    row_ref[C : 2 * C, :] = jnp.concatenate([jnp.zeros_like(weight), spread(2), gap, half_gain], axis=1)
    mine = row_ref[pl.ds(first, own), :]
    after = row_ref[pl.ds(first + C, own), :]
    o_ref[...] = jnp.concatenate([mine, after, full], axis=0).astype(jnp.bfloat16)


def active_kernel(n, got_ref, lat_ref, params_ref, odd_ref, x_ref, stream_ref, col_ref):
    own = C // n
    frames = n // PROMPT_SAMPLES * BLOCK_FRAMES
    each = LATENT_CHANNELS * BLOCK_FRAMES // n
    taps = 9 * LATENT_CHANNELS
    weight = params_ref[:, : 3 * taps + 16]
    half_gain = jnp.concatenate([params_ref[2 * own :, 512:]] * (LANES // 128), axis=1)
    ones = (lax.broadcasted_iota(jnp.int32, (16, LANES), 0) < 3).astype(jnp.float32).astype(jnp.bfloat16)
    per_frame = LATENT_CHANNELS // each
    blocks = n // PROMPT_SAMPLES
    mine = got_ref[...].astype(jnp.float32).reshape(n, -1, 128)[:, packing(own)[1] // 16 :]
    other = lat_ref[...].astype(jnp.float32).reshape(mine.shape)
    even = jnp.broadcast_to(odd_ref[0] == 0, mine.shape)
    lats = jnp.concatenate([jnp.where(even, mine, other), jnp.where(even, other, mine)], axis=1)
    lats = lats.reshape(n, LANES // 128, blocks * each, 128)
    lats = jnp.concatenate([lats[:, t] for t in range(LANES // 128)], axis=2)
    lats = lats.reshape(BLOCK_FRAMES, per_frame, blocks, each, LANES)
    for f in range(frames):
        b, g = divmod(f, BLOCK_FRAMES)
        lat = lats[g, :, b].reshape(LATENT_CHANNELS, LANES)
        for j in range(3):
            for k in range(3):
                moved = shifted(lat, LATENT_COLUMNS * (j - 1) + k - 1)
                moved = jnp.where(shift_mask(j, k), moved, 0.0)
                at = f * taps + (3 * j + k) * LATENT_CHANNELS
                col_ref[at : at + LATENT_CHANNELS, :] = moved.astype(jnp.bfloat16)
        least = max(f - 2, 0)
        z = jnp.dot(
            weight[:, (2 - (f - least)) * taps :],
            jnp.concatenate([col_ref[least * taps : (f + 1) * taps, :], ones], axis=0),
            preferred_element_type=jnp.float32,
        )
        stream_ref[f] = z[:own].astype(jnp.bfloat16).astype(jnp.float32) + z[own : 2 * own]
        s = z[2 * own :]
        scale = lax.rsqrt(jnp.sum(s * s, axis=0, keepdims=True) * (1.0 / C) + 1e-06)
        half = s.astype(jnp.bfloat16) * half_gain * scale.astype(jnp.bfloat16)
        x_ref[f * C : (f + 1) * C, :] = half + half * jnp.tanh(half)


def branch_kernel(n, got_ref, w_ref, x_ref, stream_ref, side_ref, count_ref, o_ref, out_ref):
    own = C // n
    frames = n // PROMPT_SAMPLES * BLOCK_FRAMES
    places, width = packing(own)

    def lanes(x):
        x = x.reshape(n, width // 128, 8, 128)
        return jnp.concatenate([x[:, t] for t in range(width // 128)], axis=2).reshape(n * 8, width)

    mine = lanes(got_ref[...].astype(jnp.float32).reshape(n, -1, 128)[:, : width // 16])
    other = lanes(w_ref[...].astype(jnp.float32))
    left = jnp.broadcast_to(side_ref[0] == 0, other.shape)
    halves = (jnp.where(left, mine, other), jnp.where(left, other, mine))
    pad = jnp.zeros((n * 8, 256 - 9 * own), jnp.float32)
    depths = []
    for i in range(3):
        runs = []
        for c in range(own // 8):
            side, lane = places[i, c, 0]
            if places[i, c, 8][0] == side:
                parts = [halves[side][:, lane : lane + 9 * own]]
            else:
                end = places[i, c, 5][1]
                parts = [halves[0][:, lane : lane + 5 * own], halves[1][:, end : end + 4 * own]]
            runs.append(jnp.concatenate(parts + [pad], axis=1).reshape(n, 1, 8, 256))
        depths.append(jnp.concatenate(runs, axis=1).reshape(C, 256))
    w = jnp.concatenate(depths, axis=0)
    weight = jnp.transpose(w.astype(jnp.bfloat16))[: -(-9 * own // 16) * 16]
    lane = lax.broadcasted_iota(jnp.int32, (1, LANES), 1)
    count = jnp.zeros((1, LANES), jnp.int32)
    for s in range(PROMPT_SAMPLES):
        count = jnp.where(lane // HW == s, count_ref[s], count)
    for f in range(frames):
        least = max(f - 2, 0)
        z = jnp.dot(
            weight[:, (2 - (f - least)) * C :],
            x_ref[least * C : (f + 1) * C, :],
            preferred_element_type=jnp.float32,
        )
        total = stream_ref[f]
        for k in range(3):
            part = None
            for j in range(3):
                tap = z[(3 * j + k) * own : (3 * j + k + 1) * own]
                if j != 1:
                    tap = jnp.where(shift_mask(j, 1), shifted(tap, LATENT_COLUMNS * (j - 1)), 0.0)
                part = tap if part is None else part + tap
            if k != 1:
                part = jnp.where(shift_mask(1, k), shifted(part, k - 1), 0.0)
            total = total + part
        out_ref[f] = jnp.where(count > f, total, 0.0)
        b, g = divmod(f, BLOCK_FRAMES)
        if g == BLOCK_FRAMES - 1:
            parts = [out_ref[b * BLOCK_FRAMES + t] for t in range(BLOCK_FRAMES)]
            for s in range(0, PROMPT_SAMPLES, 2):
                both = [
                    jnp.concatenate([p[:, t * HW : (t + 1) * HW] for p in parts], axis=1) for t in (s, s + 1)
                ]
                at = (b * PROMPT_SAMPLES + s) * own
                o_ref[at : at + 2 * own, :] = jnp.concatenate(both, axis=0).astype(jnp.bfloat16)


def transpose_kernel(x_ref, o_ref):
    o_ref[...] = jnp.transpose(x_ref[...])


def call(body, out, ins, outs, scratch=(), flops=0, moved=0, limit=8):
    return pl.pallas_call(
        body,
        out_shape=out,
        in_specs=ins,
        out_specs=outs,
        scratch_shapes=list(scratch),
        compiler_params=pltpu.CompilerParams(vmem_limit_bytes=limit * 1024 * 1024),
        cost_estimate=pl.CostEstimate(flops=flops, bytes_accessed=moved, transcendentals=0),
    )


def by_channel(n, latents, counts, entry_kernel, entry_bias, gain, kernel, bias):
    own = C // n
    frames = n // PROMPT_SAMPLES * BLOCK_FRAMES
    first = (lax.axis_index("tm") * own).astype(jnp.int32).reshape(1)
    shape = jax.ShapeDtypeStruct
    bf16, f32 = jnp.bfloat16, jnp.float32
    side = lax.axis_index("groups").astype(jnp.int32).reshape(1)
    each = latents.shape[1] // HW * (n // PROMPT_SAMPLES)
    odd = (lax.axis_index("tm") % 2).astype(jnp.int32).reshape(1)
    height = packing(own)[1] // 16
    extra = each * LANES // 256
    parcels = call(
        functools.partial(parcels_kernel, n),
        shape((n * (height + extra), 128), bf16),
        [ANY, ANY, SMEM],
        ANY,
        [
            pltpu.VMEM(latents.shape, bf16),
            pltpu.VMEM(kernel.shape, bf16),
            pltpu.VMEM((n * (height + extra), 128), bf16),
            pltpu.SemaphoreType.DMA((2,)),
            pltpu.SemaphoreType.DMA((n // 4,)),
        ],
        limit=58,
    )(latents, kernel, side)
    got = lax.all_to_all(parcels, "tm", split_axis=0, concat_axis=0, tiled=True)
    params = call(
        functools.partial(params_kernel, n),
        shape((2 * own + C, 640), bf16),
        [VMEM, VMEM, SMEM],
        VMEM,
        [pltpu.VMEM((2 * C, 640), f32)],
        flops=500_000_000,
        moved=2_000_000,
    )(
        entry_kernel.reshape(27 * LATENT_CHANNELS, C),
        jnp.concatenate([entry_bias, gain, bias]).reshape(-1, 128),
        first,
    )
    split = got.reshape(n, height + extra, 128)
    other = lax.ppermute(split[:, :height].reshape(n * height, 128), "groups", [(0, 1), (1, 0)])
    lats = split[:, height:].reshape(-1, 128)
    lats = lax.ppermute(lats, "tm", [(i, i ^ 1) for i in range(n)])
    active, stream = call(
        functools.partial(active_kernel, n),
        (shape((frames * C, LANES), bf16), shape((frames, own, LANES), f32)),
        [VMEM, VMEM, VMEM, SMEM],
        (VMEM, VMEM),
        [pltpu.VMEM((frames * 9 * LATENT_CHANNELS, LANES), bf16)],
        flops=2 * frames * LANES * 432 * C,
        moved=20_000_000,
        limit=24,
    )(got, lats, params, odd)
    out = call(
        functools.partial(branch_kernel, n),
        shape((n * own, BLOCK_FRAMES * HW), bf16),
        [VMEM, VMEM, VMEM, VMEM, SMEM, SMEM],
        VMEM,
        [pltpu.VMEM((frames, own, LANES), f32)],
        flops=2 * frames * LANES * 27 * C * own,
        moved=20_000_000,
        limit=24,
    )(got, other, active, stream, side, counts)
    out = lax.all_to_all(out, "tm", split_axis=0, concat_axis=0, tiled=True)
    out = call(transpose_kernel, shape((BLOCK_FRAMES * HW, C), bf16), [VMEM], VMEM)(out)
    return out.reshape(BLOCK_FRAMES, LATENT_ROWS, LATENT_COLUMNS, C)


def from_behind(block, axis, distance):
    devices = range(lax.axis_size(axis))
    route = [(i - distance, i) for i in devices if i - distance in devices]
    return lax.ppermute(block, axis, route)


def causal_conv(frames, weight):
    frames_out = frames.shape[0] - 2
    inputs = frames.shape[3]
    padded = jnp.pad(frames, ((0, 0), (1, 1), (1, 1), (0, 0)))
    total = jnp.zeros((frames_out * LATENT_ROWS * LATENT_COLUMNS, weight.shape[2]), jnp.float32)
    for time_tap in range(3):
        for row_tap in range(3):
            for col_tap in range(3):
                window = padded[
                    time_tap : time_tap + frames_out,
                    row_tap : row_tap + LATENT_ROWS,
                    col_tap : col_tap + LATENT_COLUMNS,
                    :,
                ]
                window = window.reshape(frames_out * LATENT_ROWS * LATENT_COLUMNS, inputs)
                tap = 9 * time_tap + 3 * row_tap + col_tap
                total = total + jnp.dot(window, weight[tap], preferred_element_type=jnp.float32)
    return total


def activate(stream, norm_scale_gain):
    values = stream.astype(jnp.float32)
    scale = lax.rsqrt(jnp.mean(values * values, axis=-1, keepdims=True) + 1e-06)
    return jax.nn.silu(values * scale * norm_scale_gain).astype(jnp.bfloat16)


def to_cells(planes):
    return jnp.transpose(
        planes.reshape(planes.shape[0], LATENT_CHANNELS, LATENT_ROWS, LATENT_COLUMNS), (0, 2, 3, 1)
    )


def by_block(
    sharded_latents,
    sample_frame_count,
    entry_kernel,
    entry_bias,
    norm_scale_gain,
    residual_kernel,
    residual_bias,
):
    gathered_latents = lax.all_to_all(
        sharded_latents, "tm", split_axis=0, concat_axis=1, tiled=True
    )
    latent_volume = gathered_latents.reshape(
        BLOCK_FRAMES, LATENT_CHANNELS, LATENT_ROWS * LATENT_COLUMNS
    )
    position = lax.axis_index("tm")
    block = position // PROMPT_SAMPLES
    sample = position % PROMPT_SAMPLES
    keep = block > 0
    earlier = from_behind(latent_volume, "tm", PROMPT_SAMPLES)
    earlier = jnp.where(keep, earlier, jnp.zeros_like(earlier))
    frames = to_cells(jnp.concatenate([earlier, latent_volume], axis=0))
    widened = (causal_conv(frames, entry_kernel) + entry_bias).astype(jnp.bfloat16)
    active_all = activate(widened, norm_scale_gain).reshape(
        BLOCK_FRAMES + 2, LATENT_ROWS, LATENT_COLUMNS, C
    )
    behind = jnp.where(keep, active_all[:2], jnp.zeros_like(active_all[:2]))
    extended = jnp.concatenate([behind, active_all[2:]], axis=0)
    stream = widened[2 * LATENT_ROWS * LATENT_COLUMNS :]
    kernel_all = lax.all_gather(residual_kernel, "tm", axis=1, tiled=True)
    branch = causal_conv(extended, kernel_all)
    total = (stream.astype(jnp.float32) + (branch + residual_bias)).reshape(
        BLOCK_FRAMES, LATENT_ROWS, LATENT_COLUMNS, C
    )
    limit = jnp.sum(jnp.where(jnp.arange(PROMPT_SAMPLES) == sample, sample_frame_count, 0))
    frame_index = block * BLOCK_FRAMES + jnp.arange(BLOCK_FRAMES)
    valid = (frame_index < limit)[:, None, None, None]
    return jnp.where(valid, total, jnp.zeros_like(total)).astype(jnp.bfloat16)


def solution(mesh):
    n = mesh.shape["tm"]
    cells = BLOCK_FRAMES * LATENT_CHANNELS * HW
    fits = mesh.shape["groups"] == 2 and 9 * (C // n) <= 256 and n % 4 == 0 and LANES % 256 == 0
    whole_rows = fits and cells % (n * HW) == 0 and C % n == 0 and (C // n) % 8 == 0 and n % PROMPT_SAMPLES == 0
    body = functools.partial(by_channel, n) if whole_rows else by_block
    in_specs = (P("groups", "tm"), P("groups"), P(), P(), P(), P(None, "tm", None), P())
    out_specs = P(("groups", "tm"), None, None, None)
    return jax.shard_map(body, mesh=mesh, in_specs=in_specs, out_specs=out_specs, check_vma=False)
```

```python
import functools

import jax
import jax.numpy as jnp
from jax import lax
from jax.experimental import pallas as pl
from jax.experimental.pallas import tpu as pltpu
from jax.sharding import PartitionSpec as P

LATENT_CHANNELS = 16
C = 384
PROMPT_SAMPLES = 8
BLOCK_FRAMES = 4
LATENT_ROWS = 6
LATENT_COLUMNS = 16
HW = LATENT_ROWS * LATENT_COLUMNS
LANES = PROMPT_SAMPLES * HW
VMEM = pl.BlockSpec(memory_space=pltpu.VMEM)
SMEM = pl.BlockSpec(memory_space=pltpu.SMEM)
ANY = pl.BlockSpec(memory_space=pl.ANY)


def shift_mask(j, k):
    lane = lax.broadcasted_iota(jnp.int32, (1, LANES), 1)
    row = (lane % HW) // LATENT_COLUMNS
    col = lane % LATENT_COLUMNS
    ok = lane >= 0
    if j == 0:
        ok = row > 0
    elif j == 2:
        ok = row < LATENT_ROWS - 1
    if k == 0:
        ok = ok & (col > 0)
    elif k == 2:
        ok = ok & (col < LATENT_COLUMNS - 1)
    return ok


def shifted(x, delta):
    return x if delta == 0 else pltpu.roll(x, (-delta) % x.shape[1], 1)


def packing(own):
    runs = 3 * (own // 8)
    places = {}
    for run in range(runs):
        for t in range(9):
            if run < runs // 2 * 2:
                place = (run // (runs // 2), (run % (runs // 2) * 9 + t) * own)
            else:
                place = (0 if t < 5 else 1, (runs // 2 * 9 + (t if t < 5 else t - 5)) * own)
            places[run // (own // 8), run % (own // 8), t] = place
    longest = max(lane for _, lane in places.values()) + own
    return places, -(-longest // 128) * 128


def unpacked(got, n, own):
    width = packing(own)[1]
    x = got.reshape(n, width // 128, 8, 128)
    x = jnp.concatenate([x[:, t] for t in range(width // 128)], axis=2).reshape(n * 8, width)
    runs = 3 * (own // 8)
    ends = [(r * 9 * own, (r + 1) * 9 * own) for r in range(runs // 2)]
    if runs % 2:
        ends.append((runs // 2 * 9 * own, (runs // 2 * 9 + 5) * own))
    pad = lambda a, b: jnp.zeros((n * 8, 256 - (b - a)), jnp.float32)
    return [jnp.concatenate([x[:, a:b], pad(a, b)], axis=1) for a, b in ends]


def parcels_kernel(n, x_hbm, w_hbm, side_ref, o_hbm, x_ref, w_ref, o_ref, in_sem, out_sem):
    own = C // n
    get_x = pltpu.make_async_copy(x_hbm, x_ref, in_sem.at[0])
    get_w = pltpu.make_async_copy(w_hbm, w_ref, in_sem.at[1])
    get_x.start()
    get_w.start()
    get_x.wait()
    x = x_ref[...].astype(jnp.float32)
    rows = []
    for b in range(x.shape[0] // PROMPT_SAMPLES):
        for c in range(x.shape[1] // HW):
            at = b * PROMPT_SAMPLES
            pieces = [x[r : r + 1, c * HW : (c + 1) * HW] for r in range(at, at + PROMPT_SAMPLES)]
            rows.append(jnp.concatenate(pieces, axis=1))
    rows = jnp.concatenate(rows, axis=0)
    tiles = [rows[:, t * 128 : (t + 1) * 128] for t in range(LANES // 128)]
    get_w.wait()
    w = w_ref[...].astype(jnp.float32).reshape(3, 9, own // 8, 8, C)
    puts = []
    places, width = packing(own)
    left = jnp.broadcast_to(side_ref[0] == 0, (8, C))
    by_lane = [{place[1]: w[i, t, c] for (i, c, t), place in places.items() if place[0] == side} for side in range(2)]
    chosen = []
    for lane in sorted(by_lane[0]):
        first = by_lane[0][lane]
        chosen.append(jnp.where(left, first, by_lane[1].get(lane, first)))
    gap = jnp.zeros((8, width - len(chosen) * own), jnp.float32)
    half = len(tiles) // 2
    for d in range(0, n, 2):
        both = []
        for e in (d, d + 1):
            share = jnp.concatenate([piece[:, e * own : (e + 1) * own] for piece in chosen] + [gap], axis=1)
            both += [share[:, t * 128 : (t + 1) * 128] for t in range(width // 128)]
            both += tiles[half:] if e % 2 else tiles[:half]
        both = jnp.concatenate(both, axis=0).astype(jnp.bfloat16)
        o_ref[d // 2 * both.shape[0] : (d // 2 + 1) * both.shape[0], :] = both
        if d % 4 == 2:
            rows = pl.ds((d // 4) * 2 * both.shape[0], 2 * both.shape[0])
            puts.append(pltpu.make_async_copy(o_ref.at[rows], o_hbm.at[rows], out_sem.at[d // 4]))
            puts[-1].start()
    for put in puts:
        put.wait()


def column(rows):
    parts = [jnp.transpose(jnp.broadcast_to(rows[t : t + 1], (128, 128))) for t in range(rows.shape[0])]
    return jnp.concatenate(parts, axis=0)


def thirds(x):
    parts = []
    for _ in range(3):
        part = x.astype(jnp.bfloat16).astype(jnp.float32)
        parts.append(part)
        x = x - part
    return parts


def params_kernel(n, entry_ref, vectors_ref, first_ref, o_ref, row_ref):
    own = C // n
    depth = 27 * LATENT_CHANNELS
    tall = C // 128
    first = pl.multiple_of(first_ref[0], 8)
    lane = lax.broadcasted_iota(jnp.int32, (C, 16), 1)

    def spread(t):
        tile = column(vectors_ref[t * tall : (t + 1) * tall])[:, :16]
        out = jnp.zeros((C, 16), jnp.float32)
        for t, part in enumerate(thirds(tile)):
            out = jnp.where(lane == t, part, out)
        return out

    half_gain = column(vectors_ref[tall : 2 * tall]) * 0.5
    gap = jnp.zeros((C, 512 - depth - 16), jnp.float32)
    weight = jnp.transpose(entry_ref[...].astype(jnp.float32))
    full = jnp.concatenate([weight, spread(0), gap, half_gain], axis=1)
    row_ref[0:C, :] = full
    row_ref[C : 2 * C, :] = jnp.concatenate([jnp.zeros_like(weight), spread(2), gap, half_gain], axis=1)
    mine = row_ref[pl.ds(first, own), :]
    after = row_ref[pl.ds(first + C, own), :]
    o_ref[...] = jnp.concatenate([mine, after, full], axis=0).astype(jnp.bfloat16)


def active_kernel(n, got_ref, lat_ref, params_ref, odd_ref, x_ref, stream_ref, half_ref, col_ref):
    own = C // n
    frames = n // PROMPT_SAMPLES * BLOCK_FRAMES
    each = LATENT_CHANNELS * BLOCK_FRAMES // n
    taps = 9 * LATENT_CHANNELS
    weight = params_ref[:, : 3 * taps + 16]
    half_gain = jnp.concatenate([params_ref[2 * own :, 512:]] * (LANES // 128), axis=1)
    ones = (lax.broadcasted_iota(jnp.int32, (16, LANES), 0) < 3).astype(jnp.float32).astype(jnp.bfloat16)
    per_frame = LATENT_CHANNELS // each
    blocks = n // PROMPT_SAMPLES
    got = got_ref[...].astype(jnp.float32).reshape(n, -1, 128)
    share = unpacked(got[:, : packing(own)[1] // 16], n, own)
    for r, run in enumerate(share):
        half_ref[r] = run
    mine = got[:, packing(own)[1] // 16 :]
    other = lat_ref[...].astype(jnp.float32).reshape(mine.shape)
    even = jnp.broadcast_to(odd_ref[0] == 0, mine.shape)
    lats = jnp.concatenate([jnp.where(even, mine, other), jnp.where(even, other, mine)], axis=1)
    lats = lats.reshape(n, LANES // 128, blocks * each, 128)
    lats = jnp.concatenate([lats[:, t] for t in range(LANES // 128)], axis=2)
    lats = lats.reshape(BLOCK_FRAMES, per_frame, blocks, each, LANES)
    for f in range(frames):
        b, g = divmod(f, BLOCK_FRAMES)
        lat = lats[g, :, b].reshape(LATENT_CHANNELS, LANES)
        for j in range(3):
            for k in range(3):
                moved = shifted(lat, LATENT_COLUMNS * (j - 1) + k - 1)
                moved = jnp.where(shift_mask(j, k), moved, 0.0)
                at = f * taps + (3 * j + k) * LATENT_CHANNELS
                col_ref[at : at + LATENT_CHANNELS, :] = moved.astype(jnp.bfloat16)
        least = max(f - 2, 0)
        z = jnp.dot(
            weight[:, (2 - (f - least)) * taps :],
            jnp.concatenate([col_ref[least * taps : (f + 1) * taps, :], ones], axis=0),
            preferred_element_type=jnp.float32,
        )
        stream_ref[f] = z[:own].astype(jnp.bfloat16).astype(jnp.float32) + z[own : 2 * own]
        s = z[2 * own :]
        scale = lax.rsqrt(jnp.sum(s * s, axis=0, keepdims=True) * (1.0 / C) + 1e-06)
        half = s.astype(jnp.bfloat16) * half_gain * scale.astype(jnp.bfloat16)
        x_ref[f * C : (f + 1) * C, :] = half + half * jnp.tanh(half)


def branch_kernel(n, half_ref, w_ref, x_ref, stream_ref, side_ref, count_ref, o_ref, out_ref):
    own = C // n
    frames = n // PROMPT_SAMPLES * BLOCK_FRAMES
    other = unpacked(w_ref[...].astype(jnp.float32), n, own)
    mine = [half_ref[r] for r in range(len(other))]
    left = jnp.broadcast_to(side_ref[0] == 0, (n * 8, 256))
    low = [jnp.where(left, m, o) for m, o in zip(mine, other)]
    high = [jnp.where(left, o, m) for m, o in zip(mine, other)]
    whole = 3 * (own // 8) // 2
    runs = low[:whole] + high[:whole]
    if len(low) > whole:
        rest = jnp.zeros((n * 8, 256 - 9 * own), jnp.float32)
        runs.append(jnp.concatenate([low[whole][:, : 5 * own], high[whole][:, : 4 * own], rest], axis=1))
    runs = [run.reshape(n, 1, 8, 256) for run in runs]
    depths = []
    for i in range(3):
        at = i * (own // 8)
        depths.append(jnp.concatenate(runs[at : at + own // 8], axis=1).reshape(C, 256))
    w = jnp.concatenate(depths, axis=0)
    weight = jnp.transpose(w.astype(jnp.bfloat16))[: -(-9 * own // 16) * 16]
    lane = lax.broadcasted_iota(jnp.int32, (1, LANES), 1)
    count = jnp.zeros((1, LANES), jnp.int32)
    for s in range(PROMPT_SAMPLES):
        count = jnp.where(lane // HW == s, count_ref[s], count)
    for f in range(frames):
        least = max(f - 2, 0)
        z = jnp.dot(
            weight[:, (2 - (f - least)) * C :],
            x_ref[least * C : (f + 1) * C, :],
            preferred_element_type=jnp.float32,
        )
        total = stream_ref[f]
        for k in range(3):
            part = None
            for j in range(3):
                tap = z[(3 * j + k) * own : (3 * j + k + 1) * own]
                if j != 1:
                    tap = jnp.where(shift_mask(j, 1), shifted(tap, LATENT_COLUMNS * (j - 1)), 0.0)
                part = tap if part is None else part + tap
            if k != 1:
                part = jnp.where(shift_mask(1, k), shifted(part, k - 1), 0.0)
            total = total + part
        out_ref[f] = jnp.where(count > f, total, 0.0)
        b, g = divmod(f, BLOCK_FRAMES)
        if g == BLOCK_FRAMES - 1:
            parts = [out_ref[b * BLOCK_FRAMES + t] for t in range(BLOCK_FRAMES)]
            for s in range(0, PROMPT_SAMPLES, 2):
                both = [
                    jnp.concatenate([p[:, t * HW : (t + 1) * HW] for p in parts], axis=1) for t in (s, s + 1)
                ]
                at = (b * PROMPT_SAMPLES + s) * own
                o_ref[at : at + 2 * own, :] = jnp.concatenate(both, axis=0).astype(jnp.bfloat16)


def transpose_kernel(x_ref, o_ref):
    o_ref[...] = jnp.transpose(x_ref[...])


def call(body, out, ins, outs, scratch=(), flops=0, moved=0, limit=8):
    return pl.pallas_call(
        body,
        out_shape=out,
        in_specs=ins,
        out_specs=outs,
        scratch_shapes=list(scratch),
        compiler_params=pltpu.CompilerParams(vmem_limit_bytes=limit * 1024 * 1024),
        cost_estimate=pl.CostEstimate(flops=flops, bytes_accessed=moved, transcendentals=0),
    )


def by_channel(n, latents, counts, entry_kernel, entry_bias, gain, kernel, bias):
    own = C // n
    frames = n // PROMPT_SAMPLES * BLOCK_FRAMES
    first = (lax.axis_index("tm") * own).astype(jnp.int32).reshape(1)
    shape = jax.ShapeDtypeStruct
    bf16, f32 = jnp.bfloat16, jnp.float32
    side = lax.axis_index("groups").astype(jnp.int32).reshape(1)
    each = latents.shape[1] // HW * (n // PROMPT_SAMPLES)
    odd = (lax.axis_index("tm") % 2).astype(jnp.int32).reshape(1)
    height = packing(own)[1] // 16
    extra = each * LANES // 256
    parcels = call(
        functools.partial(parcels_kernel, n),
        shape((n * (height + extra), 128), bf16),
        [ANY, ANY, SMEM],
        ANY,
        [
            pltpu.VMEM(latents.shape, bf16),
            pltpu.VMEM(kernel.shape, bf16),
            pltpu.VMEM((n * (height + extra), 128), bf16),
            pltpu.SemaphoreType.DMA((2,)),
            pltpu.SemaphoreType.DMA((n // 4,)),
        ],
        limit=58,
    )(latents, kernel, side)
    got = lax.all_to_all(parcels, "tm", split_axis=0, concat_axis=0, tiled=True)
    params = call(
        functools.partial(params_kernel, n),
        shape((2 * own + C, 640), bf16),
        [VMEM, VMEM, SMEM],
        VMEM,
        [pltpu.VMEM((2 * C, 640), f32)],
        flops=500_000_000,
        moved=2_000_000,
    )(
        entry_kernel.reshape(27 * LATENT_CHANNELS, C),
        jnp.concatenate([entry_bias, gain, bias]).reshape(-1, 128),
        first,
    )
    split = got.reshape(n, height + extra, 128)
    other = lax.ppermute(split[:, :height].reshape(n * height, 128), "groups", [(0, 1), (1, 0)])
    lats = split[:, height:].reshape(-1, 128)
    lats = lax.ppermute(lats, "tm", [(i, i ^ 1) for i in range(n)])
    halves = 3 * (own // 8) // 2 + 3 * (own // 8) % 2
    active, stream, half = call(
        functools.partial(active_kernel, n),
        (
            shape((frames * C, LANES), bf16),
            shape((frames, own, LANES), f32),
            shape((halves, n * 8, 256), f32),
        ),
        [VMEM, VMEM, VMEM, SMEM],
        (VMEM, VMEM, VMEM),
        [pltpu.VMEM((frames * 9 * LATENT_CHANNELS, LANES), bf16)],
        flops=2 * frames * LANES * 432 * C,
        moved=20_000_000,
        limit=24,
    )(got, lats, params, odd)
    out = call(
        functools.partial(branch_kernel, n),
        shape((n * own, BLOCK_FRAMES * HW), bf16),
        [VMEM, VMEM, VMEM, VMEM, SMEM, SMEM],
        VMEM,
        [pltpu.VMEM((frames, own, LANES), f32)],
        flops=2 * frames * LANES * 27 * C * own,
        moved=20_000_000,
        limit=24,
    )(half, other, active, stream, side, counts)
    out = lax.all_to_all(out, "tm", split_axis=0, concat_axis=0, tiled=True)
    out = call(transpose_kernel, shape((BLOCK_FRAMES * HW, C), bf16), [VMEM], VMEM)(out)
    return out.reshape(BLOCK_FRAMES, LATENT_ROWS, LATENT_COLUMNS, C)


def from_behind(block, axis, distance):
    devices = range(lax.axis_size(axis))
    route = [(i - distance, i) for i in devices if i - distance in devices]
    return lax.ppermute(block, axis, route)


def causal_conv(frames, weight):
    frames_out = frames.shape[0] - 2
    inputs = frames.shape[3]
    padded = jnp.pad(frames, ((0, 0), (1, 1), (1, 1), (0, 0)))
    total = jnp.zeros((frames_out * LATENT_ROWS * LATENT_COLUMNS, weight.shape[2]), jnp.float32)
    for time_tap in range(3):
        for row_tap in range(3):
            for col_tap in range(3):
                window = padded[
                    time_tap : time_tap + frames_out,
                    row_tap : row_tap + LATENT_ROWS,
                    col_tap : col_tap + LATENT_COLUMNS,
                    :,
                ]
                window = window.reshape(frames_out * LATENT_ROWS * LATENT_COLUMNS, inputs)
                tap = 9 * time_tap + 3 * row_tap + col_tap
                total = total + jnp.dot(window, weight[tap], preferred_element_type=jnp.float32)
    return total


def activate(stream, norm_scale_gain):
    values = stream.astype(jnp.float32)
    scale = lax.rsqrt(jnp.mean(values * values, axis=-1, keepdims=True) + 1e-06)
    return jax.nn.silu(values * scale * norm_scale_gain).astype(jnp.bfloat16)


def to_cells(planes):
    return jnp.transpose(
        planes.reshape(planes.shape[0], LATENT_CHANNELS, LATENT_ROWS, LATENT_COLUMNS), (0, 2, 3, 1)
    )


def by_block(
    sharded_latents,
    sample_frame_count,
    entry_kernel,
    entry_bias,
    norm_scale_gain,
    residual_kernel,
    residual_bias,
):
    gathered_latents = lax.all_to_all(
        sharded_latents, "tm", split_axis=0, concat_axis=1, tiled=True
    )
    latent_volume = gathered_latents.reshape(
        BLOCK_FRAMES, LATENT_CHANNELS, LATENT_ROWS * LATENT_COLUMNS
    )
    position = lax.axis_index("tm")
    block = position // PROMPT_SAMPLES
    sample = position % PROMPT_SAMPLES
    keep = block > 0
    earlier = from_behind(latent_volume, "tm", PROMPT_SAMPLES)
    earlier = jnp.where(keep, earlier, jnp.zeros_like(earlier))
    frames = to_cells(jnp.concatenate([earlier, latent_volume], axis=0))
    widened = (causal_conv(frames, entry_kernel) + entry_bias).astype(jnp.bfloat16)
    active_all = activate(widened, norm_scale_gain).reshape(
        BLOCK_FRAMES + 2, LATENT_ROWS, LATENT_COLUMNS, C
    )
    behind = jnp.where(keep, active_all[:2], jnp.zeros_like(active_all[:2]))
    extended = jnp.concatenate([behind, active_all[2:]], axis=0)
    stream = widened[2 * LATENT_ROWS * LATENT_COLUMNS :]
    kernel_all = lax.all_gather(residual_kernel, "tm", axis=1, tiled=True)
    branch = causal_conv(extended, kernel_all)
    total = (stream.astype(jnp.float32) + (branch + residual_bias)).reshape(
        BLOCK_FRAMES, LATENT_ROWS, LATENT_COLUMNS, C
    )
    limit = jnp.sum(jnp.where(jnp.arange(PROMPT_SAMPLES) == sample, sample_frame_count, 0))
    frame_index = block * BLOCK_FRAMES + jnp.arange(BLOCK_FRAMES)
    valid = (frame_index < limit)[:, None, None, None]
    return jnp.where(valid, total, jnp.zeros_like(total)).astype(jnp.bfloat16)


def solution(mesh):
    n = mesh.shape["tm"]
    cells = BLOCK_FRAMES * LATENT_CHANNELS * HW
    fits = mesh.shape["groups"] == 2 and 9 * (C // n) <= 256 and n % 4 == 0 and LANES % 256 == 0
    whole_rows = fits and cells % (n * HW) == 0 and C % n == 0 and (C // n) % 8 == 0 and n % PROMPT_SAMPLES == 0
    body = functools.partial(by_channel, n) if whole_rows else by_block
    in_specs = (P("groups", "tm"), P("groups"), P(), P(), P(), P(None, "tm", None), P())
    out_specs = P(("groups", "tm"), None, None, None)
    return jax.shard_map(body, mesh=mesh, in_specs=in_specs, out_specs=out_specs, check_vma=False)
```

```python
import functools

import jax
import jax.numpy as jnp
from jax import lax
from jax.experimental import pallas as pl
from jax.experimental.pallas import tpu as pltpu
from jax.sharding import PartitionSpec as P

LATENT_CHANNELS = 16
C = 384
PROMPT_SAMPLES = 8
BLOCK_FRAMES = 4
LATENT_ROWS = 6
LATENT_COLUMNS = 16
HW = LATENT_ROWS * LATENT_COLUMNS
LANES = PROMPT_SAMPLES * HW
VMEM = pl.BlockSpec(memory_space=pltpu.VMEM)
SMEM = pl.BlockSpec(memory_space=pltpu.SMEM)
ANY = pl.BlockSpec(memory_space=pl.ANY)


def shift_mask(j, k):
    lane = lax.broadcasted_iota(jnp.int32, (1, LANES), 1)
    row = (lane % HW) // LATENT_COLUMNS
    col = lane % LATENT_COLUMNS
    ok = lane >= 0
    if j == 0:
        ok = row > 0
    elif j == 2:
        ok = row < LATENT_ROWS - 1
    if k == 0:
        ok = ok & (col > 0)
    elif k == 2:
        ok = ok & (col < LATENT_COLUMNS - 1)
    return ok


def shifted(x, delta):
    return x if delta == 0 else pltpu.roll(x, (-delta) % x.shape[1], 1)


def packing(own):
    runs = 3 * (own // 8)
    places = {}
    for run in range(runs):
        for t in range(9):
            if run < runs // 2 * 2:
                place = (run // (runs // 2), (run % (runs // 2) * 9 + t) * own)
            else:
                place = (0 if t < 5 else 1, (runs // 2 * 9 + (t if t < 5 else t - 5)) * own)
            places[run // (own // 8), run % (own // 8), t] = place
    longest = max(lane for _, lane in places.values()) + own
    return places, -(-longest // 128) * 128


def unpacked(got, n, own):
    width = packing(own)[1]
    x = got.reshape(n, width // 128, 8, 128)
    x = jnp.concatenate([x[:, t] for t in range(width // 128)], axis=2).reshape(n * 8, width)
    runs = 3 * (own // 8)
    ends = [(r * 9 * own, (r + 1) * 9 * own) for r in range(runs // 2)]
    if runs % 2:
        ends.append((runs // 2 * 9 * own, (runs // 2 * 9 + 5) * own))
    pad = lambda a, b: jnp.zeros((n * 8, 256 - (b - a)), jnp.float32)
    return [jnp.concatenate([x[:, a:b], pad(a, b)], axis=1) for a, b in ends]


def parcels_kernel(n, x_hbm, w_hbm, side_ref, o_hbm, x_ref, w_ref, o_ref, in_sem, out_sem):
    own = C // n
    get_x = pltpu.make_async_copy(x_hbm, x_ref, in_sem.at[0])
    get_w = pltpu.make_async_copy(w_hbm, w_ref, in_sem.at[1])
    get_x.start()
    get_w.start()
    get_x.wait()
    x = x_ref[...].astype(jnp.float32)
    rows = []
    for b in range(x.shape[0] // PROMPT_SAMPLES):
        for c in range(x.shape[1] // HW):
            at = b * PROMPT_SAMPLES
            pieces = [x[r : r + 1, c * HW : (c + 1) * HW] for r in range(at, at + PROMPT_SAMPLES)]
            rows.append(jnp.concatenate(pieces, axis=1))
    rows = jnp.concatenate(rows, axis=0)
    tiles = [rows[:, t * 128 : (t + 1) * 128] for t in range(LANES // 128)]
    get_w.wait()
    w = w_ref[...].astype(jnp.float32).reshape(3, 9, own // 8, 8, C)
    puts = []
    places, width = packing(own)
    left = jnp.broadcast_to(side_ref[0] == 0, (8, C))
    by_lane = [{place[1]: w[i, t, c] for (i, c, t), place in places.items() if place[0] == side} for side in range(2)]
    chosen = []
    for lane in sorted(by_lane[0]):
        first = by_lane[0][lane]
        chosen.append(jnp.where(left, first, by_lane[1].get(lane, first)))
    gap = jnp.zeros((8, width - len(chosen) * own), jnp.float32)
    half = len(tiles) // 2
    for d in range(0, n, 2):
        both = []
        for e in (d, d + 1):
            share = jnp.concatenate([piece[:, e * own : (e + 1) * own] for piece in chosen] + [gap], axis=1)
            both += [share[:, t * 128 : (t + 1) * 128] for t in range(width // 128)]
            both += tiles[half:] if e % 2 else tiles[:half]
        both = jnp.concatenate(both, axis=0).astype(jnp.bfloat16)
        o_ref[d // 2 * both.shape[0] : (d // 2 + 1) * both.shape[0], :] = both
        if d % 4 == 2:
            rows = pl.ds((d // 4) * 2 * both.shape[0], 2 * both.shape[0])
            puts.append(pltpu.make_async_copy(o_ref.at[rows], o_hbm.at[rows], out_sem.at[d // 4]))
            puts[-1].start()
    for put in puts:
        put.wait()


def column(rows):
    parts = [jnp.transpose(jnp.broadcast_to(rows[t : t + 1], (128, 128))) for t in range(rows.shape[0])]
    return jnp.concatenate(parts, axis=0)


def thirds(x):
    parts = []
    for _ in range(3):
        part = x.astype(jnp.bfloat16).astype(jnp.float32)
        parts.append(part)
        x = x - part
    return parts


def params_kernel(n, entry_ref, vectors_ref, first_ref, o_ref, row_ref):
    own = C // n
    depth = 27 * LATENT_CHANNELS
    tall = C // 128
    first = pl.multiple_of(first_ref[0], 8)
    lane = lax.broadcasted_iota(jnp.int32, (C, 16), 1)

    def spread(t):
        tile = column(vectors_ref[t * tall : (t + 1) * tall])[:, :16]
        out = jnp.zeros((C, 16), jnp.float32)
        for t, part in enumerate(thirds(tile)):
            out = jnp.where(lane == t, part, out)
        return out

    half_gain = column(vectors_ref[tall : 2 * tall]) * 0.5
    gap = jnp.zeros((C, 512 - depth - 16), jnp.float32)
    weight = jnp.transpose(entry_ref[...].astype(jnp.float32))
    full = jnp.concatenate([weight, spread(0), gap, half_gain], axis=1)
    row_ref[0:C, :] = full
    row_ref[C : 2 * C, :] = jnp.concatenate([jnp.zeros_like(weight), spread(2), gap, half_gain], axis=1)
    mine = row_ref[pl.ds(first, own), :]
    after = row_ref[pl.ds(first + C, own), :]
    o_ref[...] = jnp.concatenate([mine, after, full], axis=0).astype(jnp.bfloat16)


def active_kernel(n, got_ref, lat_ref, params_ref, odd_ref, x_ref, stream_ref, half_ref, col_ref):
    own = C // n
    frames = n // PROMPT_SAMPLES * BLOCK_FRAMES
    each = LATENT_CHANNELS * BLOCK_FRAMES // n
    taps = 9 * LATENT_CHANNELS
    weight = params_ref[:, : 3 * taps + 16]
    half_gain = jnp.concatenate([params_ref[2 * own :, 512:]] * (LANES // 128), axis=1)
    ones = (lax.broadcasted_iota(jnp.int32, (16, LANES), 0) < 3).astype(jnp.float32).astype(jnp.bfloat16)
    per_frame = LATENT_CHANNELS // each
    blocks = n // PROMPT_SAMPLES
    got = got_ref[...].astype(jnp.float32).reshape(n, -1, 128)
    share = unpacked(got[:, : packing(own)[1] // 16], n, own)
    for r, run in enumerate(share):
        half_ref[r] = run
    mine = got[:, packing(own)[1] // 16 :]
    other = lat_ref[...].astype(jnp.float32).reshape(mine.shape)
    even = jnp.broadcast_to(odd_ref[0] == 0, mine.shape)
    lats = jnp.concatenate([jnp.where(even, mine, other), jnp.where(even, other, mine)], axis=1)
    lats = lats.reshape(n, LANES // 128, blocks * each, 128)
    lats = jnp.concatenate([lats[:, t] for t in range(LANES // 128)], axis=2)
    lats = lats.reshape(BLOCK_FRAMES, per_frame, blocks, each, LANES)
    for f in range(frames):
        b, g = divmod(f, BLOCK_FRAMES)
        lat = lats[g, :, b].reshape(LATENT_CHANNELS, LANES)
        for j in range(3):
            for k in range(3):
                moved = shifted(lat, LATENT_COLUMNS * (j - 1) + k - 1)
                moved = jnp.where(shift_mask(j, k), moved, 0.0)
                at = f * taps + (3 * j + k) * LATENT_CHANNELS
                col_ref[at : at + LATENT_CHANNELS, :] = moved.astype(jnp.bfloat16)
        least = max(f - 2, 0)
        z = jnp.dot(
            weight[:, (2 - (f - least)) * taps :],
            jnp.concatenate([col_ref[least * taps : (f + 1) * taps, :], ones], axis=0),
            preferred_element_type=jnp.float32,
        )
        stream_ref[f] = z[:own].astype(jnp.bfloat16).astype(jnp.float32) + z[own : 2 * own]
        s = z[2 * own :]
        scale = lax.rsqrt(jnp.sum(s * s, axis=0, keepdims=True) * (1.0 / C) + 1e-06)
        half = s.astype(jnp.bfloat16) * half_gain * scale.astype(jnp.bfloat16)
        x_ref[f * C : (f + 1) * C, :] = half + half * jnp.tanh(half)


def branch_kernel(n, half_ref, w_ref, x_ref, stream_ref, side_ref, count_ref, o_ref, out_ref):
    own = C // n
    frames = n // PROMPT_SAMPLES * BLOCK_FRAMES
    other = unpacked(w_ref[...].astype(jnp.float32), n, own)
    mine = [half_ref[r] for r in range(len(other))]
    left = jnp.broadcast_to(side_ref[0] == 0, (n * 8, 256))
    low = [jnp.where(left, m, o) for m, o in zip(mine, other)]
    high = [jnp.where(left, o, m) for m, o in zip(mine, other)]
    whole = 3 * (own // 8) // 2
    runs = low[:whole] + high[:whole]
    if len(low) > whole:
        rest = jnp.zeros((n * 8, 256 - 9 * own), jnp.float32)
        runs.append(jnp.concatenate([low[whole][:, : 5 * own], high[whole][:, : 4 * own], rest], axis=1))
    runs = [run.reshape(n, 1, 8, 256) for run in runs]
    depths = []
    for i in range(3):
        at = i * (own // 8)
        depths.append(jnp.concatenate(runs[at : at + own // 8], axis=1).reshape(C, 256))
    tall = -(-9 * own // 16) * 16
    turned = [jnp.transpose(depths[i].astype(jnp.bfloat16))[:tall] for i in (2, 1, 0)]
    lane = lax.broadcasted_iota(jnp.int32, (1, LANES), 1)
    count = jnp.zeros((1, LANES), jnp.int32)
    for s in range(PROMPT_SAMPLES):
        count = jnp.where(lane // HW == s, count_ref[s], count)
    for f in range(frames):
        least = max(f - 2, 0)
        z = jnp.dot(
            jnp.concatenate(turned[: f - least + 1][::-1], axis=1),
            x_ref[least * C : (f + 1) * C, :],
            preferred_element_type=jnp.float32,
        )
        total = stream_ref[f]
        for k in range(3):
            part = None
            for j in range(3):
                tap = z[(3 * j + k) * own : (3 * j + k + 1) * own]
                if j != 1:
                    tap = jnp.where(shift_mask(j, 1), shifted(tap, LATENT_COLUMNS * (j - 1)), 0.0)
                part = tap if part is None else part + tap
            if k != 1:
                part = jnp.where(shift_mask(1, k), shifted(part, k - 1), 0.0)
            total = total + part
        out_ref[f] = jnp.where(count > f, total, 0.0)
        b, g = divmod(f, BLOCK_FRAMES)
        if g == BLOCK_FRAMES - 1:
            parts = [out_ref[b * BLOCK_FRAMES + t] for t in range(BLOCK_FRAMES)]
            for s in range(0, PROMPT_SAMPLES, 2):
                both = [
                    jnp.concatenate([p[:, t * HW : (t + 1) * HW] for p in parts], axis=1) for t in (s, s + 1)
                ]
                at = (b * PROMPT_SAMPLES + s) * own
                o_ref[at : at + 2 * own, :] = jnp.concatenate(both, axis=0).astype(jnp.bfloat16)


def transpose_kernel(x_ref, o_ref):
    o_ref[...] = jnp.transpose(x_ref[...])


def call(body, out, ins, outs, scratch=(), flops=0, moved=0, limit=8):
    return pl.pallas_call(
        body,
        out_shape=out,
        in_specs=ins,
        out_specs=outs,
        scratch_shapes=list(scratch),
        compiler_params=pltpu.CompilerParams(vmem_limit_bytes=limit * 1024 * 1024),
        cost_estimate=pl.CostEstimate(flops=flops, bytes_accessed=moved, transcendentals=0),
    )


def by_channel(n, latents, counts, entry_kernel, entry_bias, gain, kernel, bias):
    own = C // n
    frames = n // PROMPT_SAMPLES * BLOCK_FRAMES
    first = (lax.axis_index("tm") * own).astype(jnp.int32).reshape(1)
    shape = jax.ShapeDtypeStruct
    bf16, f32 = jnp.bfloat16, jnp.float32
    side = lax.axis_index("groups").astype(jnp.int32).reshape(1)
    each = latents.shape[1] // HW * (n // PROMPT_SAMPLES)
    odd = (lax.axis_index("tm") % 2).astype(jnp.int32).reshape(1)
    height = packing(own)[1] // 16
    extra = each * LANES // 256
    parcels = call(
        functools.partial(parcels_kernel, n),
        shape((n * (height + extra), 128), bf16),
        [ANY, ANY, SMEM],
        ANY,
        [
            pltpu.VMEM(latents.shape, bf16),
            pltpu.VMEM(kernel.shape, bf16),
            pltpu.VMEM((n * (height + extra), 128), bf16),
            pltpu.SemaphoreType.DMA((2,)),
            pltpu.SemaphoreType.DMA((n // 4,)),
        ],
        limit=58,
    )(latents, kernel, side)
    got = lax.all_to_all(parcels, "tm", split_axis=0, concat_axis=0, tiled=True)
    params = call(
        functools.partial(params_kernel, n),
        shape((2 * own + C, 640), bf16),
        [VMEM, VMEM, SMEM],
        VMEM,
        [pltpu.VMEM((2 * C, 640), f32)],
        flops=500_000_000,
        moved=2_000_000,
    )(
        entry_kernel.reshape(27 * LATENT_CHANNELS, C),
        jnp.concatenate([entry_bias, gain, bias]).reshape(-1, 128),
        first,
    )
    split = got.reshape(n, height + extra, 128)
    other = lax.ppermute(split[:, :height].reshape(n * height, 128), "groups", [(0, 1), (1, 0)])
    lats = split[:, height:].reshape(-1, 128)
    lats = lax.ppermute(lats, "tm", [(i, i ^ 1) for i in range(n)])
    halves = 3 * (own // 8) // 2 + 3 * (own // 8) % 2
    active, stream, half = call(
        functools.partial(active_kernel, n),
        (
            shape((frames * C, LANES), bf16),
            shape((frames, own, LANES), f32),
            shape((halves, n * 8, 256), f32),
        ),
        [VMEM, VMEM, VMEM, SMEM],
        (VMEM, VMEM, VMEM),
        [pltpu.VMEM((frames * 9 * LATENT_CHANNELS, LANES), bf16)],
        flops=2 * frames * LANES * 432 * C,
        moved=20_000_000,
        limit=24,
    )(got, lats, params, odd)
    out = call(
        functools.partial(branch_kernel, n),
        shape((n * own, BLOCK_FRAMES * HW), bf16),
        [VMEM, VMEM, VMEM, VMEM, SMEM, SMEM],
        VMEM,
        [pltpu.VMEM((frames, own, LANES), f32)],
        flops=2 * frames * LANES * 27 * C * own,
        moved=20_000_000,
        limit=24,
    )(half, other, active, stream, side, counts)
    out = lax.all_to_all(out, "tm", split_axis=0, concat_axis=0, tiled=True)
    out = call(transpose_kernel, shape((BLOCK_FRAMES * HW, C), bf16), [VMEM], VMEM)(out)
    return out.reshape(BLOCK_FRAMES, LATENT_ROWS, LATENT_COLUMNS, C)


def from_behind(block, axis, distance):
    devices = range(lax.axis_size(axis))
    route = [(i - distance, i) for i in devices if i - distance in devices]
    return lax.ppermute(block, axis, route)


def causal_conv(frames, weight):
    frames_out = frames.shape[0] - 2
    inputs = frames.shape[3]
    padded = jnp.pad(frames, ((0, 0), (1, 1), (1, 1), (0, 0)))
    total = jnp.zeros((frames_out * LATENT_ROWS * LATENT_COLUMNS, weight.shape[2]), jnp.float32)
    for time_tap in range(3):
        for row_tap in range(3):
            for col_tap in range(3):
                window = padded[
                    time_tap : time_tap + frames_out,
                    row_tap : row_tap + LATENT_ROWS,
                    col_tap : col_tap + LATENT_COLUMNS,
                    :,
                ]
                window = window.reshape(frames_out * LATENT_ROWS * LATENT_COLUMNS, inputs)
                tap = 9 * time_tap + 3 * row_tap + col_tap
                total = total + jnp.dot(window, weight[tap], preferred_element_type=jnp.float32)
    return total


def activate(stream, norm_scale_gain):
    values = stream.astype(jnp.float32)
    scale = lax.rsqrt(jnp.mean(values * values, axis=-1, keepdims=True) + 1e-06)
    return jax.nn.silu(values * scale * norm_scale_gain).astype(jnp.bfloat16)


def to_cells(planes):
    return jnp.transpose(
        planes.reshape(planes.shape[0], LATENT_CHANNELS, LATENT_ROWS, LATENT_COLUMNS), (0, 2, 3, 1)
    )


def by_block(
    sharded_latents,
    sample_frame_count,
    entry_kernel,
    entry_bias,
    norm_scale_gain,
    residual_kernel,
    residual_bias,
):
    gathered_latents = lax.all_to_all(
        sharded_latents, "tm", split_axis=0, concat_axis=1, tiled=True
    )
    latent_volume = gathered_latents.reshape(
        BLOCK_FRAMES, LATENT_CHANNELS, LATENT_ROWS * LATENT_COLUMNS
    )
    position = lax.axis_index("tm")
    block = position // PROMPT_SAMPLES
    sample = position % PROMPT_SAMPLES
    keep = block > 0
    earlier = from_behind(latent_volume, "tm", PROMPT_SAMPLES)
    earlier = jnp.where(keep, earlier, jnp.zeros_like(earlier))
    frames = to_cells(jnp.concatenate([earlier, latent_volume], axis=0))
    widened = (causal_conv(frames, entry_kernel) + entry_bias).astype(jnp.bfloat16)
    active_all = activate(widened, norm_scale_gain).reshape(
        BLOCK_FRAMES + 2, LATENT_ROWS, LATENT_COLUMNS, C
    )
    behind = jnp.where(keep, active_all[:2], jnp.zeros_like(active_all[:2]))
    extended = jnp.concatenate([behind, active_all[2:]], axis=0)
    stream = widened[2 * LATENT_ROWS * LATENT_COLUMNS :]
    kernel_all = lax.all_gather(residual_kernel, "tm", axis=1, tiled=True)
    branch = causal_conv(extended, kernel_all)
    total = (stream.astype(jnp.float32) + (branch + residual_bias)).reshape(
        BLOCK_FRAMES, LATENT_ROWS, LATENT_COLUMNS, C
    )
    limit = jnp.sum(jnp.where(jnp.arange(PROMPT_SAMPLES) == sample, sample_frame_count, 0))
    frame_index = block * BLOCK_FRAMES + jnp.arange(BLOCK_FRAMES)
    valid = (frame_index < limit)[:, None, None, None]
    return jnp.where(valid, total, jnp.zeros_like(total)).astype(jnp.bfloat16)


def solution(mesh):
    n = mesh.shape["tm"]
    cells = BLOCK_FRAMES * LATENT_CHANNELS * HW
    fits = mesh.shape["groups"] == 2 and 9 * (C // n) <= 256 and n % 4 == 0 and LANES % 256 == 0
    whole_rows = fits and cells % (n * HW) == 0 and C % n == 0 and (C // n) % 8 == 0 and n % PROMPT_SAMPLES == 0
    body = functools.partial(by_channel, n) if whole_rows else by_block
    in_specs = (P("groups", "tm"), P("groups"), P(), P(), P(), P(None, "tm", None), P())
    out_specs = P(("groups", "tm"), None, None, None)
    return jax.shard_map(body, mesh=mesh, in_specs=in_specs, out_specs=out_specs, check_vma=False)
```
